32 devices in a mesh: dp: 2 (over x), blk: 4 (over z), uly: 4 (over y, core).
Axes of the slice: x: 2, y: 2, z: 4, core: 2. Of those that a mesh axis runs over, the one named last changes fastest.
Arguments:
- inputs: bfloat16 [2, 2048, 768], P('dp', ('blk', 'uly')), may hold values from -6 to 6
- stretch_order: int32 [2, 32], P('dp'), may hold values from 0 to 31, each once within a row
- norm_gains: bfloat16 [2, 768], P(None, ('blk', 'uly')), may hold values from 0.099609375 to 1.8984375
- biases: bfloat16 [4, 768], P(None, ('blk', 'uly')), may hold values from -3 to 3
- mid_shift: bfloat16 [768], P(('blk', 'uly')), may hold values from -3 to 3
- value_bias: bfloat16 [768], P(('blk', 'uly')), may hold values from -0.625 to 0.625
- qkv_weight: bfloat16 [768, 2304], P(('blk', 'uly')), may hold values from -0.21875 to 0.21875
- out_weight: bfloat16 [768, 768], P(('blk', 'uly')), may hold values from -6 to 6
- fc_weight: bfloat16 [768, 3072], P(('blk', 'uly')), may hold values from -0.21875 to 0.21875
- fc_bias: bfloat16 [3072], P(('blk', 'uly')), may hold values from -3 to 3
- proj_weight: bfloat16 [3072, 768], P(('blk', 'uly')), may hold values from -0.109375 to 0.109375
- cotangent: bfloat16 [2, 2048, 768], P('dp', ('blk', 'uly')), may hold values from -6 to 6
Outputs:
- output: bfloat16 [2, 2048, 768], P('dp', ('blk', 'uly'))
- input_grad: bfloat16 [2, 2048, 768], P('dp', ('blk', 'uly'))
- gains_grad: float32 [2, 768], P(None, ('blk', 'uly'))
- biases_grad: float32 [4, 768], P(None, ('blk', 'uly'))
- mid_shift_grad: float32 [768], P(('blk', 'uly'))
- value_bias_grad: float32 [768], P(('blk', 'uly'))
- qkv_grad: float32 [768, 2304], P(('blk', 'uly'))
- out_grad: float32 [768, 768], P(('blk', 'uly'))
- fc_grad: float32 [768, 3072], P(('blk', 'uly'))
- fc_bias_grad: float32 [3072], P(('blk', 'uly'))
- proj_grad: float32 [3072, 768], P(('blk', 'uly'))
The draws below stay inside these ranges and needn't reach their ends.
Inputs may be any that keep to these rules, and one draw needn't show every extreme that they name: `stretch_order`: each row holds every stretch number 0 to 31 once.
All inputs are finite; a program needn't handle non-finite values.
Results may differ from the reference program's by a relative error of at most 0.025.
Values may be sent and summed in bfloat16 or wider, within the bound.
A program may use at most 192 MiB of HBM per device.

```python
import math
import jax
import jax.numpy as jnp
from jax import lax

D = 768
HEADS = 12
FF = 3072
ROWS = 128
SEQS = 2
LEN = 2048
NCH = 32


def steps_of(own_key, dims, pieces, least, high):
    level = 1.0
    for axis_at, parts in pieces:
        heights = jax.random.uniform(jax.random.fold_in(jax.random.fold_in(own_key, 6), axis_at), (parts,), jnp.float32, least / len(pieces), high / len(pieces))
        level = level * jnp.repeat(jnp.exp(heights), dims[axis_at] // parts).reshape((-1,) + (1,) * (len(dims) - 1 - axis_at))
    return level


def bell_draw(rng, shape, scale, reach, shards=(), kind=jnp.bfloat16):
    entries = jax.random.normal(rng, shape, jnp.float32) * scale
    if len(shards) > 0:
        entries = steps_of(rng, shape, shards, -0.22, 0.18) * entries
    return jnp.clip(entries, min=-reach, max=reach).astype(kind)


def setup_inputs(seed: int = 0) -> dict:
    key_list = jax.random.split(jax.random.key(seed), 13)
    return {
        "inputs": bell_draw(key_list[0], (SEQS, LEN, D), 1.0, 6.0, ((0, 2), (1, 16))),
        "stretch_order": jax.vmap(lambda own: jax.random.permutation(own, NCH))(jax.random.split(key_list[1], SEQS)).reshape((SEQS, NCH)).astype(jnp.int32),
        "norm_gains": jnp.clip(1.0 + 0.18 * jax.random.normal(key_list[2], (2, D), jnp.float32), 0.099609375, 1.8984375).astype(jnp.bfloat16),
        "biases": bell_draw(key_list[3], (4, D), 0.5, 3.0, ((1, 16),)),
        "mid_shift": bell_draw(key_list[4], (D,), 0.5, 3.0, ((0, 16),)),
        "value_bias": bell_draw(key_list[5], (D,), 0.1, 0.625, ((0, 16),)),
        "qkv_weight": bell_draw(key_list[6], (D, 3 * D), D ** -0.5, 0.21875, ((0, 16),)),
        "out_weight": bell_draw(key_list[7], (D, D), ((LEN // (4 * D) + 1) ** 0.5), 6.0, ((0, 16),)),
        "fc_weight": bell_draw(key_list[8], (D, FF), D ** -0.5, 0.21875, ((0, 16),)),
        "fc_bias": bell_draw(key_list[9], (FF,), 0.5, 3.0, ((0, 16),)),
        "proj_weight": bell_draw(key_list[10], (FF, D), FF ** -0.5, 0.109375, ((0, 16),)),
        "cotangent": bell_draw(key_list[11], (SEQS, LEN, D), 1.0, 6.0, ((0, 2), (1, 16))),
    }


@jax.custom_vjp
def low(v):
    return lax.optimization_barrier(v.astype(jnp.bfloat16)).astype(jnp.float32)

@jax.custom_vjp
def low_back(v):
    return v

def low_keep(v):
    return (low(v), None)

def low_pass(kept, grad):
    return (grad,)

def back_keep(v):
    return (v, None)

def back_low(kept, grad):
    return (low(grad),)
low.defvjp(low_keep, low_pass)
low_back.defvjp(back_keep, back_low)

def layer_norm(values, gain, shift):
    center = values - lax.optimization_barrier(jnp.mean(values, -1, keepdims=True))
    inverse = lax.rsqrt(lax.optimization_barrier(jnp.mean(center * center, -1, keepdims=True)) + 1e-05)
    return center * inverse * gain + shift

def forward(sequence, positions, norm_gains, biases, mid_shift, value_bias, qkv_weight, out_weight, fc_weight, fc_bias, proj_weight):
    highest = lax.Precision.HIGHEST
    row_count = sequence.shape[0]
    head_dim = D // HEADS
    score_scale = head_dim ** (-0.5)
    ln_in = low(layer_norm(sequence, norm_gains[0], biases[0]))
    qkv_shift = jnp.concatenate([biases[1], jnp.zeros_like(value_bias), value_bias])
    qkv = low(low_back(jnp.dot(ln_in, qkv_weight, precision=highest) + qkv_shift))
    queries = qkv[:, :D].reshape(row_count, HEADS, head_dim)
    key_rows = qkv[:, D:2 * D].reshape(row_count, HEADS, head_dim)
    value_rows = qkv[:, 2 * D:].reshape(row_count, HEADS, head_dim)
    query_block = math.gcd(row_count, 512)

    def attend(query_pair):
        query_part, query_pos = query_pair
        scores = low_back(jnp.einsum('qhd,khd->hqk', query_part, key_rows, precision=highest) * score_scale)
        scores = jnp.where(query_pos[None, :, None] >= positions[None, None, :], scores, -1e+30)
        attn_probs = low(jax.nn.softmax(scores, axis=-1))
        return jnp.einsum('hqk,khd->qhd', attn_probs, value_rows, precision=highest)
    attended = lax.map(jax.checkpoint(attend), (queries.reshape(row_count // query_block, query_block, HEADS, head_dim), positions.reshape(row_count // query_block, query_block)))
    attended = low(low_back(attended.reshape(row_count, D)))
    resid = sequence + low_back(jnp.dot(attended, out_weight, precision=highest) + biases[2])
    ln_mid = low(layer_norm(resid, norm_gains[1], mid_shift))
    pre_act = low_back(jnp.dot(ln_mid, fc_weight, precision=highest) + fc_bias)
    act = low(jax.nn.gelu(pre_act, approximate=True))
    branch = low_back(jnp.dot(act, proj_weight, precision=highest) + biases[3])
    return resid + branch

def reference(inputs, stretch_order, norm_gains, biases, mid_shift, value_bias, qkv_weight, out_weight, fc_weight, fc_bias, proj_weight, cotangent):
    params = tuple((item.astype(jnp.float32) for item in (norm_gains, biases, mid_shift, value_bias, qkv_weight, out_weight, fc_weight, fc_bias, proj_weight)))
    half_rows = ROWS // 2

    def one_sequence(carried, element):
        sequence, order_row, seq_cot = element
        positions = (order_row[:, None] * half_rows + jnp.arange(half_rows, dtype=jnp.int32)[None, :]).reshape(-1).astype(jnp.int32)

        def apply_layer(seq_values, *weights):
            return forward(seq_values, positions, *weights)
        result, pull_back = jax.vjp(apply_layer, sequence.astype(jnp.float32), *params)
        gradients = pull_back(seq_cot.astype(jnp.float32))
        carried = tuple((total + grad for total, grad in zip(carried, gradients[1:])))
        return (carried, (result.astype(jnp.bfloat16), gradients[0].astype(jnp.bfloat16)))
    start_sums = tuple((jnp.zeros_like(item) for item in params))
    totals, stacked = lax.scan(one_sequence, start_sums, (inputs, stretch_order, cotangent))
    return (stacked[0], stacked[1], totals[0], totals[1], totals[2], totals[3], totals[4], totals[5], totals[6], totals[7], totals[8])
```

```python
import functools
import math

import jax
import jax.numpy as jnp
from jax import lax
from jax.experimental import pallas as pl
from jax.experimental.pallas import tpu as pltpu
from jax.sharding import PartitionSpec as P

HEADS = 12


masked_score = -1e30


def layer_norm(values, gain, shift):
    center = values - jnp.mean(values, -1, keepdims=True)
    inverse = lax.rsqrt(jnp.mean(center * center, -1, keepdims=True) + 1e-05)
    normed = center * inverse
    return (normed * gain + shift, normed, inverse)


def norm_back(grad_out, normed, inverse, gain):
    scaled = grad_out * gain
    mean_plain = jnp.mean(scaled, -1, keepdims=True)
    mean_mixed = jnp.mean(scaled * normed, -1, keepdims=True)
    return inverse * (scaled - mean_plain - normed * mean_mixed)


def sweep(step_fn, carried, parts):
    row_count = parts[0].shape[1]
    sweep_rows = math.gcd(row_count, 1024)

    def turn(inner, turn_number):
        offset = turn_number * sweep_rows
        blocks = tuple((lax.dynamic_slice_in_dim(part, offset, sweep_rows, 1) for part in parts))
        return (step_fn(inner, blocks, offset), None)

    result, _ = lax.scan(turn, carried, jnp.arange(row_count // sweep_rows, dtype=jnp.int32))
    return result


def per_device(
    inputs,
    stretch_order,
    norm_gains,
    biases,
    mid_shift,
    value_bias,
    qkv_weight,
    out_weight,
    fc_weight,
    fc_bias,
    proj_weight,
    cotangent,
):
    fp32 = jnp.float32
    bf16 = jnp.bfloat16
    gain_rows, shifts, mid_gathered, value_shift, w_qkv, w_out, w_fc, b_fc, w_proj = (
        lax.all_gather(norm_gains, ("blk", "uly"), axis=1, tiled=True),
        lax.all_gather(biases, ("blk", "uly"), axis=1, tiled=True),
        lax.all_gather(mid_shift, ("blk", "uly"), axis=0, tiled=True),
        lax.all_gather(value_bias, ("blk", "uly"), axis=0, tiled=True),
        lax.all_gather(qkv_weight, ("blk", "uly"), axis=0, tiled=True),
        lax.all_gather(out_weight, ("blk", "uly"), axis=0, tiled=True),
        lax.all_gather(fc_weight, ("blk", "uly"), axis=0, tiled=True),
        lax.all_gather(fc_bias, ("blk", "uly"), axis=0, tiled=True),
        lax.all_gather(proj_weight, ("blk", "uly"), axis=0, tiled=True),
    )
    gain_rows = gain_rows.astype(fp32)
    shifts = shifts.astype(fp32)
    mid_gathered = mid_gathered.astype(fp32)
    seq_count, row_len, width = inputs.shape
    uly_count = lax.axis_size("uly")
    local_heads = HEADS // uly_count
    head_dim = width // HEADS
    head_span = local_heads * head_dim
    block_rows = uly_count * row_len
    half_rows = row_len // 2
    seq_len = stretch_order.shape[1] * half_rows
    score_scale = head_dim ** (-0.5)
    tokens = inputs.astype(fp32).reshape(seq_count * row_len, width)
    ln_in, normed_in, inverse_in = layer_norm(tokens, gain_rows[0], shifts[0])
    ln_in = ln_in.astype(bf16)
    qkv_shift = jnp.concatenate([shifts[1], jnp.zeros((width,), fp32), value_shift.astype(fp32)])
    qkv = (jnp.dot(ln_in, w_qkv, preferred_element_type=fp32) + qkv_shift).astype(bf16)
    head_data = lax.all_to_all(
        qkv.reshape(seq_count, row_len, 3, uly_count, head_span),
        "uly",
        split_axis=3,
        concat_axis=1,
        tiled=True,
    )
    queries = head_data[:, :, 0, 0].reshape(seq_count, block_rows, local_heads, head_dim)
    key_rows = head_data[:, :, 1, 0]
    value_rows = head_data[:, :, 2, 0]
    positions = (
        stretch_order[:, :, None] * half_rows
        + jnp.arange(half_rows, dtype=jnp.int32)[None, None, :]
    ).reshape(seq_count, seq_len)
    query_pos = lax.dynamic_slice_in_dim(
        positions, lax.axis_index("blk") * block_rows, block_rows, 1
    )

    def score_block(key_part, key_start):
        part_rows = key_part.shape[1]
        key_pos = lax.dynamic_slice_in_dim(positions, key_start, part_rows, 1)
        scores = (
            jnp.einsum(
                "sqhd,skhd->shqk",
                queries,
                key_part.reshape(seq_count, part_rows, local_heads, head_dim),
                preferred_element_type=fp32,
            )
            * score_scale
        )
        causal = query_pos[:, None, :, None] >= key_pos[:, None, None, :]
        return (scores, causal)

    def stats_step(carried, blocks, key_start):
        row_max, row_total = carried
        scores, causal = score_block(blocks[0], key_start)
        new_max = jnp.maximum(row_max, jnp.max(jnp.where(causal, scores, masked_score), -1))
        row_total = row_total * jnp.exp(row_max - new_max) + jnp.sum(
            jnp.where(causal, jnp.exp(scores - new_max[..., None]), 0.0), -1
        )
        return (new_max, row_total)

    def softmax_of(scores, causal, row_max, row_total):
        return jnp.where(causal, jnp.exp(scores - row_max[..., None]) / row_total[..., None], 0.0)

    def make_output_step(row_max, row_total):

        def output_step(acc_out, blocks, key_start):
            scores, causal = score_block(blocks[0], key_start)
            attn_probs = softmax_of(scores, causal, row_max, row_total).astype(bf16)
            part_rows = blocks[1].shape[1]
            value_part = blocks[1].reshape(seq_count, part_rows, local_heads, head_dim)
            return acc_out + jnp.einsum(
                "shqk,skhd->sqhd", attn_probs, value_part, preferred_element_type=fp32
            )

        return output_step

    stats_init = (
        jnp.full((seq_count, local_heads, block_rows), masked_score, fp32),
        jnp.zeros((seq_count, local_heads, block_rows), fp32),
    )
    empty_out = jnp.zeros((seq_count, block_rows, local_heads, head_dim), fp32)
    all_keys, all_values = (
        lax.all_gather(key_rows, "blk", axis=1, tiled=True),
        lax.all_gather(value_rows, "blk", axis=1, tiled=True),
    )
    row_max, row_total = sweep(stats_step, stats_init, (all_keys,))
    attended = sweep(make_output_step(row_max, row_total), empty_out, (all_keys, all_values))
    attended_low = attended.astype(bf16).reshape(seq_count, block_rows, 1, head_span)
    merged = lax.all_to_all(attended_low, "uly", split_axis=1, concat_axis=2, tiled=True).reshape(
        seq_count * row_len, width
    )
    resid = tokens + (jnp.dot(merged, w_out, preferred_element_type=fp32) + shifts[2])
    ln_mid, normed_mid, inverse_mid = layer_norm(resid, gain_rows[1], mid_gathered)
    ln_mid = ln_mid.astype(bf16)
    pre_act = jnp.dot(ln_mid, w_fc, preferred_element_type=fp32) + b_fc.astype(fp32)

    def gelu_piece(pre_values):
        return jax.nn.gelu(pre_values, approximate=True)

    act, gelu_back = jax.vjp(gelu_piece, pre_act)
    act = act.astype(bf16)
    result = resid + (jnp.dot(act, w_proj, preferred_element_type=fp32) + shifts[3])
    grad_low = cotangent.reshape(seq_count * row_len, width)
    grad_out = grad_low.astype(fp32)
    proj_grad = jnp.einsum("ta,tb->ab", act, grad_low, preferred_element_type=fp32)
    proj_shift_grad = jnp.sum(grad_out, 0)
    grad_act = jnp.einsum("tb,ab->ta", grad_low, w_proj, preferred_element_type=fp32)
    grad_pre = gelu_back(grad_act)[0].astype(bf16)
    fc_grad = jnp.einsum("ta,tb->ab", ln_mid, grad_pre, preferred_element_type=fp32)
    fc_shift_grad = jnp.sum(grad_pre.astype(fp32), 0)
    grad_mid = jnp.einsum("tb,ab->ta", grad_pre, w_fc, preferred_element_type=fp32)
    gain_mid_grad = jnp.sum(grad_mid * normed_mid, 0)
    shift_mid_grad = jnp.sum(grad_mid, 0)
    grad_resid = grad_out + norm_back(grad_mid, normed_mid, inverse_mid, gain_rows[1])
    grad_branch = grad_resid.astype(bf16)
    out_grad = jnp.einsum("ta,tb->ab", merged, grad_branch, preferred_element_type=fp32)
    out_shift_grad = jnp.sum(grad_branch.astype(fp32), 0)
    grad_merged = jnp.einsum("tb,ab->ta", grad_branch, w_out, preferred_element_type=fp32).astype(
        bf16
    )
    grad_att = lax.all_to_all(
        grad_merged.reshape(seq_count, row_len, uly_count, head_span),
        "uly",
        split_axis=2,
        concat_axis=1,
        tiled=True,
    )
    grad_att = grad_att.reshape(seq_count, block_rows, local_heads, head_dim)
    delta = jnp.transpose(jnp.sum(grad_att.astype(fp32) * attended, -1), (0, 2, 1))
    back_keys, back_values = (all_keys, all_values)
    sweep_rows = math.gcd(seq_len, 1024)

    def query_terms(offset):
        key_part = lax.dynamic_slice_in_dim(back_keys, offset, sweep_rows, 1)
        value_part = lax.dynamic_slice_in_dim(back_values, offset, sweep_rows, 1)
        scores, causal = score_block(key_part, offset)
        attn_probs = softmax_of(scores, causal, row_max, row_total)
        key_heads = key_part.reshape(seq_count, sweep_rows, local_heads, head_dim)
        value_heads = value_part.reshape(seq_count, sweep_rows, local_heads, head_dim)
        grad_probs = jnp.einsum(
            "sqhd,skhd->shqk", grad_att, value_heads, preferred_element_type=fp32
        )
        grad_scores = (attn_probs * (grad_probs - delta[..., None])).astype(bf16)
        query_term = (
            jnp.einsum("shqk,skhd->sqhd", grad_scores, key_heads, preferred_element_type=fp32)
            * score_scale
        )
        return (query_term, grad_scores, attn_probs.astype(bf16))

    query_init = jnp.zeros((seq_count, block_rows, local_heads, head_dim), fp32)

    def back_step(carried, turn_number):
        grad_query, kv_buffer = carried
        offset = turn_number * sweep_rows
        query_term, grad_scores, probs_low = query_terms(offset)
        grad_key = (
            jnp.einsum("shqk,sqhd->skhd", grad_scores, queries, preferred_element_type=fp32)
            * score_scale
        )
        grad_value = jnp.einsum("shqk,sqhd->skhd", probs_low, grad_att, preferred_element_type=fp32)
        kv_pair = jnp.stack(
            [
                grad_key.reshape(seq_count, sweep_rows, head_span),
                grad_value.reshape(seq_count, sweep_rows, head_span),
            ],
            2,
        )
        kv_buffer = lax.dynamic_update_slice_in_dim(kv_buffer, kv_pair, offset, 1)
        return ((grad_query + query_term, kv_buffer), None)

    back_init = (query_init, jnp.zeros((seq_count, seq_len, 2, head_span), fp32))
    back_done, _ = lax.scan(
        back_step, back_init, jnp.arange(seq_len // sweep_rows, dtype=jnp.int32)
    )
    grad_query, kv_buffer = back_done
    kv_summed = lax.psum_scatter(
        kv_buffer.astype(jnp.bfloat16), "blk", scatter_dimension=1, tiled=True
    ).astype(jnp.float32)
    grad_heads = jnp.concatenate(
        [
            grad_query.reshape(seq_count, block_rows, 1, head_span).astype(bf16),
            kv_summed.astype(bf16),
        ],
        2,
    )
    grad_qkv = lax.all_to_all(
        grad_heads.reshape(seq_count, block_rows, 3, 1, head_span),
        "uly",
        split_axis=1,
        concat_axis=3,
        tiled=True,
    )
    grad_qkv = grad_qkv.reshape(seq_count * row_len, 3 * width)
    qkv_grad = jnp.einsum("ta,tb->ab", ln_in, grad_qkv, preferred_element_type=fp32)
    column_sums = jnp.sum(grad_qkv.astype(fp32), 0)
    grad_in_norm = jnp.einsum("tb,ab->ta", grad_qkv, w_qkv, preferred_element_type=fp32)
    gain_in_grad = jnp.sum(grad_in_norm * normed_in, 0)
    shift_in_grad = jnp.sum(grad_in_norm, 0)
    grad_input = grad_resid + norm_back(grad_in_norm, normed_in, inverse_in, gain_rows[0])
    gains_grad = jnp.stack([gain_in_grad, gain_mid_grad])
    biases_grad = jnp.stack([shift_in_grad, column_sums[:width], out_shift_grad, proj_shift_grad])
    value_grad = column_sums[2 * width :]
    shard_grads = (
        lax.psum_scatter(gains_grad, ("blk", "uly"), scatter_dimension=1, tiled=True),
        lax.psum_scatter(biases_grad, ("blk", "uly"), scatter_dimension=1, tiled=True),
        lax.psum_scatter(shift_mid_grad, ("blk", "uly"), scatter_dimension=0, tiled=True),
        lax.psum_scatter(value_grad, ("blk", "uly"), scatter_dimension=0, tiled=True),
        lax.psum_scatter(qkv_grad, ("blk", "uly"), scatter_dimension=0, tiled=True),
        lax.psum_scatter(out_grad, ("blk", "uly"), scatter_dimension=0, tiled=True),
        lax.psum_scatter(fc_grad, ("blk", "uly"), scatter_dimension=0, tiled=True),
        lax.psum_scatter(fc_shift_grad, ("blk", "uly"), scatter_dimension=0, tiled=True),
        lax.psum_scatter(proj_grad, ("blk", "uly"), scatter_dimension=0, tiled=True),
    )
    shard_grads = (
        lax.psum(shard_grads[0].astype(jnp.bfloat16), "dp").astype(jnp.float32),
        lax.psum(shard_grads[1].astype(jnp.bfloat16), "dp").astype(jnp.float32),
        lax.psum(shard_grads[2].astype(jnp.bfloat16), "dp").astype(jnp.float32),
        lax.psum(shard_grads[3].astype(jnp.bfloat16), "dp").astype(jnp.float32),
        lax.psum(shard_grads[4].astype(jnp.bfloat16), "dp").astype(jnp.float32),
        lax.psum(shard_grads[5].astype(jnp.bfloat16), "dp").astype(jnp.float32),
        lax.psum(shard_grads[6].astype(jnp.bfloat16), "dp").astype(jnp.float32),
        lax.psum(shard_grads[7].astype(jnp.bfloat16), "dp").astype(jnp.float32),
        lax.psum(shard_grads[8].astype(jnp.bfloat16), "dp").astype(jnp.float32),
    )
    output = result.astype(bf16).reshape(seq_count, row_len, width)
    input_grad = grad_input.astype(bf16).reshape(seq_count, row_len, width)
    return (
        output,
        input_grad,
        shard_grads[0],
        shard_grads[1],
        shard_grads[2],
        shard_grads[3],
        shard_grads[4],
        shard_grads[5],
        shard_grads[6],
        shard_grads[7],
        shard_grads[8],
    )


MESH = pl.DeviceIdType.MESH
BF = jnp.bfloat16
F32 = jnp.float32
VSPEC = pl.BlockSpec(memory_space=pltpu.VMEM)


class Net:
    def __init__(self, send_sem, recv_sem, nz):
        self.send_sem, self.recv_sem = send_sem, recv_sem
        self.count = 0
        self.sent = []
        self.nz = nz
        self.x = lax.axis_index("dp")
        self.z = lax.axis_index("blk")
        self.u = lax.axis_index("uly")

    def slot(self):
        self.count += 1
        return self.count - 1

    def make(self, src, dst, dev):
        k = self.slot()
        return pltpu.make_async_remote_copy(
            src_ref=src,
            dst_ref=dst,
            send_sem=self.send_sem.at[k],
            recv_sem=self.recv_sem.at[k],
            device_id=dev,
            device_id_type=MESH,
        )

    def send(self, src, dst, dev):
        copy = self.make(src, dst, dev)
        copy.start()
        self.sent.append(copy)
        return copy

    def plane(self, m):
        return (self.x, self.z, self.u ^ m)

    def other_x(self):
        return (1 - self.x, self.z, self.u)

    def zplus(self, d):
        return lax.rem(self.z + d, self.nz)

    def line(self, d):
        return (self.x, self.zplus(d), self.u)

    def enter(self):
        barrier = pltpu.get_barrier_semaphore()
        near = [self.plane(m) for m in (1, 2, 3)] + [self.other_x()]
        near += [self.line(d) for d in range(1, self.nz)]
        near += [(1 - self.x, self.z, self.u ^ m) for m in (1, 2, 3)]
        for dev in near:
            pl.semaphore_signal(barrier, inc=1, device_id=dev, device_id_type=MESH)
        pl.semaphore_wait(barrier, len(near))

    def finish(self):
        for copy in self.sent:
            copy.wait_send()


def rows_at(start, count):
    return pl.ds(pl.multiple_of(start, 16), count)


def gather_kernel(nz, qkv_pre, fc_pre, out_s, proj_s, vec_pre, w_qkv, w_fc, w_proj, w_out, vec, land_z, vec_u, land_p, send_sem, recv_sem, local_sem):
    net = Net(send_sem, recv_sem, nz)
    x, z, u = net.x, net.z, net.u
    own48 = (4 * z + u) * 48
    locals_ = [
        pltpu.make_async_copy(qkv_pre.at[u], w_qkv.at[rows_at(own48, 48)], local_sem.at[0]),
        pltpu.make_async_copy(fc_pre.at[u], w_fc.at[rows_at(own48, 48)], local_sem.at[1]),
        pltpu.make_async_copy(proj_s, w_proj.at[rows_at(192 * z, 192)], local_sem.at[2]),
        pltpu.make_async_copy(out_s, w_out.at[rows_at(own48, 48)], local_sem.at[3]),
    ]
    for copy in locals_:
        copy.start()
    net.enter()
    vec_z = [net.send(vec_pre, land_z.at[d - 1], net.line(d)) for d in range(1, nz)]
    in_plane = {}
    for name, pre, full in (("qkv", qkv_pre, w_qkv), ("fc", fc_pre, w_fc)):
        in_plane[name] = [
            net.send(pre.at[u ^ m], full.at[rows_at(own48, 48)], net.plane(m)) for m in (1, 2, 3)
        ]
    half_cols = pl.ds(pl.multiple_of(384 * x, 128), 384)
    for copy in vec_z:
        copy.wait_recv()
    total = vec_pre[...]
    for d in range(nz - 1):
        total = total + land_z[d]
    vec_u[...] = total
    vec_p = [net.send(vec_u, land_p.at[m - 1], net.plane(m)) for m in (1, 2, 3)]
    for copy in locals_:
        copy.wait()

    def along_z(full):
        mine = rows_at(192 * z + 96 * x, 96)
        return [net.send(full.at[mine], full.at[mine], net.line(d)) for d in range(1, nz)]

    def across_x(full, arrivals):
        sent = []
        for d, copy in enumerate(arrivals, 1):
            copy.wait_recv()
            part = rows_at(192 * net.zplus(nz - d) + 96 * x, 96)
            sent.append(net.send(full.at[part], full.at[part], net.other_x()))
        return sent

    for copy in in_plane["qkv"]:
        copy.wait_recv()
    qkv_z = along_z(w_qkv)
    out_z = [
        net.send(out_s.at[:, half_cols], w_out.at[rows_at(own48, 48), half_cols], net.line(d))
        for d in range(1, nz)
    ]
    for copy in in_plane["fc"]:
        copy.wait_recv()
    fc_z = along_z(w_fc)
    proj_mine = rows_at(192 * z + 96 * x, 96)
    proj_z = [
        net.send(proj_s.at[rows_at(96 * x, 96)], w_proj.at[proj_mine], net.line(d))
        for d in range(1, nz)
    ]
    waits = across_x(w_qkv, qkv_z)
    out_x = []
    for d, copy in enumerate(out_z, 1):
        copy.wait_recv()
        part = w_out.at[rows_at((4 * net.zplus(nz - d) + u) * 48, 48), half_cols]
        out_x.append(net.send(part, part, net.other_x()))
    for copy in out_x:
        copy.wait_recv()

    def out_rows(zz, who):
        return w_out.at[rows_at((4 * zz + who) * 48, 48)]

    out_y = [net.send(out_rows(zz, u), out_rows(zz, u), net.plane(2)) for zz in range(nz)]
    out_c = [net.send(out_rows(zz, u), out_rows(zz, u), net.plane(1)) for zz in range(nz)]
    for zz, copy in enumerate(out_y):
        copy.wait_recv()
        out_c.append(net.send(out_rows(zz, u ^ 2), out_rows(zz, u ^ 2), net.plane(1)))
    waits += out_c
    waits += across_x(w_fc, fc_z)
    waits += across_x(w_proj, proj_z)
    total = vec_u[...].astype(F32)
    row = lax.broadcasted_iota(jnp.int32, total.shape, 0)
    for m, copy in enumerate(vec_p):
        copy.wait_recv()
        total = total + jnp.where(row == 8, 0.0, land_p[m].astype(F32))
    vec[...] = total
    for copy in waits:
        copy.wait_recv()
    net.finish()


def gather_weights(nz, qkv_pre, fc_pre, out_s, proj_s, vec_pre):
    return pl.pallas_call(
        functools.partial(gather_kernel, nz),
        out_shape=(
            jax.ShapeDtypeStruct((768, 576), BF),
            jax.ShapeDtypeStruct((768, 768), BF),
            jax.ShapeDtypeStruct((768, 768), BF),
            jax.ShapeDtypeStruct((768, 768), BF),
            jax.ShapeDtypeStruct((16, 768), F32),
        ),
        in_specs=[VSPEC] * 5,
        out_specs=(VSPEC,) * 5,
        scratch_shapes=[
            pltpu.VMEM((nz - 1, 16, 768), BF),
            pltpu.VMEM((16, 768), BF),
            pltpu.VMEM((3, 16, 768), BF),
            pltpu.SemaphoreType.DMA((64,)),
            pltpu.SemaphoreType.DMA((64,)),
            pltpu.SemaphoreType.DMA((4,)),
        ],
        compiler_params=pltpu.CompilerParams(
            collective_id=0, has_side_effects=True, vmem_limit_bytes=50 * 2**20
        ),
        name="gather_weights",
    )(qkv_pre, fc_pre, out_s, proj_s, vec_pre)


def scatter_kernel(nz, qkv_g, fc_g, proj_g, out_g, vec_g, qkv_o, fc_o, proj_o, out_o, vec_o,
                   qkv_x, fc_x, proj_x, qkv_s, fc_s, proj_s, qkv_z, fc_z, proj_z, qkv_f, fc_f, proj_f,
                   out_c, out_1, out_y, out_2, out_x, out_3, out_z, vec_p, vec_1, vec_z, vec_2, vec_x,
                   send_sem, recv_sem, fsend_sem, frecv_sem):
    net = Net(send_sem, recv_sem, nz)
    x, z, u = net.x, net.z, net.u
    y, c = u // 2, lax.rem(u, 2)
    net.enter()
    vec_m = [net.send(vec_g, vec_p.at[m - 1], net.plane(m)) for m in (1, 2, 3)]

    def start_x(grad, land):
        return [
            net.send(grad.at[rows_at(192 * zz + 96 * (1 - x), 96)], land.at[zz], net.other_x())
            for zz in range(nz)
        ]

    def start_z(copies, grad, land, mine, land_z):
        for zz in range(nz):
            copies[zz].wait_recv()
            mine[zz] = (grad[rows_at(192 * zz + 96 * x, 96), :].astype(F32) + land[zz].astype(F32)).astype(BF)
        return [
            net.send(mine.at[net.zplus(d)], land_z.at[d - 1], net.line(d)) for d in range(1, nz)
        ]

    def end_z(copies, mine, land_z, final):
        total = mine[z].astype(F32)
        for d in range(nz - 1):
            copies[d].wait_recv()
            total = total + land_z[d].astype(F32)
        final[...] = total.astype(BF)

    out_first = net.send(out_g.at[1 - c], out_c, net.plane(1))
    proj_a = start_x(proj_g, proj_x)
    fc_a = start_x(fc_g, fc_x)
    qkv_a = start_x(qkv_g, qkv_x)
    out_first.wait_recv()
    out_1[...] = (out_g[c].astype(F32) + out_c[...].astype(F32)).astype(BF)
    out_second = net.send(out_1.at[1 - y], out_y, net.plane(2))
    total = vec_g[...]
    for m in range(3):
        vec_m[m].wait_recv()
        total = total + vec_p[m]
    vec_1[...] = total
    vec_l = [net.send(vec_1, vec_z.at[d - 1], net.line(d)) for d in range(1, nz)]
    proj_b = start_z(proj_a, proj_g, proj_x, proj_s, proj_z)
    fc_b = start_z(fc_a, fc_g, fc_x, fc_s, fc_z)
    out_second.wait_recv()
    out_2[...] = (out_1[y].astype(F32) + out_y[...].astype(F32)).astype(BF)
    half = lambda which: pl.ds(pl.multiple_of(384 * which, 128), 384)
    out_third = net.send(out_2.at[:, half(1 - x)], out_x, net.other_x())
    total = vec_1[...]
    for d in range(nz - 1):
        vec_l[d].wait_recv()
        total = total + vec_z[d]
    vec_2[...] = total
    vec_last = net.send(vec_2, vec_x, net.other_x())
    qkv_b = start_z(qkv_a, qkv_g, qkv_x, qkv_s, qkv_z)
    out_third.wait_recv()
    out_3[...] = (out_2[:, half(x)].astype(F32) + out_x[...].astype(F32)).astype(BF)
    out_l = [
        net.send(out_3.at[rows_at(48 * net.zplus(d), 48)], out_z.at[d - 1], net.line(d))
        for d in range(1, nz)
    ]
    end_z(proj_b, proj_s, proj_z, proj_f)
    proj_o[rows_at(96 * x, 96), :] = proj_f[...]
    mine = rows_at(96 * x, 96)
    proj_c = net.send(proj_f, proj_o.at[mine], net.other_x())

    finals = []

    def hand_out(base, final, native):
        for xx in range(2):
            for cc in range(2):
                target_x = x ^ xx
                target_u = 2 * x + cc
                here = jnp.logical_and(xx == 0, target_u == u)
                src = final.at[pl.ds(48 * cc, 48)]
                k = base + 2 * xx + cc
                copy = pltpu.make_async_remote_copy(
                    src_ref=src, dst_ref=native.at[u], send_sem=fsend_sem.at[k],
                    recv_sem=frecv_sem.at[base + u], device_id=(target_x, z, target_u), device_id_type=MESH)

                @pl.when(jnp.logical_not(here))
                def _():
                    copy.start()

                @pl.when(here)
                def _():
                    native[u] = final[pl.ds(48 * cc, 48), :]

                finals.append((here, copy))

    def await_native(base, final, native):
        for who in range(4):
            copy = pltpu.make_async_remote_copy(
                src_ref=final.at[pl.ds(0, 48)], dst_ref=native.at[who], send_sem=fsend_sem.at[base],
                recv_sem=frecv_sem.at[base + who], device_id=(1 - x, z, u), device_id_type=MESH)

            @pl.when(jnp.logical_not(jnp.logical_and(x == y, u == who)))
            def _():
                copy.wait_recv()

    end_z(fc_b, fc_s, fc_z, fc_f)
    hand_out(0, fc_f, fc_o)
    total = out_3[rows_at(48 * z, 48), :].astype(F32)
    for d in range(nz - 1):
        out_l[d].wait_recv()
        total = total + out_z[d].astype(F32)
    out_o[:, half(x)] = total.astype(BF)
    out_last = net.send(out_o.at[:, half(x)], out_o.at[:, half(x)], net.other_x())
    end_z(qkv_b, qkv_s, qkv_z, qkv_f)
    hand_out(4, qkv_f, qkv_o)
    vec_last.wait_recv()
    vec_o[...] = vec_2[...] + vec_x[...]
    proj_c.wait_recv()
    out_last.wait_recv()
    await_native(0, fc_f, fc_o)
    await_native(4, qkv_f, qkv_o)
    for here, copy in finals:
        @pl.when(jnp.logical_not(here))
        def _():
            copy.wait_send()
    net.finish()


def scatter_grads(nz, qkv_g, fc_g, proj_g, out_g, vec_g):
    def vm(*shape, kind=BF):
        return pltpu.VMEM(shape, kind)

    return pl.pallas_call(
        functools.partial(scatter_kernel, nz),
        out_shape=(
            jax.ShapeDtypeStruct((4, 48, 576), BF),
            jax.ShapeDtypeStruct((4, 48, 768), BF),
            jax.ShapeDtypeStruct((192, 768), BF),
            jax.ShapeDtypeStruct((48, 768), BF),
            jax.ShapeDtypeStruct((16, 768), F32),
        ),
        in_specs=[VSPEC] * 5,
        out_specs=(VSPEC,) * 5,
        scratch_shapes=[
            vm(nz, 96, 576), vm(nz, 96, 768), vm(nz, 96, 768),
            vm(nz, 96, 576), vm(nz, 96, 768), vm(nz, 96, 768),
            vm(nz - 1, 96, 576), vm(nz - 1, 96, 768), vm(nz - 1, 96, 768),
            vm(96, 576), vm(96, 768), vm(96, 768),
            vm(2, 192, 768), vm(2, 192, 768), vm(192, 768), vm(192, 768), vm(192, 384), vm(192, 384), vm(nz - 1, 48, 384),
            vm(3, 16, 768, kind=F32), vm(16, 768, kind=F32), vm(nz - 1, 16, 768, kind=F32), vm(16, 768, kind=F32), vm(16, 768, kind=F32),
            pltpu.SemaphoreType.DMA((48,)),
            pltpu.SemaphoreType.DMA((48,)),
            pltpu.SemaphoreType.DMA((8,)),
            pltpu.SemaphoreType.DMA((8,)),
        ],
        compiler_params=pltpu.CompilerParams(
            collective_id=1, has_side_effects=True, vmem_limit_bytes=50 * 2**20
        ),
        name="scatter_grads",
    )(qkv_g, fc_g, proj_g, out_g, vec_g)


def arrange_qkv(w):
    rows = w.shape[0]
    parts = w.reshape(rows, 3, 4, 3, 64)
    order = ((0, 0), (0, 1), (1, 0), (1, 1), (2, 0), (2, 1), (1, 2), (2, 2), (0, 2))
    return jnp.stack([parts[:, t, :, h] for t, h in order], 2).transpose(1, 0, 2, 3).reshape(4, rows, 576)


def restore_qkv(g):
    rows = g.shape[1]
    parts = g.reshape(4, rows, 9, 64)
    q = jnp.stack([parts[:, :, i] for i in (0, 1, 8)], 2)
    k = jnp.stack([parts[:, :, i] for i in (2, 3, 6)], 2)
    v = jnp.stack([parts[:, :, i] for i in (4, 5, 7)], 2)
    return jnp.stack([q, k, v], 0).transpose(2, 0, 1, 3, 4).reshape(rows, 2304)


def device_fast(nz, inputs, stretch_order, norm_gains, biases, mid_shift, value_bias, qkv_weight, out_weight, fc_weight, fc_bias, proj_weight, cotangent):
    x, z, u = lax.axis_index("dp"), lax.axis_index("blk"), lax.axis_index("uly")
    qkv_pre = arrange_qkv(qkv_weight)
    fc_pre = fc_weight.reshape(48, nz, 4, 192).transpose(2, 0, 1, 3).reshape(4, 48, 768)
    pack = jnp.concatenate([norm_gains, biases, mid_shift[None], value_bias[None]], 0)
    place = (4 * z + u) * 48
    vec8 = lax.dynamic_update_slice(jnp.zeros((8, 768), BF), pack, (0, place))
    fcb = lax.dynamic_update_slice(jnp.zeros((1, 768), BF), fc_bias[None], (0, 192 * z))
    wide = lax.dynamic_update_slice(jnp.zeros((2, 192), BF), jnp.stack([biases[1], value_bias]), (0, 48 * u))
    zero = jnp.zeros((64,), BF)
    q, v = wide[0].reshape(3, 64), wide[1].reshape(3, 64)
    local = jnp.concatenate([q[0], q[1], zero, zero, v[0], v[1], zero, v[2], q[2], jnp.zeros((192,), BF)])[None]
    four = lax.dynamic_update_slice(jnp.zeros((4, 768), BF), local, (z, 0))
    vec_pre = jnp.concatenate([vec8, fcb, four, jnp.zeros((3, 768), BF)], 0)
    w_qkv, w_fc, w_proj, w_out, vec = gather_weights(nz, qkv_pre, fc_pre, out_weight, proj_weight, vec_pre)
    bias_u = lax.dynamic_slice(vec, (9 + u, 0), (1, 576))
    gains, shifts = vec[0:2], vec[2:6]
    x_own = inputs[0]
    x_all = lax.all_gather(x_own, "uly", axis=0, tiled=True).astype(F32)
    cot_own = cotangent[0]
    cot_all = lax.all_gather(cot_own, "uly", axis=0, tiled=True)
    ln_all, _, _ = layer_norm(x_all, gains[0], shifts[0])
    ln_all = ln_all.astype(BF)
    _, normed_in, inverse_in = layer_norm(x_own.astype(F32), gains[0], shifts[0])
    qkv = (jnp.dot(ln_all, w_qkv, preferred_element_type=F32) + bias_u).astype(BF)
    kv_all = lax.all_gather(qkv[:, 128:512], "blk", axis=0, tiled=True)

    def heads(cols, arr):
        return jnp.stack([arr[:, c:c + 64] for c in cols], 0)

    qh = heads((0, 64, 512), qkv)
    kh, vh = heads((0, 64, 256), kv_all), heads((128, 192, 320), kv_all)
    pos = (stretch_order[0][:, None] * 64 + jnp.arange(64, dtype=jnp.int32)[None]).reshape(-1)
    qpos = lax.dynamic_slice(pos, (512 * z,), (512,))
    causal = qpos[:, None] >= pos[None, :]
    s = jnp.where(causal[None], jnp.einsum("hqd,hkd->hqk", qh, kh, preferred_element_type=F32) * 0.125, -1e30)
    p = jax.nn.softmax(s, -1)
    pl_ = p.astype(BF)
    att = jnp.einsum("hqk,hkd->hqd", pl_, vh, preferred_element_type=F32)
    att_l = att.astype(BF).transpose(1, 0, 2).reshape(4, 128, 192)
    merged = lax.all_to_all(att_l, "uly", 0, 0, tiled=True).transpose(1, 0, 2).reshape(128, 768)
    resid = x_own.astype(F32) + jnp.dot(merged, w_out, preferred_element_type=F32) + shifts[2]
    ln_mid, normed_mid, inverse_mid = layer_norm(resid, gains[1], vec[6])
    lm_all = lax.all_gather(ln_mid.astype(BF), "uly", axis=0, tiled=True)
    pre = jnp.dot(lm_all, w_fc, preferred_element_type=F32) + vec[8]
    act, back = jax.vjp(lambda t: jax.nn.gelu(t, approximate=True), pre)
    act = act.astype(BF)
    out_part = jnp.dot(act, w_proj, preferred_element_type=F32)
    branch = lax.psum_scatter(out_part, "uly", scatter_dimension=0, tiled=True)
    output = (resid + branch + shifts[3]).astype(BF)
    proj_g = jnp.einsum("ta,tb->ab", act, cot_all, preferred_element_type=F32).astype(BF)
    gact = jnp.einsum("tb,ab->ta", cot_all, w_proj, preferred_element_type=F32)
    grad_pre = back(gact)[0].astype(BF)
    fc_g = jnp.einsum("ta,tb->ab", lm_all, grad_pre, preferred_element_type=F32).astype(BF)
    fcb_g = jnp.sum(grad_pre.astype(F32), 0)
    gm_part = jnp.einsum("tb,ab->ta", grad_pre, w_fc, preferred_element_type=F32)
    grad_mid = lax.psum_scatter(gm_part, "uly", scatter_dimension=0, tiled=True)
    cot32 = cot_own.astype(F32)
    grad_resid = cot32 + norm_back(grad_mid, normed_mid, inverse_mid, gains[1])
    gb = grad_resid.astype(BF)
    out_g = jnp.einsum("ta,tb->ab", merged, gb, preferred_element_type=F32).astype(BF)
    gmer = jnp.einsum("tb,ab->ta", gb, w_out, preferred_element_type=F32).astype(BF)
    ga = lax.all_to_all(gmer.reshape(128, 4, 192).transpose(1, 0, 2), "uly", 0, 0, tiled=True)
    ga = ga.reshape(512, 3, 64).transpose(1, 0, 2)
    gp = jnp.einsum("hqd,hkd->hqk", ga, vh, preferred_element_type=F32)
    delta = jnp.sum(ga.astype(F32) * att, -1, keepdims=True)
    gs = (p * (gp - delta)).astype(BF)
    gq = (jnp.einsum("hqk,hkd->qhd", gs, kh, preferred_element_type=F32) * 0.125).astype(BF)
    gk = jnp.einsum("hqk,hqd->khd", gs, qh, preferred_element_type=F32) * 0.125
    gv = jnp.einsum("hqk,hqd->khd", pl_, ga, preferred_element_type=F32)
    kvg = jnp.concatenate([gk[:, 0], gk[:, 1], gv[:, 0], gv[:, 1], gk[:, 2], gv[:, 2]], 1)
    kvg = lax.psum_scatter(kvg, "blk", scatter_dimension=0, tiled=True).astype(BF)
    gqkv = jnp.concatenate([gq[:, 0], gq[:, 1], kvg, gq[:, 2]], 1)
    qkv_g = jnp.einsum("ta,tb->ab", ln_all, gqkv, preferred_element_type=F32).astype(BF)
    qsum = jnp.sum(gqkv.astype(F32), 0)
    gin_part = jnp.einsum("tb,ab->ta", gqkv, w_qkv, preferred_element_type=F32)
    gin = lax.psum_scatter(gin_part, "uly", scatter_dimension=0, tiled=True)
    input_grad = (grad_resid + norm_back(gin, normed_in, inverse_in, gains[0])).astype(BF)
    rows = jnp.stack([
        jnp.sum(gin * normed_in, 0), jnp.sum(grad_mid * normed_mid, 0), jnp.sum(gin, 0),
        jnp.sum(gb.astype(F32), 0), jnp.sum(cot32, 0), jnp.sum(grad_mid, 0)])
    qrow = lax.dynamic_update_slice(jnp.zeros((4, 768), F32), jnp.pad(qsum, (0, 192))[None], (u, 0))
    frow = lax.dynamic_update_slice(jnp.zeros((4, 768), F32), fcb_g[None], (u, 0))
    vec_g = jnp.concatenate([rows, qrow, frow, jnp.zeros((2, 768), F32)], 0)
    og = out_g.reshape(nz, 2, 2, 48, 768).transpose(2, 1, 0, 3, 4).reshape(2, 2, 192, 768)
    qkv_o, fc_o, proj_o, out_o, vec_o = scatter_grads(nz, qkv_g, fc_g, proj_g, og, vec_g)
    mine = lax.dynamic_slice(vec_o, (0, place), (6, 48))
    qs = lax.dynamic_slice(vec_o, (6 + z, 0), (1, 576))[0].reshape(9, 64)
    qb = lax.dynamic_slice(jnp.concatenate([qs[0], qs[1], qs[8]]), (48 * u,), (48,))
    vb = lax.dynamic_slice(jnp.concatenate([qs[4], qs[5], qs[7]]), (48 * u,), (48,))
    fb = lax.dynamic_slice(vec_o, (10 + u, 192 * z), (1, 192))[0]
    return (
        output[None], input_grad[None], mine[0:2],
        jnp.stack([mine[2], qb, mine[3], mine[4]]), mine[5], vb,
        restore_qkv(qkv_o).astype(F32), out_o.astype(F32),
        fc_o.reshape(4, 48, nz, 192).transpose(1, 2, 0, 3).reshape(48, 3072).astype(F32), fb, proj_o.astype(F32))


def solution(mesh):
    placed = (
        P("dp", ("blk", "uly"), None),
        P("dp", None),
        P(None, ("blk", "uly")),
        P(None, ("blk", "uly")),
        P(("blk", "uly")),
        P(("blk", "uly")),
        P(("blk", "uly"), None),
        P(("blk", "uly"), None),
        P(("blk", "uly"), None),
        P(("blk", "uly")),
        P(("blk", "uly"), None),
        P("dp", ("blk", "uly"), None),
    )
    sizes = dict(mesh.shape)
    nz = sizes["blk"]
    fast = sizes["uly"] == 4 and sizes["dp"] == 2 and 768 % (nz * 4 * 16) == 0
    chosen = functools.partial(device_fast, nz) if fast else per_device
    return jax.shard_map(
        chosen,
        mesh=mesh,
        in_specs=placed,
        out_specs=(
            P("dp", ("blk", "uly"), None),
            P("dp", ("blk", "uly"), None),
            P(None, ("blk", "uly")),
            P(None, ("blk", "uly")),
            P(("blk", "uly")),
            P(("blk", "uly")),
            P(("blk", "uly"), None),
            P(("blk", "uly"), None),
            P(("blk", "uly"), None),
            P(("blk", "uly")),
            P(("blk", "uly"), None),
        ),
        check_vma=False,
    )
```

```python
import functools
import math
import types

import jax
import jax.numpy as jnp
from jax import lax
from jax.experimental import pallas as pl
from jax.experimental.pallas import tpu as pltpu
from jax.sharding import PartitionSpec as P

HEADS = 12


masked_score = -1e30


def layer_norm(values, gain, shift):
    center = values - jnp.mean(values, -1, keepdims=True)
    inverse = lax.rsqrt(jnp.mean(center * center, -1, keepdims=True) + 1e-05)
    normed = center * inverse
    return (normed * gain + shift, normed, inverse)


def norm_back(grad_out, normed, inverse, gain):
    scaled = grad_out * gain
    mean_plain = jnp.mean(scaled, -1, keepdims=True)
    mean_mixed = jnp.mean(scaled * normed, -1, keepdims=True)
    return inverse * (scaled - mean_plain - normed * mean_mixed)


def sweep(step_fn, carried, parts):
    row_count = parts[0].shape[1]
    sweep_rows = math.gcd(row_count, 1024)

    def turn(inner, turn_number):
        offset = turn_number * sweep_rows
        blocks = tuple((lax.dynamic_slice_in_dim(part, offset, sweep_rows, 1) for part in parts))
        return (step_fn(inner, blocks, offset), None)

    result, _ = lax.scan(turn, carried, jnp.arange(row_count // sweep_rows, dtype=jnp.int32))
    return result


def per_device(
    inputs,
    stretch_order,
    norm_gains,
    biases,
    mid_shift,
    value_bias,
    qkv_weight,
    out_weight,
    fc_weight,
    fc_bias,
    proj_weight,
    cotangent,
):
    fp32 = jnp.float32
    bf16 = jnp.bfloat16
    gain_rows, shifts, mid_gathered, value_shift, w_qkv, w_out, w_fc, b_fc, w_proj = (
        lax.all_gather(norm_gains, ("blk", "uly"), axis=1, tiled=True),
        lax.all_gather(biases, ("blk", "uly"), axis=1, tiled=True),
        lax.all_gather(mid_shift, ("blk", "uly"), axis=0, tiled=True),
        lax.all_gather(value_bias, ("blk", "uly"), axis=0, tiled=True),
        lax.all_gather(qkv_weight, ("blk", "uly"), axis=0, tiled=True),
        lax.all_gather(out_weight, ("blk", "uly"), axis=0, tiled=True),
        lax.all_gather(fc_weight, ("blk", "uly"), axis=0, tiled=True),
        lax.all_gather(fc_bias, ("blk", "uly"), axis=0, tiled=True),
        lax.all_gather(proj_weight, ("blk", "uly"), axis=0, tiled=True),
    )
    gain_rows = gain_rows.astype(fp32)
    shifts = shifts.astype(fp32)
    mid_gathered = mid_gathered.astype(fp32)
    seq_count, row_len, width = inputs.shape
    uly_count = lax.axis_size("uly")
    local_heads = HEADS // uly_count
    head_dim = width // HEADS
    head_span = local_heads * head_dim
    block_rows = uly_count * row_len
    half_rows = row_len // 2
    seq_len = stretch_order.shape[1] * half_rows
    score_scale = head_dim ** (-0.5)
    tokens = inputs.astype(fp32).reshape(seq_count * row_len, width)
    ln_in, normed_in, inverse_in = layer_norm(tokens, gain_rows[0], shifts[0])
    ln_in = ln_in.astype(bf16)
    qkv_shift = jnp.concatenate([shifts[1], jnp.zeros((width,), fp32), value_shift.astype(fp32)])
    qkv = (jnp.dot(ln_in, w_qkv, preferred_element_type=fp32) + qkv_shift).astype(bf16)
    head_data = lax.all_to_all(
        qkv.reshape(seq_count, row_len, 3, uly_count, head_span),
        "uly",
        split_axis=3,
        concat_axis=1,
        tiled=True,
    )
    queries = head_data[:, :, 0, 0].reshape(seq_count, block_rows, local_heads, head_dim)
    key_rows = head_data[:, :, 1, 0]
    value_rows = head_data[:, :, 2, 0]
    positions = (
        stretch_order[:, :, None] * half_rows
        + jnp.arange(half_rows, dtype=jnp.int32)[None, None, :]
    ).reshape(seq_count, seq_len)
    query_pos = lax.dynamic_slice_in_dim(
        positions, lax.axis_index("blk") * block_rows, block_rows, 1
    )

    def score_block(key_part, key_start):
        part_rows = key_part.shape[1]
        key_pos = lax.dynamic_slice_in_dim(positions, key_start, part_rows, 1)
        scores = (
            jnp.einsum(
                "sqhd,skhd->shqk",
                queries,
                key_part.reshape(seq_count, part_rows, local_heads, head_dim),
                preferred_element_type=fp32,
            )
            * score_scale
        )
        causal = query_pos[:, None, :, None] >= key_pos[:, None, None, :]
        return (scores, causal)

    def stats_step(carried, blocks, key_start):
        row_max, row_total = carried
        scores, causal = score_block(blocks[0], key_start)
        new_max = jnp.maximum(row_max, jnp.max(jnp.where(causal, scores, masked_score), -1))
        row_total = row_total * jnp.exp(row_max - new_max) + jnp.sum(
            jnp.where(causal, jnp.exp(scores - new_max[..., None]), 0.0), -1
        )
        return (new_max, row_total)

    def softmax_of(scores, causal, row_max, row_total):
        return jnp.where(causal, jnp.exp(scores - row_max[..., None]) / row_total[..., None], 0.0)

    def make_output_step(row_max, row_total):

        def output_step(acc_out, blocks, key_start):
            scores, causal = score_block(blocks[0], key_start)
            attn_probs = softmax_of(scores, causal, row_max, row_total).astype(bf16)
            part_rows = blocks[1].shape[1]
            value_part = blocks[1].reshape(seq_count, part_rows, local_heads, head_dim)
            return acc_out + jnp.einsum(
                "shqk,skhd->sqhd", attn_probs, value_part, preferred_element_type=fp32
            )

        return output_step

    stats_init = (
        jnp.full((seq_count, local_heads, block_rows), masked_score, fp32),
        jnp.zeros((seq_count, local_heads, block_rows), fp32),
    )
    empty_out = jnp.zeros((seq_count, block_rows, local_heads, head_dim), fp32)
    all_keys, all_values = (
        lax.all_gather(key_rows, "blk", axis=1, tiled=True),
        lax.all_gather(value_rows, "blk", axis=1, tiled=True),
    )
    row_max, row_total = sweep(stats_step, stats_init, (all_keys,))
    attended = sweep(make_output_step(row_max, row_total), empty_out, (all_keys, all_values))
    attended_low = attended.astype(bf16).reshape(seq_count, block_rows, 1, head_span)
    merged = lax.all_to_all(attended_low, "uly", split_axis=1, concat_axis=2, tiled=True).reshape(
        seq_count * row_len, width
    )
    resid = tokens + (jnp.dot(merged, w_out, preferred_element_type=fp32) + shifts[2])
    ln_mid, normed_mid, inverse_mid = layer_norm(resid, gain_rows[1], mid_gathered)
    ln_mid = ln_mid.astype(bf16)
    pre_act = jnp.dot(ln_mid, w_fc, preferred_element_type=fp32) + b_fc.astype(fp32)

    def gelu_piece(pre_values):
        return jax.nn.gelu(pre_values, approximate=True)

    act, gelu_back = jax.vjp(gelu_piece, pre_act)
    act = act.astype(bf16)
    result = resid + (jnp.dot(act, w_proj, preferred_element_type=fp32) + shifts[3])
    grad_low = cotangent.reshape(seq_count * row_len, width)
    grad_out = grad_low.astype(fp32)
    proj_grad = jnp.einsum("ta,tb->ab", act, grad_low, preferred_element_type=fp32)
    proj_shift_grad = jnp.sum(grad_out, 0)
    grad_act = jnp.einsum("tb,ab->ta", grad_low, w_proj, preferred_element_type=fp32)
    grad_pre = gelu_back(grad_act)[0].astype(bf16)
    fc_grad = jnp.einsum("ta,tb->ab", ln_mid, grad_pre, preferred_element_type=fp32)
    fc_shift_grad = jnp.sum(grad_pre.astype(fp32), 0)
    grad_mid = jnp.einsum("tb,ab->ta", grad_pre, w_fc, preferred_element_type=fp32)
    gain_mid_grad = jnp.sum(grad_mid * normed_mid, 0)
    shift_mid_grad = jnp.sum(grad_mid, 0)
    grad_resid = grad_out + norm_back(grad_mid, normed_mid, inverse_mid, gain_rows[1])
    grad_branch = grad_resid.astype(bf16)
    out_grad = jnp.einsum("ta,tb->ab", merged, grad_branch, preferred_element_type=fp32)
    out_shift_grad = jnp.sum(grad_branch.astype(fp32), 0)
    grad_merged = jnp.einsum("tb,ab->ta", grad_branch, w_out, preferred_element_type=fp32).astype(
        bf16
    )
    grad_att = lax.all_to_all(
        grad_merged.reshape(seq_count, row_len, uly_count, head_span),
        "uly",
        split_axis=2,
        concat_axis=1,
        tiled=True,
    )
    grad_att = grad_att.reshape(seq_count, block_rows, local_heads, head_dim)
    delta = jnp.transpose(jnp.sum(grad_att.astype(fp32) * attended, -1), (0, 2, 1))
    back_keys, back_values = (all_keys, all_values)
    sweep_rows = math.gcd(seq_len, 1024)

    def query_terms(offset):
        key_part = lax.dynamic_slice_in_dim(back_keys, offset, sweep_rows, 1)
        value_part = lax.dynamic_slice_in_dim(back_values, offset, sweep_rows, 1)
        scores, causal = score_block(key_part, offset)
        attn_probs = softmax_of(scores, causal, row_max, row_total)
        key_heads = key_part.reshape(seq_count, sweep_rows, local_heads, head_dim)
        value_heads = value_part.reshape(seq_count, sweep_rows, local_heads, head_dim)
        grad_probs = jnp.einsum(
            "sqhd,skhd->shqk", grad_att, value_heads, preferred_element_type=fp32
        )
        grad_scores = (attn_probs * (grad_probs - delta[..., None])).astype(bf16)
        query_term = (
            jnp.einsum("shqk,skhd->sqhd", grad_scores, key_heads, preferred_element_type=fp32)
            * score_scale
        )
        return (query_term, grad_scores, attn_probs.astype(bf16))

    query_init = jnp.zeros((seq_count, block_rows, local_heads, head_dim), fp32)

    def back_step(carried, turn_number):
        grad_query, kv_buffer = carried
        offset = turn_number * sweep_rows
        query_term, grad_scores, probs_low = query_terms(offset)
        grad_key = (
            jnp.einsum("shqk,sqhd->skhd", grad_scores, queries, preferred_element_type=fp32)
            * score_scale
        )
        grad_value = jnp.einsum("shqk,sqhd->skhd", probs_low, grad_att, preferred_element_type=fp32)
        kv_pair = jnp.stack(
            [
                grad_key.reshape(seq_count, sweep_rows, head_span),
                grad_value.reshape(seq_count, sweep_rows, head_span),
            ],
            2,
        )
        kv_buffer = lax.dynamic_update_slice_in_dim(kv_buffer, kv_pair, offset, 1)
        return ((grad_query + query_term, kv_buffer), None)

    back_init = (query_init, jnp.zeros((seq_count, seq_len, 2, head_span), fp32))
    back_done, _ = lax.scan(
        back_step, back_init, jnp.arange(seq_len // sweep_rows, dtype=jnp.int32)
    )
    grad_query, kv_buffer = back_done
    kv_summed = lax.psum_scatter(
        kv_buffer.astype(jnp.bfloat16), "blk", scatter_dimension=1, tiled=True
    ).astype(jnp.float32)
    grad_heads = jnp.concatenate(
        [
            grad_query.reshape(seq_count, block_rows, 1, head_span).astype(bf16),
            kv_summed.astype(bf16),
        ],
        2,
    )
    grad_qkv = lax.all_to_all(
        grad_heads.reshape(seq_count, block_rows, 3, 1, head_span),
        "uly",
        split_axis=1,
        concat_axis=3,
        tiled=True,
    )
    grad_qkv = grad_qkv.reshape(seq_count * row_len, 3 * width)
    qkv_grad = jnp.einsum("ta,tb->ab", ln_in, grad_qkv, preferred_element_type=fp32)
    column_sums = jnp.sum(grad_qkv.astype(fp32), 0)
    grad_in_norm = jnp.einsum("tb,ab->ta", grad_qkv, w_qkv, preferred_element_type=fp32)
    gain_in_grad = jnp.sum(grad_in_norm * normed_in, 0)
    shift_in_grad = jnp.sum(grad_in_norm, 0)
    grad_input = grad_resid + norm_back(grad_in_norm, normed_in, inverse_in, gain_rows[0])
    gains_grad = jnp.stack([gain_in_grad, gain_mid_grad])
    biases_grad = jnp.stack([shift_in_grad, column_sums[:width], out_shift_grad, proj_shift_grad])
    value_grad = column_sums[2 * width :]
    shard_grads = (
        lax.psum_scatter(gains_grad, ("blk", "uly"), scatter_dimension=1, tiled=True),
        lax.psum_scatter(biases_grad, ("blk", "uly"), scatter_dimension=1, tiled=True),
        lax.psum_scatter(shift_mid_grad, ("blk", "uly"), scatter_dimension=0, tiled=True),
        lax.psum_scatter(value_grad, ("blk", "uly"), scatter_dimension=0, tiled=True),
        lax.psum_scatter(qkv_grad, ("blk", "uly"), scatter_dimension=0, tiled=True),
        lax.psum_scatter(out_grad, ("blk", "uly"), scatter_dimension=0, tiled=True),
        lax.psum_scatter(fc_grad, ("blk", "uly"), scatter_dimension=0, tiled=True),
        lax.psum_scatter(fc_shift_grad, ("blk", "uly"), scatter_dimension=0, tiled=True),
        lax.psum_scatter(proj_grad, ("blk", "uly"), scatter_dimension=0, tiled=True),
    )
    shard_grads = (
        lax.psum(shard_grads[0].astype(jnp.bfloat16), "dp").astype(jnp.float32),
        lax.psum(shard_grads[1].astype(jnp.bfloat16), "dp").astype(jnp.float32),
        lax.psum(shard_grads[2].astype(jnp.bfloat16), "dp").astype(jnp.float32),
        lax.psum(shard_grads[3].astype(jnp.bfloat16), "dp").astype(jnp.float32),
        lax.psum(shard_grads[4].astype(jnp.bfloat16), "dp").astype(jnp.float32),
        lax.psum(shard_grads[5].astype(jnp.bfloat16), "dp").astype(jnp.float32),
        lax.psum(shard_grads[6].astype(jnp.bfloat16), "dp").astype(jnp.float32),
        lax.psum(shard_grads[7].astype(jnp.bfloat16), "dp").astype(jnp.float32),
        lax.psum(shard_grads[8].astype(jnp.bfloat16), "dp").astype(jnp.float32),
    )
    output = result.astype(bf16).reshape(seq_count, row_len, width)
    input_grad = grad_input.astype(bf16).reshape(seq_count, row_len, width)
    return (
        output,
        input_grad,
        shard_grads[0],
        shard_grads[1],
        shard_grads[2],
        shard_grads[3],
        shard_grads[4],
        shard_grads[5],
        shard_grads[6],
        shard_grads[7],
        shard_grads[8],
    )


MESH = pl.DeviceIdType.MESH
BF = jnp.bfloat16
F32 = jnp.float32
VSPEC = pl.BlockSpec(memory_space=pltpu.VMEM)
GELU_IN = math.sqrt(2.0 / math.pi)


class Net:
    def __init__(self, send_sem, recv_sem, nz):
        self.send_sem, self.recv_sem = send_sem, recv_sem
        self.count = 0
        self.sent = []
        self.nz = nz
        self.x = lax.axis_index("dp")
        self.z = lax.axis_index("blk")
        self.u = lax.axis_index("uly")

    def send(self, src, dst, dev):
        k = self.count
        self.count += 1
        copy = pltpu.make_async_remote_copy(
            src_ref=src,
            dst_ref=dst,
            send_sem=self.send_sem.at[k],
            recv_sem=self.recv_sem.at[k],
            device_id=dev,
            device_id_type=MESH,
        )
        copy.start()
        self.sent.append(copy)
        return copy

    def plane(self, m):
        return (self.x, self.z, self.u ^ m)

    def other_x(self):
        return (1 - self.x, self.z, self.u)

    def zplus(self, d):
        return lax.rem(self.z + d, self.nz)

    def line(self, d):
        return (self.x, self.zplus(d), self.u)

    def enter(self):
        barrier = pltpu.get_barrier_semaphore()
        near = [self.plane(m) for m in (1, 2, 3)] + [self.other_x()]
        near += [self.line(d) for d in range(1, self.nz)]
        near += [(1 - self.x, self.z, self.u ^ m) for m in (1, 2, 3)]
        for dev in near:
            pl.semaphore_signal(barrier, inc=1, device_id=dev, device_id_type=MESH)
        pl.semaphore_wait(barrier, len(near))

    def finish(self):
        for copy in self.sent:
            copy.wait_send()


def rows_at(start, count):
    return pl.ds(pl.multiple_of(start, 16), count)


def dot_nn(a, b):
    return jnp.dot(a, b, preferred_element_type=F32)


def dot_nt(a, b):
    return lax.dot_general(a, b, (((1,), (1,)), ((), ())), preferred_element_type=F32)


def dot_tn(a, b):
    return lax.dot_general(a, b, (((0,), (0,)), ((), ())), preferred_element_type=F32)


def loop(count, body):
    def step(i, carry):
        body(i)
        return carry

    lax.fori_loop(0, count, step, 0)


def block_kernel(nz, refs):
    r = refs
    net = Net(r.send_sem, r.recv_sem, nz)
    x, z, u = net.x, net.z, net.u
    y, c = u // 2, lax.rem(u, 2)
    own48 = (4 * z + u) * 48
    tile = lambda t: rows_at(128 * t, 128)
    half_cols = lambda which: pl.ds(pl.multiple_of(384 * which, 128), 384)
    lane = lambda shape: lax.broadcasted_iota(jnp.int32, shape, 1)

    local = [
        pltpu.make_async_copy(r.qkv_pre.at[u], r.w_qkv.at[rows_at(own48, 48)], r.local_sem.at[0]),
        pltpu.make_async_copy(r.fc_pre.at[u], r.w_fc.at[rows_at(own48, 48)], r.local_sem.at[1]),
        pltpu.make_async_copy(r.proj_s, r.w_proj.at[rows_at(192 * z, 192)], r.local_sem.at[2]),
        pltpu.make_async_copy(r.out_s, r.w_out.at[rows_at(own48, 48)], r.local_sem.at[3]),
        pltpu.make_async_copy(r.x_own, r.x_all.at[tile(u)], r.local_sem.at[4]),
        pltpu.make_async_copy(r.cot_own, r.cot_all.at[tile(u)], r.local_sem.at[5]),
    ]
    for copy in local:
        copy.start()
    net.enter()

    def plane_gather_start(own, full):
        return [net.send(own, full.at[tile(u)], net.plane(m)) for m in (2, 1)]

    def plane_gather_forward(sent, full):
        sent[0].wait_recv()
        sent.append(net.send(full.at[tile(u ^ 2)], full.at[tile(u ^ 2)], net.plane(1)))

    in_plane = lambda pre, full: [
        net.send(pre.at[u ^ m], full.at[rows_at(own48, 48)], net.plane(m)) for m in (1, 2, 3)
    ]
    qkv_p = in_plane(r.qkv_pre, r.w_qkv)
    x_g = plane_gather_start(r.x_own, r.x_all)
    vec_z = [net.send(r.vec_pre, r.vec_land_z.at[d - 1], net.line(d)) for d in range(1, nz)]

    def along_z(full):
        mine = rows_at(192 * z + 96 * x, 96)
        return [net.send(full.at[mine], full.at[mine], net.line(d)) for d in range(1, nz)]

    def across_x(full, arrivals):
        sent = []
        for d, copy in enumerate(arrivals, 1):
            copy.wait_recv()
            part = rows_at(192 * net.zplus(nz - d) + 96 * x, 96)
            sent.append(net.send(full.at[part], full.at[part], net.other_x()))
        return sent

    local[0].wait()
    for copy in qkv_p:
        copy.wait_recv()
    qkv_z = along_z(r.w_qkv)
    total = r.vec_pre[...]
    for d in range(nz - 1):
        vec_z[d].wait_recv()
        total = total + r.vec_land_z[d]
    r.vec_u[...] = total
    vec_p = [net.send(r.vec_u, r.vec_land_p.at[m - 1], net.plane(m)) for m in (1, 2, 3)]
    plane_gather_forward(x_g, r.x_all)
    fc_p = in_plane(r.fc_pre, r.w_fc)
    proj_mine = rows_at(192 * z + 96 * x, 96)
    total = r.vec_u[...].astype(F32)
    row = lax.broadcasted_iota(jnp.int32, total.shape, 0)
    for m in range(3):
        vec_p[m].wait_recv()
        total = total + jnp.where(row == 8, 0.0, r.vec_land_p[m].astype(F32))
    r.vec[...] = total
    for copy in local[1:]:
        copy.wait()
    for copy in x_g[1:]:
        copy.wait_recv()
    gain = lambda i: r.vec[pl.ds(i, 1), :]

    def normalize(values):
        center = values - jnp.mean(values, -1, keepdims=True)
        inverse = lax.rsqrt(jnp.mean(center * center, -1, keepdims=True) + 1e-05)
        return center * inverse, inverse

    def ln_tile(t):
        normed, _ = normalize(r.x_all[tile(t), :].astype(F32))
        r.ln_all[tile(t), :] = (normed * gain(0) + gain(2)).astype(BF)

    loop(4, ln_tile)
    proj_z = [
        net.send(r.proj_s.at[rows_at(96 * x, 96)], r.w_proj.at[proj_mine], net.line(d))
        for d in range(1, nz)
    ]
    qkv_x = across_x(r.w_qkv, qkv_z)
    out_z = [
        net.send(r.out_s.at[:, half_cols(x)], r.w_out.at[rows_at(own48, 48), half_cols(x)], net.line(d))
        for d in range(1, nz)
    ]
    cot_g = plane_gather_start(r.cot_own, r.cot_all)
    r.qm[2] = jnp.zeros((512, 128), BF)
    for copy in qkv_x:
        copy.wait_recv()

    bias_u = jnp.sum(jnp.where(row == 9 + u, r.vec[...], 0.0), 0, keepdims=True)[:, 0:576]

    def qkv_tile(t):
        res = dot_nn(r.ln_all[tile(t), :], r.w_qkv[...]) + bias_u
        res = res.astype(BF)
        q01 = res[:, 0:128].astype(F32) * 0.125
        low = lane(q01.shape) < 64
        r.qm[0, tile(t), :] = jnp.where(low, q01, 0.0).astype(BF)
        r.qm[1, tile(t), :] = jnp.where(low, 0.0, q01).astype(BF)
        r.qm[2, tile(t), 0:64] = (res[:, 512:576].astype(F32) * 0.125).astype(BF)
        r.kv_all[z, tile(t), :] = res[:, 128:512]

    loop(4, qkv_tile)

    def kv_copy(way, step):
        block = z - step if way == 0 else z + step
        target = z + 1 if way == 0 else z - 1
        block, target = jnp.clip(block, 0, nz - 1), jnp.clip(target, 0, nz - 1)
        return pltpu.make_async_remote_copy(
            src_ref=r.kv_all.at[block], dst_ref=r.kv_all.at[block],
            send_sem=r.kv_send.at[way * nz + step], recv_sem=r.kv_recv.at[way * nz + step],
            device_id=(x, target, u), device_id_type=MESH)

    def kv_sends(way, step):
        if way == 0:
            return jnp.logical_and(z - step >= 0, z + 1 < nz)
        return jnp.logical_and(z + step < nz, z >= 1)

    def kv_start(step):
        for way in range(2):
            @pl.when(kv_sends(way, step))
            def _():
                kv_copy(way, step).start()

    def attend(j):
        qp = r.pos_row[:, pl.ds(pl.multiple_of(512 * z, 128), 512)]
        for h in range(3):
            kc = 0 if h < 2 else 256
            vc = 128 if h < 2 else 256
            q = r.qm[h]

            def score(kt, top):
                s = dot_nt(r.kv_all[j, rows_at(128 * kt, 128), kc:kc + 128], q)
                kp = r.pos_col[pl.ds(pl.multiple_of(512 * j + 128 * kt, 128), 128), :]
                s = jnp.where(kp <= qp, s, -1e30)
                r.s_buf[rows_at(128 * kt, 128), :] = s
                return jnp.maximum(top, jnp.max(s, 0, keepdims=True))

            old = r.m_run[h]
            top = lax.fori_loop(0, 4, score, old)
            shrink = jnp.exp(old - top)

            def weigh(kt, got):
                p = jnp.exp(r.s_buf[rows_at(128 * kt, 128), :] - top)
                r.pt[j * 3 + h, rows_at(128 * kt, 128), :] = p.astype(BF)
                return got + jnp.sum(p, 0, keepdims=True)

            got = lax.fori_loop(0, 4, weigh, jnp.zeros((1, 512), F32))
            r.m_run[h] = top
            r.m_at[j * 3 + h] = top
            r.l_run[h] = r.l_run[h] * shrink + got
            r.o_t[h] = r.o_t[h] * shrink + dot_tn(r.kv_all[j, :, vc:vc + 128], r.pt[j * 3 + h])

    r.m_run[...] = jnp.full((3, 1, 512), -1e30, F32)
    r.l_run[...] = jnp.zeros((3, 1, 512), F32)
    r.o_t[...] = jnp.zeros((3, 128, 512), F32)
    kv_start(0)
    for copy in fc_p:
        copy.wait_recv()
    fc_z = along_z(r.w_fc)
    plane_gather_forward(cot_g, r.cot_all)
    attend(z)

    weights = {}
    for step in range(1, nz):
        for way in range(2):
            @pl.when(z - step >= 0 if way == 0 else z + step < nz)
            def _():
                kv_copy(way, step - 1).wait_recv()

        if step < nz - 1:
            kv_start(step)
        if step == 1:
            weights["proj"] = across_x(r.w_proj, proj_z)
            out_x = []
            for d, copy in enumerate(out_z, 1):
                copy.wait_recv()
                part = r.w_out.at[rows_at((4 * net.zplus(nz - d) + u) * 48, 48), half_cols(x)]
                out_x.append(net.send(part, part, net.other_x()))
        if step == 2:
            out_rows = lambda zz, who: r.w_out.at[rows_at((4 * zz + who) * 48, 48)]
            for copy in out_x:
                copy.wait_recv()
            out_y = [net.send(out_rows(zz, u), out_rows(zz, u), net.plane(2)) for zz in range(nz)]
            out_c = [net.send(out_rows(zz, u), out_rows(zz, u), net.plane(1)) for zz in range(nz)]

        def either(way):
            j = jnp.where(way == 0, z - step, z + step)

            @pl.when(jnp.logical_and(j >= 0, j < nz))
            def _():
                attend(j)

        loop(2, either)
        if step == nz - 1:
            for zz, copy in enumerate(out_y):
                copy.wait_recv()
                out_c.append(net.send(out_rows(zz, u ^ 2), out_rows(zz, u ^ 2), net.plane(1)))
    weights["fc"] = across_x(r.w_fc, fc_z)

    rowi = lax.broadcasted_iota(jnp.int32, (128, 512), 0)
    r.l_inv[...] = 1.0 / r.l_run[...]
    r.att_t[0] = jnp.where(rowi < 64, r.o_t[0] * r.l_inv[0], r.o_t[1] * r.l_inv[1])
    r.att_t[1] = jnp.where(rowi < 64, 0.0, r.o_t[2] * r.l_inv[2])
    r.att[:, 0:128] = jnp.transpose(r.att_t[0]).astype(BF)
    r.att[:, 128:256] = jnp.transpose(r.att_t[1]).astype(BF)
    att_p = [net.send(r.att.at[tile(u ^ m)], r.merged.at[u], net.plane(m)) for m in (2, 3, 1)]
    r.merged[u] = r.att[tile(u), :]

    for copy in out_c:
        copy.wait_recv()
    for g in range(4):
        r.w_outp[256 * g:256 * g + 128, :] = r.w_out[192 * g:192 * g + 128, :]
        r.w_outp[256 * g + 128:256 * g + 192, :] = jnp.zeros((64, 768), BF)
        r.w_outp[256 * g + 192:256 * g + 256, :] = r.w_out[192 * g + 128:192 * g + 192, :]
    for copy in cot_g[1:]:
        copy.wait_recv()
    for copy in weights["proj"]:
        copy.wait_recv()

    def gact_tile(t):
        r.gact[tile(t), :] = dot_nt(r.cot_all[tile(t), :], r.w_proj[...])

    loop(4, gact_tile)
    for copy in att_p:
        copy.wait_recv()
    resid = r.x_own[...].astype(F32) + gain(4)
    for g in range(4):
        resid = resid + dot_nn(r.merged[g], r.w_outp[256 * g:256 * g + 256, :])
    r.resid[...] = resid
    normed, inverse = normalize(resid)
    r.normed_mid[...] = normed
    r.inverse_mid[...] = inverse
    r.lm_all[tile(u), :] = (normed * gain(1) + gain(6)).astype(BF)
    lm_own = r.lm_all.at[tile(u)]
    lm_g = [net.send(lm_own, lm_own, net.plane(m)) for m in (2, 1)]
    for copy in weights["fc"]:
        copy.wait_recv()

    r.vec_g[...] = jnp.zeros((16, 768), F32)

    def mlp_tile(t, part):
        rows = tile(t)
        pre = dot_nn(r.lm_all[rows, :], r.w_fc[...]) + gain(8)
        square = pre * pre
        th = jnp.tanh(GELU_IN * (pre * (1.0 + 0.044715 * square)))
        r.act[rows, :] = (0.5 * pre * (1.0 + th)).astype(BF)
        slope = 0.5 * (1.0 + th) + (0.5 * GELU_IN) * pre * (1.0 - th * th) * (1.0 + 0.134145 * square)
        gp = (slope * r.gact[rows, :]).astype(BF)
        r.grad_pre[rows, :] = gp
        r.fcb[...] += jnp.sum(gp.astype(F32), 0, keepdims=True)
        part[t] = dot_nt(gp, r.w_fc[...]).astype(BF)

    r.fcb[...] = jnp.zeros((1, 768), F32)
    mlp_tile(u, r.gm_part)
    lm_g[1].wait_recv()
    mlp_tile(u ^ 1, r.gm_part)
    plane_gather_forward(lm_g, r.lm_all)

    def reduce_core(i, t, part, land_c):
        return net.send(part.at[t], land_c.at[i], net.plane(1))

    def reduce_y(copy, part, land_c, mid, land_y):
        copy.wait_recv()
        mid[...] = (part[u ^ 2].astype(F32) + land_c[0].astype(F32)).astype(BF)
        return net.send(mid, land_y, net.plane(2))

    def reduce_end(copy_c, copy_y, part, land_c, land_y):
        copy_c.wait_recv()
        copy_y.wait_recv()
        return part[u].astype(F32) + land_c[1].astype(F32) + land_y[...].astype(F32)

    gm_c1 = reduce_core(1, u ^ 1, r.gm_part, r.gm_c)
    mlp_tile(u ^ 2, r.gm_part)
    lm_g[2].wait_recv()
    mlp_tile(u ^ 3, r.gm_part)
    gm_c0 = reduce_core(0, u ^ 3, r.gm_part, r.gm_c)
    r.vec_g[...] += jnp.where(row == 10 + u, r.fcb[...], 0.0)

    def branch_tile(t):
        r.br_part[t] = dot_nn(r.act[tile(t), :], r.w_proj[...]).astype(BF)

    branch_tile(u ^ 3)
    branch_tile(u ^ 1)
    gm_y = reduce_y(gm_c0, r.gm_part, r.gm_c, r.gm_mid, r.gm_y)
    br_c = [reduce_core(0, u ^ 3, r.br_part, r.br_c), reduce_core(1, u ^ 1, r.br_part, r.br_c)]
    branch_tile(u ^ 2)
    branch_tile(u)

    def weight_grad(a, b, out, tiles):
        def one(i):
            cols = pl.ds(pl.multiple_of(128 * i, 128), 128)
            out[tile(i), :] = dot_tn(a[:, cols], b[...]).astype(BF)

        loop(tiles, one)

    def start_x(grad, land):
        return [
            net.send(grad.at[rows_at(192 * zz + 96 * (1 - x), 96)], land.at[zz], net.other_x())
            for zz in range(nz)
        ]

    def start_z(copies, grad, land, mine, land_z):
        for zz in range(nz):
            copies[zz].wait_recv()
            mine[zz] = (grad[rows_at(192 * zz + 96 * x, 96), :].astype(F32) + land[zz].astype(F32)).astype(BF)
        return [
            net.send(mine.at[net.zplus(d)], land_z.at[d - 1], net.line(d)) for d in range(1, nz)
        ]

    def end_z(copies, mine, land_z, final):
        total = mine[z].astype(F32)
        for d in range(nz - 1):
            copies[d].wait_recv()
            total = total + land_z[d].astype(F32)
        final[...] = total.astype(BF)

    weight_grad(r.act, r.cot_all, r.proj_g, 6)
    proj_a = start_x(r.proj_g, r.proj_x)

    gm = reduce_end(gm_c1, gm_y, r.gm_part, r.gm_c, r.gm_y)
    normed = r.normed_mid[...]
    r.vec_g[1:2, :] = jnp.sum(gm * normed, 0, keepdims=True)
    r.vec_g[5:6, :] = jnp.sum(gm, 0, keepdims=True)

    def norm_grad(grad, normed, inverse, g):
        e = grad * g
        return inverse * (
            e - jnp.mean(e, -1, keepdims=True) - normed * jnp.mean(e * normed, -1, keepdims=True)
        )

    cot = r.cot_own[...].astype(F32)
    r.vec_g[4:5, :] = jnp.sum(cot, 0, keepdims=True)
    grad_resid = cot + norm_grad(gm, normed, r.inverse_mid[...], gain(1))
    r.grad_resid[...] = grad_resid
    gb = grad_resid.astype(BF)
    r.gb[...] = gb
    r.vec_g[3:4, :] = jnp.sum(gb.astype(F32), 0, keepdims=True)

    def gmer_tile(g):
        r.gmer[g] = dot_nt(r.gb[...], r.w_outp[pl.ds(pl.multiple_of(256 * g, 256), 256), :]).astype(BF)

    loop(4, gmer_tile)
    ga_p = [net.send(r.gmer.at[u ^ m], r.ga.at[tile(u)], net.plane(m)) for m in (2, 3, 1)]
    r.ga[tile(u), :] = r.gmer[u]
    br_y = reduce_y(br_c[0], r.br_part, r.br_c, r.br_mid, r.br_y)
    weight_grad(r.lm_all, r.grad_pre, r.fc_g, 6)
    fc_a = start_x(r.fc_g, r.fc_x)
    for g in range(4):
        res = dot_tn(r.merged[g], r.gb[...]).astype(BF)
        at = slice(48 * g, 48 * g + 48)
        r.out_g[0, 0, at, :] = res[0:48]
        r.out_g[1, 0, at, :] = res[48:96]
        r.out_g[0, 1, 48 * g:48 * g + 32, :] = res[96:128]
        r.out_g[0, 1, 48 * g + 32:48 * g + 48, :] = res[192:208]
        r.out_g[1, 1, at, :] = res[208:256]
    og_c = net.send(r.out_g.at[1 - c], r.og_c, net.plane(1))
    r.output[...] = (
        r.resid[...] + gain(5) + reduce_end(br_c[1], br_y, r.br_part, r.br_c, r.br_y)
    ).astype(BF)
    for copy in ga_p:
        copy.wait_recv()

    low = lane((512, 128)) < 64
    ga01 = r.ga[:, 0:128]
    zero = jnp.zeros((512, 128), BF)
    r.gam[0] = jnp.where(low, ga01.astype(F32), 0.0).astype(BF)
    r.gam[1] = jnp.where(low, 0.0, ga01.astype(F32)).astype(BF)
    r.gam[2] = r.ga[:, 128:256]
    prod = jnp.transpose(ga01.astype(F32)) * r.att_t[0]
    r.delta[0] = jnp.sum(prod[0:64], 0, keepdims=True)
    r.delta[1] = jnp.sum(prod[64:128], 0, keepdims=True)
    prod = jnp.transpose(r.ga[:, 128:256].astype(F32)) * r.att_t[1]
    r.delta[2] = jnp.sum(prod, 0, keepdims=True)
    r.dq_t[...] = jnp.zeros((3, 128, 512), F32)

    def back(j):
        factor = [jnp.exp(r.m_at[j * 3 + h] - r.m_run[h]) * r.l_inv[h] for h in range(3)]

        def keys(kt):
            rows = rows_at(128 * kt, 128)
            for h in range(3):
                vc = 128 if h < 2 else 256
                p = r.pt[j * 3 + h, rows, :].astype(F32) * factor[h]
                dp = dot_nt(r.kv_all[j, rows, vc:vc + 128], r.gam[h])
                r.ds[h, rows, :] = (p * (dp - r.delta[h])).astype(BF)
                r.pt[j * 3 + h, rows, :] = p.astype(BF)

        def sums(kt):
            rows = rows_at(128 * kt, 128)
            pair = lambda of, first, second: dot_nn(of(0), first) + dot_nn(of(1), second)
            ds = lambda h: r.ds[h, rows, :]
            p = lambda h: r.pt[j * 3 + h, rows, :]
            r.dkv[rows, 0:128] = pair(ds, r.qm[0], r.qm[1])
            r.dkv[rows, 128:256] = pair(p, r.gam[0], r.gam[1])
            r.dkv[rows, 256:384] = dot_nn(ds(2), r.qm[2]) + dot_nn(p(2), r.gam[2])

        loop(4, keys)
        loop(4, sums)
        for h in range(3):
            kc = 0 if h < 2 else 256
            r.dq_t[h] += dot_tn(r.kv_all[j, :, kc:kc + 128], r.ds[h])

    def chain_copy(way, step):
        target = jnp.clip(jnp.where(way == 0, z - 1, z + 1), 0, nz - 1)
        at = way * (nz - 1) + step - 1
        return pltpu.make_async_remote_copy(
            src_ref=r.chain.at[at], dst_ref=r.chain_land.at[at],
            send_sem=r.ch_send.at[at], recv_sem=r.ch_recv.at[at],
            device_id=(x, target, u), device_id_type=MESH)

    def chain_step(step):
        def either(way):
            j = jnp.where(way == 0, z - step, z + step)
            behind = jnp.where(way == 0, z + 1, z - 1)

            @pl.when(jnp.logical_and(j >= 0, j < nz))
            def _():
                back(j)
                at = way * (nz - 1) + step - 1
                comes = jnp.logical_and(behind >= 0, behind < nz)
                if step < nz - 1:
                    @pl.when(comes)
                    def _():
                        chain_copy(way, step + 1).wait_recv()
                        r.chain[at] = (r.dkv[...] + r.chain_land[at + 1].astype(F32)).astype(BF)

                    @pl.when(jnp.logical_not(comes))
                    def _():
                        r.chain[at] = r.dkv[...].astype(BF)
                else:
                    r.chain[at] = r.dkv[...].astype(BF)
                chain_copy(way, step).start()

        loop(2, either)

    for step in range(nz - 1, 0, -1):
        chain_step(step)
        if step == nz - 1:
            proj_b = start_z(proj_a, r.proj_g, r.proj_x, r.proj_m, r.proj_z)
            og_c.wait_recv()
            r.og_1[...] = (r.out_g[c].astype(F32) + r.og_c[...].astype(F32)).astype(BF)
            og_y = net.send(r.og_1.at[1 - y], r.og_y, net.plane(2))
        if step == nz - 2:
            fc_b = start_z(fc_a, r.fc_g, r.fc_x, r.fc_m, r.fc_z)
            og_y.wait_recv()
            r.og_2[...] = (r.og_1[y].astype(F32) + r.og_y[...].astype(F32)).astype(BF)
            og_x = net.send(r.og_2.at[:, half_cols(1 - x)], r.og_x, net.other_x())
        if step == 1:
            og_x.wait_recv()
            r.og_3[...] = (r.og_2[:, half_cols(x)].astype(F32) + r.og_x[...].astype(F32)).astype(BF)
            og_z = [
                net.send(r.og_3.at[rows_at(48 * net.zplus(d), 48)], r.og_z.at[d - 1], net.line(d))
                for d in range(1, nz)
            ]
    back(z)

    @pl.when(z + 1 < nz)
    def _():
        chain_copy(0, 1).wait_recv()
        r.dkv[...] += r.chain_land[0].astype(F32)

    @pl.when(z >= 1)
    def _():
        chain_copy(1, 1).wait_recv()
        r.dkv[...] += r.chain_land[nz - 1].astype(F32)

    r.gqkv[:, 128:512] = r.dkv[...].astype(BF)
    dq = jnp.transpose(jnp.where(rowi < 64, r.dq_t[0], r.dq_t[1]) * 0.125)
    r.gqkv[:, 0:128] = dq.astype(BF)
    r.gqkv[:, 512:576] = jnp.transpose(r.dq_t[2] * 0.125)[:, 0:64].astype(BF)

    weight_grad(r.ln_all, r.gqkv, r.qkv_g, 6)
    qkv_a = start_x(r.qkv_g, r.qkv_x)

    def gin_tile(t):
        r.gi_part[t] = dot_nt(r.gqkv[tile(t), :], r.w_qkv[...]).astype(BF)

    gin_tile(u ^ 3)
    gi_c0 = reduce_core(0, u ^ 3, r.gi_part, r.gi_c)
    gin_tile(u ^ 1)
    gi_c1 = reduce_core(1, u ^ 1, r.gi_part, r.gi_c)
    gin_tile(u ^ 2)
    gi_y = reduce_y(gi_c0, r.gi_part, r.gi_c, r.gi_mid, r.gi_y)
    gin_tile(u)
    r.vec_g[:, 0:576] += jnp.where(row[:, 0:576] == 6 + u, jnp.sum(r.gqkv[...].astype(F32), 0, keepdims=True), 0.0)
    qkv_b = start_z(qkv_a, r.qkv_g, r.qkv_x, r.qkv_m, r.qkv_z)
    end_z(proj_b, r.proj_m, r.proj_z, r.proj_f)
    mine = rows_at(96 * x, 96)
    r.proj_o[mine, :] = r.proj_f[...]
    proj_c = net.send(r.proj_f, r.proj_o.at[mine], net.other_x())

    finals = []

    def hand_out(base, final, native):
        for xx in range(2):
            for cc in range(2):
                target_x = x ^ xx
                target_u = 2 * x + cc
                here = jnp.logical_and(xx == 0, target_u == u)
                k = base + 2 * xx + cc
                copy = pltpu.make_async_remote_copy(
                    src_ref=final.at[pl.ds(48 * cc, 48)], dst_ref=native.at[u], send_sem=r.f_send.at[k],
                    recv_sem=r.f_recv.at[base + u], device_id=(target_x, z, target_u), device_id_type=MESH)

                @pl.when(jnp.logical_not(here))
                def _():
                    copy.start()

                @pl.when(here)
                def _():
                    native[u] = final[pl.ds(48 * cc, 48), :]

                finals.append((here, copy))

    def await_native(base, final, native):
        for who in range(4):
            copy = pltpu.make_async_remote_copy(
                src_ref=final.at[pl.ds(0, 48)], dst_ref=native.at[who], send_sem=r.f_send.at[base],
                recv_sem=r.f_recv.at[base + who], device_id=(1 - x, z, u), device_id_type=MESH)

            @pl.when(jnp.logical_not(jnp.logical_and(x == y, u == who)))
            def _():
                copy.wait_recv()

    gin = reduce_end(gi_c1, gi_y, r.gi_part, r.gi_c, r.gi_y)
    normed, inverse = normalize(r.x_own[...].astype(F32))
    r.vec_g[0:1, :] = jnp.sum(gin * normed, 0, keepdims=True)
    r.vec_g[2:3, :] = jnp.sum(gin, 0, keepdims=True)
    vec_m = [net.send(r.vec_g, r.vg_p.at[m - 1], net.plane(m)) for m in (1, 2, 3)]
    r.input_grad[...] = (r.grad_resid[...] + norm_grad(gin, normed, inverse, gain(0))).astype(BF)
    end_z(fc_b, r.fc_m, r.fc_z, r.fc_f)
    hand_out(0, r.fc_f, r.fc_o)
    total = r.vec_g[...]
    for m in range(3):
        vec_m[m].wait_recv()
        total = total + r.vg_p[m]
    r.vg_1[...] = total
    vec_l = [net.send(r.vg_1, r.vg_z.at[d - 1], net.line(d)) for d in range(1, nz)]
    total = r.og_3[rows_at(48 * z, 48), :].astype(F32)
    for d in range(nz - 1):
        og_z[d].wait_recv()
        total = total + r.og_z[d].astype(F32)
    r.out_o[:, half_cols(x)] = total.astype(BF)
    og_last = net.send(r.out_o.at[:, half_cols(x)], r.out_o.at[:, half_cols(x)], net.other_x())
    total = r.vg_1[...]
    for d in range(nz - 1):
        vec_l[d].wait_recv()
        total = total + r.vg_z[d]
    r.vg_2[...] = total
    vec_last = net.send(r.vg_2, r.vg_x, net.other_x())
    end_z(qkv_b, r.qkv_m, r.qkv_z, r.qkv_f)
    hand_out(4, r.qkv_f, r.qkv_o)
    vec_last.wait_recv()
    r.vec_o[...] = r.vg_2[...] + r.vg_x[...]
    proj_c.wait_recv()
    og_last.wait_recv()
    await_native(0, r.fc_f, r.fc_o)
    await_native(4, r.qkv_f, r.qkv_o)

    for here, copy in finals:
        @pl.when(jnp.logical_not(here))
        def _():
            copy.wait_send()
    for step in range(nz - 1):
        for way in range(2):
            @pl.when(kv_sends(way, step))
            def _():
                kv_copy(way, step).wait_send()
    for step in range(1, nz):
        for way in range(2):
            @pl.when(z - step >= 0 if way == 0 else z + step < nz)
            def _():
                chain_copy(way, step).wait_send()
    net.finish()


def block_call(nz, **operands):
    def vm(*shape, kind=BF):
        return pltpu.VMEM(shape, kind)

    outs = dict(
        output=((128, 768), BF), input_grad=((128, 768), BF), qkv_o=((4, 48, 576), BF),
        fc_o=((4, 48, 768), BF), proj_o=((192, 768), BF), out_o=((48, 768), BF), vec_o=((16, 768), F32),
    )
    f = lambda *shape: vm(*shape, kind=F32)
    keys = 512 * nz
    scratch = dict(
        w_qkv=vm(768, 576), w_fc=vm(768, 768), w_proj=vm(768, 768), w_out=vm(768, 768), w_outp=vm(1024, 768),
        vec_land_z=vm(nz - 1, 16, 768), vec_u=vm(16, 768), vec_land_p=vm(3, 16, 768), vec=f(16, 768),
        x_all=vm(512, 768), cot_all=vm(512, 768), ln_all=vm(512, 768), lm_all=vm(512, 768),
        qm=vm(3, 512, 128), kv_all=vm(nz, 512, 384), s_buf=f(512, 512), pt=vm(nz * 3, 512, 512),
        m_run=f(3, 1, 512), l_run=f(3, 1, 512), l_inv=f(3, 1, 512), m_at=f(nz * 3, 1, 512), o_t=f(3, 128, 512),
        att_t=f(2, 128, 512), att=vm(512, 256), merged=vm(4, 128, 256),
        resid=f(128, 768), normed_mid=f(128, 768), inverse_mid=f(128, 1), gact=f(512, 768),
        act=vm(512, 768), grad_pre=vm(512, 768), fcb=f(1, 768), vec_g=f(16, 768),
        gm_part=vm(4, 128, 768), gm_c=vm(2, 128, 768), gm_mid=vm(128, 768), gm_y=vm(128, 768),
        br_part=vm(4, 128, 768), br_c=vm(2, 128, 768), br_mid=vm(128, 768), br_y=vm(128, 768),
        gi_part=vm(4, 128, 768), gi_c=vm(2, 128, 768), gi_mid=vm(128, 768), gi_y=vm(128, 768),
        grad_resid=f(128, 768), gb=vm(128, 768), gmer=vm(4, 128, 256), ga=vm(512, 256), gam=vm(3, 512, 128),
        delta=f(3, 1, 512), ds=vm(3, 512, 512), dq_t=f(3, 128, 512), dkv=f(512, 384),
        chain=vm(2 * (nz - 1), 512, 384), chain_land=vm(2 * (nz - 1), 512, 384), gqkv=vm(512, 576),
        qkv_g=vm(768, 576), fc_g=vm(768, 768), proj_g=vm(768, 768), out_g=vm(2, 2, 192, 768),
        qkv_x=vm(nz, 96, 576), fc_x=vm(nz, 96, 768), proj_x=vm(nz, 96, 768),
        qkv_m=vm(nz, 96, 576), fc_m=vm(nz, 96, 768), proj_m=vm(nz, 96, 768),
        qkv_z=vm(nz - 1, 96, 576), fc_z=vm(nz - 1, 96, 768), proj_z=vm(nz - 1, 96, 768),
        qkv_f=vm(96, 576), fc_f=vm(96, 768), proj_f=vm(96, 768),
        og_c=vm(2, 192, 768), og_1=vm(2, 192, 768), og_y=vm(192, 768), og_2=vm(192, 768),
        og_x=vm(192, 384), og_3=vm(192, 384), og_z=vm(nz - 1, 48, 384),
        vg_p=f(3, 16, 768), vg_1=f(16, 768), vg_z=f(nz - 1, 16, 768), vg_2=f(16, 768), vg_x=f(16, 768),
        send_sem=pltpu.SemaphoreType.DMA((112,)), recv_sem=pltpu.SemaphoreType.DMA((112,)),
        local_sem=pltpu.SemaphoreType.DMA((6,)),
        kv_send=pltpu.SemaphoreType.DMA((2 * nz,)), kv_recv=pltpu.SemaphoreType.DMA((2 * nz,)),
        ch_send=pltpu.SemaphoreType.DMA((2 * nz,)), ch_recv=pltpu.SemaphoreType.DMA((2 * nz,)),
        f_send=pltpu.SemaphoreType.DMA((8,)), f_recv=pltpu.SemaphoreType.DMA((8,)),
    )
    names = [*operands, *outs, *scratch]

    def kernel(*refs):
        block_kernel(nz, types.SimpleNamespace(**dict(zip(names, refs, strict=True))))

    got = pl.pallas_call(
        kernel,
        out_shape=tuple(jax.ShapeDtypeStruct(*s) for s in outs.values()),
        in_specs=[VSPEC] * len(operands),
        out_specs=(VSPEC,) * len(outs),
        scratch_shapes=list(scratch.values()),
        compiler_params=pltpu.CompilerParams(
            collective_id=0, has_side_effects=True, vmem_limit_bytes=60 * 2**20
        ),
        name="transformer_block",
    )(*operands.values())
    return dict(zip(outs, got, strict=True))


def arrange_qkv(w):
    rows = w.shape[0]
    parts = w.reshape(rows, 3, 4, 3, 64)
    order = ((0, 0), (0, 1), (1, 0), (1, 1), (2, 0), (2, 1), (1, 2), (2, 2), (0, 2))
    return jnp.stack([parts[:, t, :, h] for t, h in order], 2).transpose(1, 0, 2, 3).reshape(4, rows, 576)


def restore_qkv(g):
    rows = g.shape[1]
    parts = g.reshape(4, rows, 9, 64)
    q = jnp.stack([parts[:, :, i] for i in (0, 1, 8)], 2)
    k = jnp.stack([parts[:, :, i] for i in (2, 3, 6)], 2)
    v = jnp.stack([parts[:, :, i] for i in (4, 5, 7)], 2)
    return jnp.stack([q, k, v], 0).transpose(2, 0, 1, 3, 4).reshape(rows, 2304)


def device_fast(nz, inputs, stretch_order, norm_gains, biases, mid_shift, value_bias, qkv_weight, out_weight, fc_weight, fc_bias, proj_weight, cotangent):
    z, u = lax.axis_index("blk"), lax.axis_index("uly")
    place = (4 * z + u) * 48
    pack = jnp.concatenate([norm_gains, biases, mid_shift[None], value_bias[None]], 0)
    vec8 = lax.dynamic_update_slice(jnp.zeros((8, 768), BF), pack, (0, place))
    fcb = lax.dynamic_update_slice(jnp.zeros((1, 768), BF), fc_bias[None], (0, 192 * z))
    wide = lax.dynamic_update_slice(jnp.zeros((2, 192), BF), jnp.stack([biases[1], value_bias]), (0, 48 * u))
    zero = jnp.zeros((64,), BF)
    q, v = wide[0].reshape(3, 64), wide[1].reshape(3, 64)
    local = jnp.concatenate([q[0], q[1], zero, zero, v[0], v[1], zero, v[2], q[2], jnp.zeros((192,), BF)])[None]
    four = lax.dynamic_update_slice(jnp.zeros((4, 768), BF), local, (z, 0))
    vec_pre = jnp.concatenate([vec8, fcb, four, jnp.zeros((3, 768), BF)], 0)
    pos = (stretch_order[0][:, None] * 64 + jnp.arange(64, dtype=jnp.int32)[None]).reshape(-1)
    got = block_call(
        nz,
        x_own=inputs[0],
        cot_own=cotangent[0],
        qkv_pre=arrange_qkv(qkv_weight),
        fc_pre=fc_weight.reshape(48, nz, 4, 192).transpose(2, 0, 1, 3).reshape(4, 48, 768),
        out_s=out_weight,
        proj_s=proj_weight,
        vec_pre=vec_pre,
        pos_row=pos[None],
        pos_col=pos[:, None],
    )
    vec_o = got["vec_o"]
    mine = lax.dynamic_slice(vec_o, (0, place), (6, 48))
    qs = lax.dynamic_slice(vec_o, (6 + z, 0), (1, 576))[0].reshape(9, 64)
    qb = lax.dynamic_slice(jnp.concatenate([qs[0], qs[1], qs[8]]), (48 * u,), (48,))
    vb = lax.dynamic_slice(jnp.concatenate([qs[4], qs[5], qs[7]]), (48 * u,), (48,))
    fb = lax.dynamic_slice(vec_o, (10 + u, 192 * z), (1, 192))[0]
    fc_g = got["fc_o"].reshape(4, 48, nz, 192).transpose(1, 2, 0, 3).reshape(48, 3072)
    return (
        got["output"][None],
        got["input_grad"][None],
        mine[0:2],
        jnp.stack([mine[2], qb, mine[3], mine[4]]),
        mine[5],
        vb,
        restore_qkv(got["qkv_o"]).astype(F32),
        got["out_o"].astype(F32),
        fc_g.astype(F32),
        fb,
        got["proj_o"].astype(F32),
    )


def solution(mesh):
    placed = (
        P("dp", ("blk", "uly"), None),
        P("dp", None),
        P(None, ("blk", "uly")),
        P(None, ("blk", "uly")),
        P(("blk", "uly")),
        P(("blk", "uly")),
        P(("blk", "uly"), None),
        P(("blk", "uly"), None),
        P(("blk", "uly"), None),
        P(("blk", "uly")),
        P(("blk", "uly"), None),
        P("dp", ("blk", "uly"), None),
    )
    sizes = dict(mesh.shape)
    nz = sizes["blk"]
    fast = sizes["uly"] == 4 and sizes["dp"] == 2 and 768 % (nz * 4 * 16) == 0
    chosen = functools.partial(device_fast, nz) if fast else per_device
    return jax.shard_map(
        chosen,
        mesh=mesh,
        in_specs=placed,
        out_specs=(
            P("dp", ("blk", "uly"), None),
            P("dp", ("blk", "uly"), None),
            P(None, ("blk", "uly")),
            P(None, ("blk", "uly")),
            P(("blk", "uly")),
            P(("blk", "uly")),
            P(("blk", "uly"), None),
            P(("blk", "uly"), None),
            P(("blk", "uly"), None),
            P(("blk", "uly")),
            P(("blk", "uly"), None),
        ),
        check_vma=False,
    )
```

```python
import functools
import math
import types

import jax
import jax.numpy as jnp
from jax import lax
from jax.experimental import pallas as pl
from jax.experimental.pallas import tpu as pltpu
from jax.sharding import PartitionSpec as P

HEADS = 12


masked_score = -1e30


def layer_norm(values, gain, shift):
    center = values - jnp.mean(values, -1, keepdims=True)
    inverse = lax.rsqrt(jnp.mean(center * center, -1, keepdims=True) + 1e-05)
    normed = center * inverse
    return (normed * gain + shift, normed, inverse)


def norm_back(grad_out, normed, inverse, gain):
    scaled = grad_out * gain
    mean_plain = jnp.mean(scaled, -1, keepdims=True)
    mean_mixed = jnp.mean(scaled * normed, -1, keepdims=True)
    return inverse * (scaled - mean_plain - normed * mean_mixed)


def sweep(step_fn, carried, parts):
    row_count = parts[0].shape[1]
    sweep_rows = math.gcd(row_count, 1024)

    def turn(inner, turn_number):
        offset = turn_number * sweep_rows
        blocks = tuple((lax.dynamic_slice_in_dim(part, offset, sweep_rows, 1) for part in parts))
        return (step_fn(inner, blocks, offset), None)

    result, _ = lax.scan(turn, carried, jnp.arange(row_count // sweep_rows, dtype=jnp.int32))
    return result


def per_device(
    inputs,
    stretch_order,
    norm_gains,
    biases,
    mid_shift,
    value_bias,
    qkv_weight,
    out_weight,
    fc_weight,
    fc_bias,
    proj_weight,
    cotangent,
):
    fp32 = jnp.float32
    bf16 = jnp.bfloat16
    gain_rows, shifts, mid_gathered, value_shift, w_qkv, w_out, w_fc, b_fc, w_proj = (
        lax.all_gather(norm_gains, ("blk", "uly"), axis=1, tiled=True),
        lax.all_gather(biases, ("blk", "uly"), axis=1, tiled=True),
        lax.all_gather(mid_shift, ("blk", "uly"), axis=0, tiled=True),
        lax.all_gather(value_bias, ("blk", "uly"), axis=0, tiled=True),
        lax.all_gather(qkv_weight, ("blk", "uly"), axis=0, tiled=True),
        lax.all_gather(out_weight, ("blk", "uly"), axis=0, tiled=True),
        lax.all_gather(fc_weight, ("blk", "uly"), axis=0, tiled=True),
        lax.all_gather(fc_bias, ("blk", "uly"), axis=0, tiled=True),
        lax.all_gather(proj_weight, ("blk", "uly"), axis=0, tiled=True),
    )
    gain_rows = gain_rows.astype(fp32)
    shifts = shifts.astype(fp32)
    mid_gathered = mid_gathered.astype(fp32)
    seq_count, row_len, width = inputs.shape
    uly_count = lax.axis_size("uly")
    local_heads = HEADS // uly_count
    head_dim = width // HEADS
    head_span = local_heads * head_dim
    block_rows = uly_count * row_len
    half_rows = row_len // 2
    seq_len = stretch_order.shape[1] * half_rows
    score_scale = head_dim ** (-0.5)
    tokens = inputs.astype(fp32).reshape(seq_count * row_len, width)
    ln_in, normed_in, inverse_in = layer_norm(tokens, gain_rows[0], shifts[0])
    ln_in = ln_in.astype(bf16)
    qkv_shift = jnp.concatenate([shifts[1], jnp.zeros((width,), fp32), value_shift.astype(fp32)])
    qkv = (jnp.dot(ln_in, w_qkv, preferred_element_type=fp32) + qkv_shift).astype(bf16)
    head_data = lax.all_to_all(
        qkv.reshape(seq_count, row_len, 3, uly_count, head_span),
        "uly",
        split_axis=3,
        concat_axis=1,
        tiled=True,
    )
    queries = head_data[:, :, 0, 0].reshape(seq_count, block_rows, local_heads, head_dim)
    key_rows = head_data[:, :, 1, 0]
    value_rows = head_data[:, :, 2, 0]
    positions = (
        stretch_order[:, :, None] * half_rows
        + jnp.arange(half_rows, dtype=jnp.int32)[None, None, :]
    ).reshape(seq_count, seq_len)
    query_pos = lax.dynamic_slice_in_dim(
        positions, lax.axis_index("blk") * block_rows, block_rows, 1
    )

    def score_block(key_part, key_start):
        part_rows = key_part.shape[1]
        key_pos = lax.dynamic_slice_in_dim(positions, key_start, part_rows, 1)
        scores = (
            jnp.einsum(
                "sqhd,skhd->shqk",
                queries,
                key_part.reshape(seq_count, part_rows, local_heads, head_dim),
                preferred_element_type=fp32,
            )
            * score_scale
        )
        causal = query_pos[:, None, :, None] >= key_pos[:, None, None, :]
        return (scores, causal)

    def stats_step(carried, blocks, key_start):
        row_max, row_total = carried
        scores, causal = score_block(blocks[0], key_start)
        new_max = jnp.maximum(row_max, jnp.max(jnp.where(causal, scores, masked_score), -1))
        row_total = row_total * jnp.exp(row_max - new_max) + jnp.sum(
            jnp.where(causal, jnp.exp(scores - new_max[..., None]), 0.0), -1
        )
        return (new_max, row_total)

    def softmax_of(scores, causal, row_max, row_total):
        return jnp.where(causal, jnp.exp(scores - row_max[..., None]) / row_total[..., None], 0.0)

    def make_output_step(row_max, row_total):

        def output_step(acc_out, blocks, key_start):
            scores, causal = score_block(blocks[0], key_start)
            attn_probs = softmax_of(scores, causal, row_max, row_total).astype(bf16)
            part_rows = blocks[1].shape[1]
            value_part = blocks[1].reshape(seq_count, part_rows, local_heads, head_dim)
            return acc_out + jnp.einsum(
                "shqk,skhd->sqhd", attn_probs, value_part, preferred_element_type=fp32
            )

        return output_step

    stats_init = (
        jnp.full((seq_count, local_heads, block_rows), masked_score, fp32),
        jnp.zeros((seq_count, local_heads, block_rows), fp32),
    )
    empty_out = jnp.zeros((seq_count, block_rows, local_heads, head_dim), fp32)
    all_keys, all_values = (
        lax.all_gather(key_rows, "blk", axis=1, tiled=True),
        lax.all_gather(value_rows, "blk", axis=1, tiled=True),
    )
    row_max, row_total = sweep(stats_step, stats_init, (all_keys,))
    attended = sweep(make_output_step(row_max, row_total), empty_out, (all_keys, all_values))
    attended_low = attended.astype(bf16).reshape(seq_count, block_rows, 1, head_span)
    merged = lax.all_to_all(attended_low, "uly", split_axis=1, concat_axis=2, tiled=True).reshape(
        seq_count * row_len, width
    )
    resid = tokens + (jnp.dot(merged, w_out, preferred_element_type=fp32) + shifts[2])
    ln_mid, normed_mid, inverse_mid = layer_norm(resid, gain_rows[1], mid_gathered)
    ln_mid = ln_mid.astype(bf16)
    pre_act = jnp.dot(ln_mid, w_fc, preferred_element_type=fp32) + b_fc.astype(fp32)

    def gelu_piece(pre_values):
        return jax.nn.gelu(pre_values, approximate=True)

    act, gelu_back = jax.vjp(gelu_piece, pre_act)
    act = act.astype(bf16)
    result = resid + (jnp.dot(act, w_proj, preferred_element_type=fp32) + shifts[3])
    grad_low = cotangent.reshape(seq_count * row_len, width)
    grad_out = grad_low.astype(fp32)
    proj_grad = jnp.einsum("ta,tb->ab", act, grad_low, preferred_element_type=fp32)
    proj_shift_grad = jnp.sum(grad_out, 0)
    grad_act = jnp.einsum("tb,ab->ta", grad_low, w_proj, preferred_element_type=fp32)
    grad_pre = gelu_back(grad_act)[0].astype(bf16)
    fc_grad = jnp.einsum("ta,tb->ab", ln_mid, grad_pre, preferred_element_type=fp32)
    fc_shift_grad = jnp.sum(grad_pre.astype(fp32), 0)
    grad_mid = jnp.einsum("tb,ab->ta", grad_pre, w_fc, preferred_element_type=fp32)
    gain_mid_grad = jnp.sum(grad_mid * normed_mid, 0)
    shift_mid_grad = jnp.sum(grad_mid, 0)
    grad_resid = grad_out + norm_back(grad_mid, normed_mid, inverse_mid, gain_rows[1])
    grad_branch = grad_resid.astype(bf16)
    out_grad = jnp.einsum("ta,tb->ab", merged, grad_branch, preferred_element_type=fp32)
    out_shift_grad = jnp.sum(grad_branch.astype(fp32), 0)
    grad_merged = jnp.einsum("tb,ab->ta", grad_branch, w_out, preferred_element_type=fp32).astype(
        bf16
    )
    grad_att = lax.all_to_all(
        grad_merged.reshape(seq_count, row_len, uly_count, head_span),
        "uly",
        split_axis=2,
        concat_axis=1,
        tiled=True,
    )
    grad_att = grad_att.reshape(seq_count, block_rows, local_heads, head_dim)
    delta = jnp.transpose(jnp.sum(grad_att.astype(fp32) * attended, -1), (0, 2, 1))
    back_keys, back_values = (all_keys, all_values)
    sweep_rows = math.gcd(seq_len, 1024)

    def query_terms(offset):
        key_part = lax.dynamic_slice_in_dim(back_keys, offset, sweep_rows, 1)
        value_part = lax.dynamic_slice_in_dim(back_values, offset, sweep_rows, 1)
        scores, causal = score_block(key_part, offset)
        attn_probs = softmax_of(scores, causal, row_max, row_total)
        key_heads = key_part.reshape(seq_count, sweep_rows, local_heads, head_dim)
        value_heads = value_part.reshape(seq_count, sweep_rows, local_heads, head_dim)
        grad_probs = jnp.einsum(
            "sqhd,skhd->shqk", grad_att, value_heads, preferred_element_type=fp32
        )
        grad_scores = (attn_probs * (grad_probs - delta[..., None])).astype(bf16)
        query_term = (
            jnp.einsum("shqk,skhd->sqhd", grad_scores, key_heads, preferred_element_type=fp32)
            * score_scale
        )
        return (query_term, grad_scores, attn_probs.astype(bf16))

    query_init = jnp.zeros((seq_count, block_rows, local_heads, head_dim), fp32)

    def back_step(carried, turn_number):
        grad_query, kv_buffer = carried
        offset = turn_number * sweep_rows
        query_term, grad_scores, probs_low = query_terms(offset)
        grad_key = (
            jnp.einsum("shqk,sqhd->skhd", grad_scores, queries, preferred_element_type=fp32)
            * score_scale
        )
        grad_value = jnp.einsum("shqk,sqhd->skhd", probs_low, grad_att, preferred_element_type=fp32)
        kv_pair = jnp.stack(
            [
                grad_key.reshape(seq_count, sweep_rows, head_span),
                grad_value.reshape(seq_count, sweep_rows, head_span),
            ],
            2,
        )
        kv_buffer = lax.dynamic_update_slice_in_dim(kv_buffer, kv_pair, offset, 1)
        return ((grad_query + query_term, kv_buffer), None)

    back_init = (query_init, jnp.zeros((seq_count, seq_len, 2, head_span), fp32))
    back_done, _ = lax.scan(
        back_step, back_init, jnp.arange(seq_len // sweep_rows, dtype=jnp.int32)
    )
    grad_query, kv_buffer = back_done
    kv_summed = lax.psum_scatter(
        kv_buffer.astype(jnp.bfloat16), "blk", scatter_dimension=1, tiled=True
    ).astype(jnp.float32)
    grad_heads = jnp.concatenate(
        [
            grad_query.reshape(seq_count, block_rows, 1, head_span).astype(bf16),
            kv_summed.astype(bf16),
        ],
        2,
    )
    grad_qkv = lax.all_to_all(
        grad_heads.reshape(seq_count, block_rows, 3, 1, head_span),
        "uly",
        split_axis=1,
        concat_axis=3,
        tiled=True,
    )
    grad_qkv = grad_qkv.reshape(seq_count * row_len, 3 * width)
    qkv_grad = jnp.einsum("ta,tb->ab", ln_in, grad_qkv, preferred_element_type=fp32)
    column_sums = jnp.sum(grad_qkv.astype(fp32), 0)
    grad_in_norm = jnp.einsum("tb,ab->ta", grad_qkv, w_qkv, preferred_element_type=fp32)
    gain_in_grad = jnp.sum(grad_in_norm * normed_in, 0)
    shift_in_grad = jnp.sum(grad_in_norm, 0)
    grad_input = grad_resid + norm_back(grad_in_norm, normed_in, inverse_in, gain_rows[0])
    gains_grad = jnp.stack([gain_in_grad, gain_mid_grad])
    biases_grad = jnp.stack([shift_in_grad, column_sums[:width], out_shift_grad, proj_shift_grad])
    value_grad = column_sums[2 * width :]
    shard_grads = (
        lax.psum_scatter(gains_grad, ("blk", "uly"), scatter_dimension=1, tiled=True),
        lax.psum_scatter(biases_grad, ("blk", "uly"), scatter_dimension=1, tiled=True),
        lax.psum_scatter(shift_mid_grad, ("blk", "uly"), scatter_dimension=0, tiled=True),
        lax.psum_scatter(value_grad, ("blk", "uly"), scatter_dimension=0, tiled=True),
        lax.psum_scatter(qkv_grad, ("blk", "uly"), scatter_dimension=0, tiled=True),
        lax.psum_scatter(out_grad, ("blk", "uly"), scatter_dimension=0, tiled=True),
        lax.psum_scatter(fc_grad, ("blk", "uly"), scatter_dimension=0, tiled=True),
        lax.psum_scatter(fc_shift_grad, ("blk", "uly"), scatter_dimension=0, tiled=True),
        lax.psum_scatter(proj_grad, ("blk", "uly"), scatter_dimension=0, tiled=True),
    )
    shard_grads = (
        lax.psum(shard_grads[0].astype(jnp.bfloat16), "dp").astype(jnp.float32),
        lax.psum(shard_grads[1].astype(jnp.bfloat16), "dp").astype(jnp.float32),
        lax.psum(shard_grads[2].astype(jnp.bfloat16), "dp").astype(jnp.float32),
        lax.psum(shard_grads[3].astype(jnp.bfloat16), "dp").astype(jnp.float32),
        lax.psum(shard_grads[4].astype(jnp.bfloat16), "dp").astype(jnp.float32),
        lax.psum(shard_grads[5].astype(jnp.bfloat16), "dp").astype(jnp.float32),
        lax.psum(shard_grads[6].astype(jnp.bfloat16), "dp").astype(jnp.float32),
        lax.psum(shard_grads[7].astype(jnp.bfloat16), "dp").astype(jnp.float32),
        lax.psum(shard_grads[8].astype(jnp.bfloat16), "dp").astype(jnp.float32),
    )
    output = result.astype(bf16).reshape(seq_count, row_len, width)
    input_grad = grad_input.astype(bf16).reshape(seq_count, row_len, width)
    return (
        output,
        input_grad,
        shard_grads[0],
        shard_grads[1],
        shard_grads[2],
        shard_grads[3],
        shard_grads[4],
        shard_grads[5],
        shard_grads[6],
        shard_grads[7],
        shard_grads[8],
    )


MESH = pl.DeviceIdType.MESH
BF = jnp.bfloat16
F32 = jnp.float32
VSPEC = pl.BlockSpec(memory_space=pltpu.VMEM)
GELU_IN = math.sqrt(2.0 / math.pi)


class Net:
    def __init__(self, send_sem, recv_sem, nz):
        self.send_sem, self.recv_sem = send_sem, recv_sem
        self.count = 0
        self.sent = []
        self.nz = nz
        self.x = lax.axis_index("dp")
        self.z = lax.axis_index("blk")
        self.u = lax.axis_index("uly")

    def send(self, src, dst, dev):
        k = self.count
        self.count += 1
        copy = pltpu.make_async_remote_copy(
            src_ref=src,
            dst_ref=dst,
            send_sem=self.send_sem.at[k],
            recv_sem=self.recv_sem.at[k],
            device_id=dev,
            device_id_type=MESH,
        )
        copy.start()
        self.sent.append(copy)
        return copy

    def plane(self, m):
        return (self.x, self.z, self.u ^ m)

    def other_x(self):
        return (1 - self.x, self.z, self.u)

    def zplus(self, d):
        return lax.rem(self.z + d, self.nz)

    def line(self, d):
        return (self.x, self.zplus(d), self.u)

    def hail(self):
        barrier = pltpu.get_barrier_semaphore()
        near = [self.plane(m) for m in (1, 2, 3)] + [self.other_x()]
        near += [self.line(d) for d in range(1, self.nz)]
        near += [(1 - self.x, self.z, self.u ^ m) for m in (1, 2, 3)]
        for dev in near:
            pl.semaphore_signal(barrier, inc=1, device_id=dev, device_id_type=MESH)
        self.met = len(near)

    def meet(self):
        pl.semaphore_wait(pltpu.get_barrier_semaphore(), self.met)

    def finish(self):
        for copy in self.sent:
            copy.wait_send()


class Line:
    def __init__(self, net, send_sem, recv_sem, base):
        self.net, self.send_sem, self.recv_sem, self.base = net, send_sem, recv_sem, base
        self.z = net.z
        self.inner = jnp.logical_and(net.z >= 1, net.z <= net.nz - 2)
        self.far = net.nz - 1 - net.z

    def copy(self, src, dst, k, target, recv=None):
        target = jnp.clip(target, 0, self.net.nz - 1)
        return pltpu.make_async_remote_copy(
            src_ref=src,
            dst_ref=dst,
            send_sem=self.send_sem.at[self.base + k],
            recv_sem=self.recv_sem.at[self.base + (k if recv is None else recv)],
            device_id=(self.net.x, target, self.net.u),
            device_id_type=MESH,
        )

    def target(self, d):
        return lax.rem(self.z + d, self.net.nz)

    def source(self, d):
        return lax.rem(self.z - d + self.net.nz, self.net.nz)


class Spread(Line):
    def __init__(self, net, send_sem, recv_sem, base, block):
        super().__init__(net, send_sem, recv_sem, base)
        self.block = block

    def direct(self, d):
        return self.copy(self.block(self.z), self.block(self.z), d, self.target(d))

    def start(self):
        for d in (2, 1, 3):
            if d == 2:
                self.direct(d).start()
            else:
                @pl.when(jnp.logical_or(self.inner, self.target(d) != self.far))
                def _():
                    self.direct(d).start()

    def relay_copy(self):
        block = self.block(self.source(2))
        target = jnp.where(self.z == 2, 3, 0)
        return self.copy(block, block, 4, target, jnp.where(self.z == 2, 3, 1))

    def across(self, d):
        block = self.block(self.source(d))
        return pltpu.make_async_remote_copy(
            src_ref=block, dst_ref=block, send_sem=self.send_sem.at[self.base + 4 + d],
            recv_sem=self.recv_sem.at[self.base + 4 + d], device_id=self.net.other_x(), device_id_type=MESH)

    def arrive(self, d):
        block = self.block(self.source(d))
        self.copy(block, block, d, self.z).wait_recv()

    def relay(self):
        self.arrive(2)

        @pl.when(self.inner)
        def _():
            self.relay_copy().start()

        self.across(2).start()

    def rest(self):
        first = jnp.where(self.z == 0, 3, 1)
        for d in (first, 4 - first):
            self.arrive(d)
            self.across(d).start()

    def finish_recv(self):
        for d in (2, 1, 3):
            self.across(d).wait_recv()

    def finish(self):
        self.direct(2).wait_send()
        for d in (1, 3):
            @pl.when(jnp.logical_or(self.inner, self.target(d) != self.far))
            def _():
                self.direct(d).wait_send()
        for d in (1, 2, 3):
            self.across(d).wait_send()

        @pl.when(self.inner)
        def _():
            self.relay_copy().wait_send()


class Collect(Line):
    def __init__(self, net, send_sem, recv_sem, base, theirs, ours, land_x, mine, land_z, relay):
        super().__init__(net, send_sem, recv_sem, base)
        self.theirs, self.ours = theirs, ours
        self.land_x, self.mine, self.land_z, self.relay = land_x, mine, land_z, relay

    def order(self, i):
        pick = lambda table: table[i]
        z = self.z
        return jnp.where(z == 0, 3 - i, jnp.where(z == 3, i, jnp.where(z == 1, pick((0, 2, 3, 1)), pick((3, 1, 0, 2)))))

    def across(self, i):
        zz = self.order(i)
        return pltpu.make_async_remote_copy(
            src_ref=self.theirs(zz), dst_ref=self.land_x.at[zz], send_sem=self.send_sem.at[self.base + 5 + i],
            recv_sem=self.recv_sem.at[self.base + 5 + i], device_id=self.net.other_x(), device_id_type=MESH)

    def start(self):
        for i in range(4):
            self.across(i).start()

    def own(self, i):
        zz = self.order(i)
        self.across(i).wait_recv()
        self.mine[zz] = (self.ours(zz) + self.land_x[zz].astype(F32)).astype(BF)

    def direct(self, zz):
        d = lax.rem(zz - self.z + 4, 4)
        return self.copy(self.mine.at[zz], self.land_z.at[d - 1], d, zz)

    def to_neighbour(self):
        return self.copy(self.mine.at[self.far], self.relay, 4, jnp.where(self.z == 0, 1, 2))

    def part(self, i):
        self.own(i)
        if i == 0:
            @pl.when(self.inner)
            def _():
                self.direct(self.order(0)).start()

            @pl.when(jnp.logical_not(self.inner))
            def _():
                self.to_neighbour().start()
        elif i == 1:
            self.direct(self.order(1)).start()
        elif i == 2:
            @pl.when(jnp.logical_not(self.inner))
            def _():
                self.direct(self.order(2)).start()

    def first(self):
        for i in range(4):
            self.part(i)

    def second(self):
        @pl.when(self.inner)
        def _():
            zz = self.order(2)
            self.copy(self.relay, self.relay, 4, self.z).wait_recv()
            self.mine[zz] = (self.mine[zz].astype(F32) + self.relay[...].astype(F32)).astype(BF)
            self.direct(zz).start()

    def total(self, final):
        skip = jnp.where(self.z == 0, 1, 3)
        final[...] = self.mine[self.z].astype(F32)
        for d in (1, 2, 3):
            @pl.when(jnp.logical_or(self.inner, skip != d))
            def _():
                self.copy(self.land_z.at[d - 1], self.land_z.at[d - 1], d, self.z).wait_recv()
                final[...] += self.land_z[d - 1].astype(F32)

    def finish(self):
        for i in range(4):
            self.across(i).wait_send()

        @pl.when(self.inner)
        def _():
            for i in range(3):
                self.direct(self.order(i)).wait_send()

        @pl.when(jnp.logical_not(self.inner))
        def _():
            self.to_neighbour().wait_send()
            for i in (1, 2):
                self.direct(self.order(i)).wait_send()


def rows_at(start, count):
    return pl.ds(pl.multiple_of(start, 16), count)


def dot_nn(a, b):
    return jnp.dot(a, b, preferred_element_type=F32)


def dot_nt(a, b):
    return lax.dot_general(a, b, (((1,), (1,)), ((), ())), preferred_element_type=F32)


def dot_tn(a, b):
    return lax.dot_general(a, b, (((0,), (0,)), ((), ())), preferred_element_type=F32)


def loop(count, body):
    def step(i, carry):
        body(i)
        return carry

    lax.fori_loop(0, count, step, 0)


def block_kernel(nz, refs):
    r = refs
    net = Net(r.send_sem, r.recv_sem, nz)
    x, z, u = net.x, net.z, net.u
    y, c = u // 2, lax.rem(u, 2)
    own48 = (4 * z + u) * 48
    tile = lambda t: rows_at(128 * t, 128)
    half_cols = lambda which: pl.ds(pl.multiple_of(384 * which, 128), 384)
    lane = lambda shape: lax.broadcasted_iota(jnp.int32, shape, 1)

    x_own, cot_own = r.x_all.at[tile(u)], r.cot_all.at[tile(u)]
    local = [
        pltpu.make_async_copy(r.qkv_in, r.qkv_raw, r.local_sem.at[0]),
        pltpu.make_async_copy(r.fc_in, r.fc_raw, r.local_sem.at[1]),
        pltpu.make_async_copy(r.x_in, x_own, r.local_sem.at[2]),
        pltpu.make_async_copy(r.out_in, r.w_out.at[rows_at(own48, 48)], r.local_sem.at[3]),
        pltpu.make_async_copy(r.proj_in, r.w_proj.at[rows_at(192 * z, 192)], r.local_sem.at[4]),
        pltpu.make_async_copy(r.cot_in, cot_own, r.local_sem.at[5]),
    ]
    for copy in local:
        copy.start()
    net.hail()
    local[0].wait()
    for g in range(4):
        for t in range(3):
            r.qkv_pre[g, :, 128 * t:128 * t + 128] = r.qkv_raw[:, 768 * t + 192 * g:768 * t + 192 * g + 128]
        for at, t in ((384, 1), (448, 2), (512, 0)):
            r.qkv_pre[g, :, at:at + 64] = r.qkv_raw[:, 768 * t + 192 * g + 128:768 * t + 192 * g + 192]
    r.w_qkv[rows_at(own48, 48), :] = r.qkv_pre[u]
    vp = r.vec_f32
    vp[...] = jnp.zeros((16, 768), F32)
    vp[0:2, 0:48] = r.gains_in[...].astype(F32)
    vp[2:6, 0:48] = r.biases_in[...].astype(F32)
    vp[6:7, 0:48] = r.mid_in[...].astype(F32)
    vp[7:8, 0:48] = r.vb_in[...].astype(F32)
    bias = r.bias_f32
    bias[...] = jnp.zeros((8, 256), F32)
    bias[0:1, 0:48] = r.biases_in[1:2, :].astype(F32)
    bias[1:2, 0:48] = r.vb_in[...].astype(F32)
    bias[...] = pltpu.roll(bias[...], 48 * u, 1)
    vp[0:8, :] = pltpu.roll(vp[0:8, :], 48 * (4 * z + u), 1)
    vp[8:9, 0:192] = r.fcb_in[...].astype(F32)
    vp[9:10, 0:128] = bias[0:1, 0:128]
    vp[9:10, 256:384] = bias[1:2, 0:128]
    vp[9:10, 448:512] = bias[1:2, 128:192]
    vp[9:10, 512:576] = bias[0:1, 128:192]
    high = vp[8:16, :]
    row8 = lax.broadcasted_iota(jnp.int32, high.shape, 0)
    fcb_row = pltpu.roll(jnp.where(row8 == 0, high, 0.0), 192 * z, 1)
    bias_row = jnp.sum(jnp.where(row8 == 1, high, 0.0), 0, keepdims=True)
    vp[8:16, :] = fcb_row + jnp.where(row8 == 1 + z, bias_row, 0.0)
    r.vec_pre[...] = vp[...].astype(BF)
    net.meet()

    def plane_gather_start(own, full):
        return [net.send(own, full.at[tile(u)], net.plane(m)) for m in (2, 1)]

    def plane_gather_forward(sent, full):
        sent[0].wait_recv()
        sent.append(net.send(full.at[tile(u ^ 2)], full.at[tile(u ^ 2)], net.plane(1)))

    in_plane = lambda pre, full: [
        net.send(pre.at[u ^ m], full.at[rows_at(own48, 48)], net.plane(m)) for m in (1, 2, 3)
    ]
    block96 = lambda full: lambda j: full.at[rows_at(192 * j + 96 * x, 96)]
    spread = lambda base, block: Spread(net, r.sp_send, r.sp_recv, base, block)
    qkv_s = spread(0, block96(r.w_qkv))
    fc_s = spread(8, block96(r.w_fc))
    proj_s = spread(16, block96(r.w_proj))
    out_s = spread(24, lambda j: r.w_out.at[rows_at((4 * j + u) * 48, 48), half_cols(x)])
    qkv_p = in_plane(r.qkv_pre, r.w_qkv)
    vec_z = [net.send(r.vec_pre, r.vec_land_z.at[d - 1], net.line(d)) for d in range(1, nz)]
    for copy in local[1:]:
        copy.wait()
    out_s.start()
    for g in range(4):
        for zz in range(nz):
            r.fc_pre[g, :, 192 * zz:192 * zz + 192] = r.fc_raw[:, 768 * zz + 192 * g:768 * zz + 192 * g + 192]
    r.w_fc[rows_at(own48, 48), :] = r.fc_pre[u]
    inner64 = lax.broadcasted_iota(jnp.int32, (64, 1), 0)
    inner64_row = lax.broadcasted_iota(jnp.int32, (1, 64), 1)
    for i in range(8 * nz):
        first = r.order_in[0, i] * 64
        r.pos_col[64 * i:64 * i + 64, :] = first + inner64
        r.pos_row[:, 64 * i:64 * i + 64] = first + inner64_row
    for copy in qkv_p:
        copy.wait_recv()
    qkv_s.start()
    x_g = plane_gather_start(x_own, r.x_all)
    total = r.vec_pre[...]
    for d in range(nz - 1):
        vec_z[d].wait_recv()
        total = total + r.vec_land_z[d]
    r.vec_u[...] = total
    vec_p = [net.send(r.vec_u, r.vec_land_p.at[m - 1], net.plane(m)) for m in (1, 2, 3)]
    plane_gather_forward(x_g, r.x_all)
    fc_p = in_plane(r.fc_pre, r.w_fc)
    total = r.vec_u[...].astype(F32)
    row = lax.broadcasted_iota(jnp.int32, total.shape, 0)
    for m in range(3):
        vec_p[m].wait_recv()
        total = total + jnp.where(row == 8, 0.0, r.vec_land_p[m].astype(F32))
    r.vec[...] = total
    for copy in x_g[1:]:
        copy.wait_recv()
    gain = lambda i: r.vec[pl.ds(i, 1), :]

    def normalize(values):
        center = values - jnp.mean(values, -1, keepdims=True)
        inverse = lax.rsqrt(jnp.mean(center * center, -1, keepdims=True) + 1e-05)
        return center * inverse, inverse

    def ln_tile(t):
        normed, _ = normalize(r.x_all[tile(t), :].astype(F32))
        r.ln_all[tile(t), :] = (normed * gain(0) + gain(2)).astype(BF)

    loop(4, ln_tile)
    qkv_s.relay()
    qkv_s.rest()
    for copy in fc_p:
        copy.wait_recv()
    fc_s.start()
    cot_g = plane_gather_start(cot_own, r.cot_all)
    r.qm[2] = jnp.zeros((512, 128), BF)
    out_s.relay()
    out_s.rest()
    qkv_s.finish_recv()

    bias_u = jnp.sum(jnp.where(row == 9 + u, r.vec[...], 0.0), 0, keepdims=True)[:, 0:576]

    def qkv_tile(t):
        res = dot_nn(r.ln_all[tile(t), :], r.w_qkv[...]) + bias_u
        res = res.astype(BF)
        q01 = res[:, 0:128].astype(F32) * 0.125
        low = lane(q01.shape) < 64
        r.qm[0, tile(t), :] = jnp.where(low, q01, 0.0).astype(BF)
        r.qm[1, tile(t), :] = jnp.where(low, 0.0, q01).astype(BF)
        r.qm[2, tile(t), 0:64] = (res[:, 512:576].astype(F32) * 0.125).astype(BF)
        r.kv_all[z, tile(t), :] = res[:, 128:512]

    loop(4, qkv_tile)

    def kv_copy(way, step):
        block = z - step if way == 0 else z + step
        target = z + 1 if way == 0 else z - 1
        block, target = jnp.clip(block, 0, nz - 1), jnp.clip(target, 0, nz - 1)
        return pltpu.make_async_remote_copy(
            src_ref=r.kv_all.at[block], dst_ref=r.kv_all.at[block],
            send_sem=r.kv_send.at[way * nz + step], recv_sem=r.kv_recv.at[way * nz + step],
            device_id=(x, target, u), device_id_type=MESH)

    def kv_sends(way, step):
        if way == 0:
            return jnp.logical_and(z - step >= 0, z + 1 < nz)
        return jnp.logical_and(z + step < nz, z >= 1)

    def kv_start(step):
        for way in range(2):
            @pl.when(kv_sends(way, step))
            def _():
                kv_copy(way, step).start()

    def attend(j):
        qp = r.pos_row[:, pl.ds(pl.multiple_of(512 * z, 128), 512)]
        for h in range(3):
            kc = 0 if h < 2 else 256
            vc = 128 if h < 2 else 256
            q = r.qm[h]

            def score(kt, top):
                s = dot_nt(r.kv_all[j, rows_at(128 * kt, 128), kc:kc + 128], q)
                kp = r.pos_col[pl.ds(pl.multiple_of(512 * j + 128 * kt, 128), 128), :]
                s = jnp.where(kp <= qp, s, -1e30)
                r.s_buf[rows_at(128 * kt, 128), :] = s
                return jnp.maximum(top, jnp.max(s, 0, keepdims=True))

            old = r.m_run[h]
            top = lax.fori_loop(0, 4, score, old)
            shrink = jnp.exp(old - top)

            def weigh(kt, got):
                p = jnp.exp(r.s_buf[rows_at(128 * kt, 128), :] - top)
                r.pt[j * 3 + h, rows_at(128 * kt, 128), :] = p.astype(BF)
                return got + jnp.sum(p, 0, keepdims=True)

            got = lax.fori_loop(0, 4, weigh, jnp.zeros((1, 512), F32))
            r.m_run[h] = top
            r.m_at[j * 3 + h] = top
            r.l_run[h] = r.l_run[h] * shrink + got
            r.o_t[h] = r.o_t[h] * shrink + dot_tn(r.kv_all[j, :, vc:vc + 128], r.pt[j * 3 + h])

    r.m_run[...] = jnp.full((3, 1, 512), -1e30, F32)
    r.l_run[...] = jnp.zeros((3, 1, 512), F32)
    r.o_t[...] = jnp.zeros((3, 128, 512), F32)
    kv_start(0)
    plane_gather_forward(cot_g, r.cot_all)
    attend(z)
    fc_s.relay()

    for step in range(1, nz):
        for way in range(2):
            @pl.when(z - step >= 0 if way == 0 else z + step < nz)
            def _():
                kv_copy(way, step - 1).wait_recv()

        if step < nz - 1:
            kv_start(step)
        if step == 1:
            fc_s.rest()
            out_s.finish_recv()
            out_rows = lambda zz, who: r.w_out.at[rows_at((4 * zz + who) * 48, 48)]
            out_y = [net.send(out_rows(zz, u), out_rows(zz, u), net.plane(2)) for zz in range(nz)]
            out_c = [net.send(out_rows(zz, u), out_rows(zz, u), net.plane(1)) for zz in range(nz)]
        if step == 2:
            for zz, copy in enumerate(out_y):
                copy.wait_recv()
                out_c.append(net.send(out_rows(zz, u ^ 2), out_rows(zz, u ^ 2), net.plane(1)))
        if step == nz - 1:
            proj_s.start()

        def either(way):
            j = jnp.where(way == 0, z - step, z + step)

            @pl.when(jnp.logical_and(j >= 0, j < nz))
            def _():
                attend(j)

        loop(2, either)

    rowi = lax.broadcasted_iota(jnp.int32, (128, 512), 0)
    r.l_inv[...] = 1.0 / r.l_run[...]
    r.att_t[0] = jnp.where(rowi < 64, r.o_t[0] * r.l_inv[0], r.o_t[1] * r.l_inv[1])
    r.att_t[1] = jnp.where(rowi < 64, 0.0, r.o_t[2] * r.l_inv[2])
    r.att[:, 0:128] = jnp.transpose(r.att_t[0]).astype(BF)
    r.att[:, 128:256] = jnp.transpose(r.att_t[1]).astype(BF)
    att_p = [net.send(r.att.at[tile(u ^ m)], r.merged.at[u], net.plane(m)) for m in (2, 3, 1)]
    r.merged[u] = r.att[tile(u), :]

    for copy in out_c:
        copy.wait_recv()
    for g in range(4):
        r.w_outp[256 * g:256 * g + 128, :] = r.w_out[192 * g:192 * g + 128, :]
        r.w_outp[256 * g + 128:256 * g + 192, :] = jnp.zeros((64, 768), BF)
        r.w_outp[256 * g + 192:256 * g + 256, :] = r.w_out[192 * g + 128:192 * g + 192, :]
    for copy in cot_g[1:]:
        copy.wait_recv()
    proj_s.relay()
    for copy in att_p:
        copy.wait_recv()
    resid = x_own[...].astype(F32) + gain(4)
    for g in range(4):
        resid = resid + dot_nn(r.merged[g], r.w_outp[256 * g:256 * g + 256, :])
    r.resid[...] = resid
    normed, inverse = normalize(resid)
    r.normed_mid[...] = normed
    r.inverse_mid[...] = inverse
    r.lm_all[tile(u), :] = (normed * gain(1) + gain(6)).astype(BF)
    lm_own = r.lm_all.at[tile(u)]
    lm_g = [net.send(lm_own, lm_own, net.plane(m)) for m in (2, 1)]
    fc_s.finish_recv()

    r.vec_g[...] = jnp.zeros((16, 768), F32)

    def mlp_front(t):
        rows = tile(t)
        pre = dot_nn(r.lm_all[rows, :], r.w_fc[...]) + gain(8)
        square = pre * pre
        th = jnp.tanh(GELU_IN * (pre * (1.0 + 0.044715 * square)))
        r.act[rows, :] = (0.5 * pre * (1.0 + th)).astype(BF)
        r.slope[rows, :] = 0.5 * (1.0 + th) + (0.5 * GELU_IN) * pre * (1.0 - th * th) * (1.0 + 0.134145 * square)

    def mlp_back(t):
        rows = tile(t)
        gp = (r.slope[rows, :] * dot_nt(r.cot_all[rows, :], r.w_proj[...])).astype(BF)
        r.grad_pre[rows, :] = gp
        r.fcb[...] += jnp.sum(gp.astype(F32), 0, keepdims=True)
        r.gm_part[t] = dot_nt(gp, r.w_fc[...]).astype(BF)

    r.fcb[...] = jnp.zeros((1, 768), F32)
    mlp_front(u)
    lm_g[1].wait_recv()
    mlp_front(u ^ 1)
    plane_gather_forward(lm_g, r.lm_all)

    def reduce_core(i, t, part, land_c):
        return net.send(part.at[t], land_c.at[i], net.plane(1))

    def reduce_y(copy, part, land_c, mid, land_y):
        copy.wait_recv()
        mid[...] = (part[u ^ 2].astype(F32) + land_c[0].astype(F32)).astype(BF)
        return net.send(mid, land_y, net.plane(2))

    def reduce_end(copy_c, copy_y, part, land_c, land_y):
        copy_c.wait_recv()
        copy_y.wait_recv()
        return part[u].astype(F32) + land_c[1].astype(F32) + land_y[...].astype(F32)

    mlp_front(u ^ 2)
    proj_s.rest()
    lm_g[2].wait_recv()
    mlp_front(u ^ 3)
    proj_s.finish_recv()
    mlp_back(u ^ 3)
    gm_c0 = reduce_core(0, u ^ 3, r.gm_part, r.gm_c)
    mlp_back(u ^ 1)
    gm_c1 = reduce_core(1, u ^ 1, r.gm_part, r.gm_c)
    mlp_back(u ^ 2)
    gm_y = reduce_y(gm_c0, r.gm_part, r.gm_c, r.gm_mid, r.gm_y)
    mlp_back(u)
    r.vec_g[...] += jnp.where(row == 10 + u, r.fcb[...], 0.0)

    def branch_tile(t):
        r.br_part[t] = dot_nn(r.act[tile(t), :], r.w_proj[...]).astype(BF)

    def weight_grad(a, b, out, tiles):
        def one(i):
            cols = pl.ds(pl.multiple_of(128 * i, 128), 128)
            out[tile(i), :] = dot_tn(a[:, cols], b[...]).astype(BF)

        loop(tiles, one)

    def collect(base, grad, land_x, mine, land_z, relay):
        return Collect(
            net, r.co_send, r.co_recv, base,
            lambda zz: grad.at[rows_at(192 * zz + 96 * (1 - x), 96)],
            lambda zz: grad[rows_at(192 * zz + 96 * x, 96), :].astype(F32),
            land_x, mine, land_z, relay)

    proj_c = collect(0, r.proj_g, r.proj_x, r.proj_m, r.proj_z, r.proj_r)
    fc_c = collect(9, r.fc_g, r.fc_x, r.fc_m, r.fc_z, r.fc_r)
    qkv_c = collect(18, r.qkv_g, r.qkv_x, r.qkv_m, r.qkv_z, r.qkv_r)

    weight_grad(r.act, r.cot_all, r.proj_g, 6)
    proj_c.start()
    branch_tile(u ^ 3)
    branch_tile(u ^ 1)
    br_c = [reduce_core(0, u ^ 3, r.br_part, r.br_c), reduce_core(1, u ^ 1, r.br_part, r.br_c)]
    branch_tile(u ^ 2)
    branch_tile(u)

    gm = reduce_end(gm_c1, gm_y, r.gm_part, r.gm_c, r.gm_y)
    normed = r.normed_mid[...]
    r.vec_g[1:2, :] = jnp.sum(gm * normed, 0, keepdims=True)
    r.vec_g[5:6, :] = jnp.sum(gm, 0, keepdims=True)

    def norm_grad(grad, normed, inverse, g):
        e = grad * g
        return inverse * (
            e - jnp.mean(e, -1, keepdims=True) - normed * jnp.mean(e * normed, -1, keepdims=True)
        )

    cot = cot_own[...].astype(F32)
    r.vec_g[4:5, :] = jnp.sum(cot, 0, keepdims=True)
    grad_resid = cot + norm_grad(gm, normed, r.inverse_mid[...], gain(1))
    r.grad_resid[...] = grad_resid
    gb = grad_resid.astype(BF)
    r.gb[...] = gb
    r.vec_g[3:4, :] = jnp.sum(gb.astype(F32), 0, keepdims=True)

    def gmer_tile(g):
        r.gmer[g] = dot_nt(r.gb[...], r.w_outp[pl.ds(pl.multiple_of(256 * g, 256), 256), :]).astype(BF)

    loop(4, gmer_tile)
    ga_p = [net.send(r.gmer.at[u ^ m], r.ga.at[tile(u)], net.plane(m)) for m in (2, 3, 1)]
    r.ga[tile(u), :] = r.gmer[u]
    weight_grad(r.lm_all, r.grad_pre, r.fc_g, 6)
    for g in range(4):
        res = dot_tn(r.merged[g], r.gb[...]).astype(BF)
        at = slice(48 * g, 48 * g + 48)
        r.out_g[0, 0, at, :] = res[0:48]
        r.out_g[1, 0, at, :] = res[48:96]
        r.out_g[0, 1, 48 * g:48 * g + 32, :] = res[96:128]
        r.out_g[0, 1, 48 * g + 32:48 * g + 48, :] = res[192:208]
        r.out_g[1, 1, at, :] = res[208:256]
    og_c = net.send(r.out_g.at[1 - c], r.og_c, net.plane(1))
    proj_c.part(0)
    proj_c.part(1)
    for copy in ga_p:
        copy.wait_recv()

    low = lane((512, 128)) < 64
    ga01 = r.ga[:, 0:128]
    zero = jnp.zeros((512, 128), BF)
    r.gam[0] = jnp.where(low, ga01.astype(F32), 0.0).astype(BF)
    r.gam[1] = jnp.where(low, 0.0, ga01.astype(F32)).astype(BF)
    r.gam[2] = r.ga[:, 128:256]
    prod = jnp.transpose(ga01.astype(F32)) * r.att_t[0]
    r.delta[0] = jnp.sum(prod[0:64], 0, keepdims=True)
    r.delta[1] = jnp.sum(prod[64:128], 0, keepdims=True)
    prod = jnp.transpose(r.ga[:, 128:256].astype(F32)) * r.att_t[1]
    r.delta[2] = jnp.sum(prod, 0, keepdims=True)
    r.dq_t[...] = jnp.zeros((3, 128, 512), F32)

    def back(j):
        factor = [jnp.exp(r.m_at[j * 3 + h] - r.m_run[h]) * r.l_inv[h] for h in range(3)]

        def keys(kt):
            rows = rows_at(128 * kt, 128)
            for h in range(3):
                vc = 128 if h < 2 else 256
                p = r.pt[j * 3 + h, rows, :].astype(F32) * factor[h]
                dp = dot_nt(r.kv_all[j, rows, vc:vc + 128], r.gam[h])
                r.ds[h, rows, :] = (p * (dp - r.delta[h])).astype(BF)
                r.pt[j * 3 + h, rows, :] = p.astype(BF)

        def sums(kt):
            rows = rows_at(128 * kt, 128)
            pair = lambda of, first, second: dot_nn(of(0), first) + dot_nn(of(1), second)
            ds = lambda h: r.ds[h, rows, :]
            p = lambda h: r.pt[j * 3 + h, rows, :]
            r.dkv[rows, 0:128] = pair(ds, r.qm[0], r.qm[1])
            r.dkv[rows, 128:256] = pair(p, r.gam[0], r.gam[1])
            r.dkv[rows, 256:384] = dot_nn(ds(2), r.qm[2]) + dot_nn(p(2), r.gam[2])

        loop(4, keys)
        loop(4, sums)
        for h in range(3):
            kc = 0 if h < 2 else 256
            r.dq_t[h] += dot_tn(r.kv_all[j, :, kc:kc + 128], r.ds[h])

    def chain_copy(way, step):
        target = jnp.clip(jnp.where(way == 0, z - 1, z + 1), 0, nz - 1)
        at = way * (nz - 1) + step - 1
        return pltpu.make_async_remote_copy(
            src_ref=r.chain.at[at], dst_ref=r.chain_land.at[at],
            send_sem=r.ch_send.at[at], recv_sem=r.ch_recv.at[at],
            device_id=(x, target, u), device_id_type=MESH)

    def chain_step(step):
        def either(way):
            j = jnp.where(way == 0, z - step, z + step)
            behind = jnp.where(way == 0, z + 1, z - 1)

            @pl.when(jnp.logical_and(j >= 0, j < nz))
            def _():
                back(j)
                at = way * (nz - 1) + step - 1
                comes = jnp.logical_and(behind >= 0, behind < nz)
                if step < nz - 1:
                    @pl.when(comes)
                    def _():
                        chain_copy(way, step + 1).wait_recv()
                        r.chain[at] = (r.dkv[...] + r.chain_land[at + 1].astype(F32)).astype(BF)

                    @pl.when(jnp.logical_not(comes))
                    def _():
                        r.chain[at] = r.dkv[...].astype(BF)
                else:
                    r.chain[at] = r.dkv[...].astype(BF)
                chain_copy(way, step).start()

        loop(2, either)

    for step in range(nz - 1, 0, -1):
        chain_step(step)
        if step == nz - 1:
            proj_c.part(2)
            proj_c.part(3)
            fc_c.start()
            br_y = reduce_y(br_c[0], r.br_part, r.br_c, r.br_mid, r.br_y)
            og_c.wait_recv()
            r.og_1[...] = (r.out_g[c].astype(F32) + r.og_c[...].astype(F32)).astype(BF)
            og_y = net.send(r.og_1.at[1 - y], r.og_y, net.plane(2))
        if step == nz - 2:
            proj_c.second()
            r.output[...] = (
                r.resid[...] + gain(5) + reduce_end(br_c[1], br_y, r.br_part, r.br_c, r.br_y)
            ).astype(BF)
            fc_c.part(0)
            fc_c.part(1)
            og_y.wait_recv()
            r.og_2[...] = (r.og_1[y].astype(F32) + r.og_y[...].astype(F32)).astype(BF)
            og_x = net.send(r.og_2.at[:, half_cols(1 - x)], r.og_x, net.other_x())
        if step == 1:
            og_x.wait_recv()
            r.og_3[...] = (r.og_2[:, half_cols(x)].astype(F32) + r.og_x[...].astype(F32)).astype(BF)
            og_z = [
                net.send(r.og_3.at[rows_at(48 * net.zplus(d), 48)], r.og_z.at[d - 1], net.line(d))
                for d in range(1, nz)
            ]
            fc_c.part(2)
            fc_c.part(3)
    back(z)

    fc_c.second()
    @pl.when(z + 1 < nz)
    def _():
        chain_copy(0, 1).wait_recv()
        r.dkv[...] += r.chain_land[0].astype(F32)

    @pl.when(z >= 1)
    def _():
        chain_copy(1, 1).wait_recv()
        r.dkv[...] += r.chain_land[nz - 1].astype(F32)

    r.gqkv[:, 128:512] = r.dkv[...].astype(BF)
    dq = jnp.transpose(jnp.where(rowi < 64, r.dq_t[0], r.dq_t[1]) * 0.125)
    r.gqkv[:, 0:128] = dq.astype(BF)
    r.gqkv[:, 512:576] = jnp.transpose(r.dq_t[2] * 0.125)[:, 0:64].astype(BF)

    weight_grad(r.ln_all, r.gqkv, r.qkv_g, 6)
    qkv_c.start()

    def gin_tile(t):
        r.gi_part[t] = dot_nt(r.gqkv[tile(t), :], r.w_qkv[...]).astype(BF)

    gin_tile(u ^ 3)
    gi_c0 = reduce_core(0, u ^ 3, r.gi_part, r.gi_c)
    gin_tile(u ^ 1)
    gi_c1 = reduce_core(1, u ^ 1, r.gi_part, r.gi_c)
    gin_tile(u ^ 2)
    gi_y = reduce_y(gi_c0, r.gi_part, r.gi_c, r.gi_mid, r.gi_y)
    gin_tile(u)
    r.vec_g[:, 0:576] += jnp.where(row[:, 0:576] == 6 + u, jnp.sum(r.gqkv[...].astype(F32), 0, keepdims=True), 0.0)
    qkv_c.first()
    proj_c.total(r.acc)
    r.proj_f[...] = r.acc[...].astype(BF)
    mine = rows_at(96 * x, 96)
    r.proj_o[mine, :] = r.proj_f[...]
    proj_last = net.send(r.proj_f, r.proj_o.at[mine], net.other_x())

    finals = []

    def hand_out(base, final, native):
        for xx in range(2):
            for cc in range(2):
                target_x = x ^ xx
                target_u = 2 * x + cc
                here = jnp.logical_and(xx == 0, target_u == u)
                k = base + 2 * xx + cc
                copy = pltpu.make_async_remote_copy(
                    src_ref=final.at[pl.ds(48 * cc, 48)], dst_ref=native.at[u], send_sem=r.f_send.at[k],
                    recv_sem=r.f_recv.at[base + u], device_id=(target_x, z, target_u), device_id_type=MESH)

                @pl.when(jnp.logical_not(here))
                def _():
                    copy.start()

                @pl.when(here)
                def _():
                    native[u] = final[pl.ds(48 * cc, 48), :]

                finals.append((here, copy))

    def await_native(base, final, native):
        for who in range(4):
            copy = pltpu.make_async_remote_copy(
                src_ref=final.at[pl.ds(0, 48)], dst_ref=native.at[who], send_sem=r.f_send.at[base],
                recv_sem=r.f_recv.at[base + who], device_id=(1 - x, z, u), device_id_type=MESH)

            @pl.when(jnp.logical_not(jnp.logical_and(x == y, u == who)))
            def _():
                copy.wait_recv()

    gin = reduce_end(gi_c1, gi_y, r.gi_part, r.gi_c, r.gi_y)
    normed, inverse = normalize(x_own[...].astype(F32))
    r.vec_g[0:1, :] = jnp.sum(gin * normed, 0, keepdims=True)
    r.vec_g[2:3, :] = jnp.sum(gin, 0, keepdims=True)
    vec_m = [net.send(r.vec_g, r.vg_p.at[m - 1], net.plane(m)) for m in (1, 2, 3)]
    r.input_grad[...] = (r.grad_resid[...] + norm_grad(gin, normed, inverse, gain(0))).astype(BF)
    qkv_c.second()
    fc_c.total(r.acc)
    r.fc_f[...] = r.acc[...].astype(BF)
    hand_out(0, r.fc_f, r.fc_o)
    total = r.vec_g[...]
    for m in range(3):
        vec_m[m].wait_recv()
        total = total + r.vg_p[m]
    r.vg_1[...] = total
    vec_l = [net.send(r.vg_1, r.vg_z.at[d - 1], net.line(d)) for d in range(1, nz)]
    total = r.og_3[rows_at(48 * z, 48), :].astype(F32)
    for d in range(nz - 1):
        og_z[d].wait_recv()
        total = total + r.og_z[d].astype(F32)
    r.out_o[:, half_cols(x)] = total.astype(BF)
    og_last = net.send(r.out_o.at[:, half_cols(x)], r.out_o.at[:, half_cols(x)], net.other_x())
    total = r.vg_1[...]
    for d in range(nz - 1):
        vec_l[d].wait_recv()
        total = total + r.vg_z[d]
    r.vg_2[...] = total
    vec_last = net.send(r.vg_2, r.vg_x, net.other_x())
    qkv_c.total(r.acc_q)
    r.qkv_f[...] = r.acc_q[...].astype(BF)
    hand_out(4, r.qkv_f, r.qkv_o)
    vec_last.wait_recv()
    total = r.vg_2[...] + r.vg_x[...]
    pick = lambda i: jnp.sum(jnp.where(row == i, total, 0.0), 0, keepdims=True)
    heads, hidden = pick(6 + z), pick(10 + u)
    bias[0:1, 0:128] = heads[:, 0:128]
    bias[0:1, 128:192] = heads[:, 512:576]
    bias[1:2, 0:128] = heads[:, 256:384]
    bias[1:2, 128:192] = heads[:, 448:512]
    mine8 = pltpu.roll(total[0:8], 768 - 48 * (4 * z + u), 1)
    vp[0:8, :] = mine8
    both = pltpu.roll(bias[...], 256 - 48 * u, 1)
    vp[6:8, 0:256] = both[0:2]
    vp[8:16, :] = pltpu.roll(jnp.broadcast_to(hidden, (8, 768)), 768 - 192 * z, 1)
    r.vec_o[...] = vp[...]
    proj_last.wait_recv()
    og_last.wait_recv()
    await_native(0, r.fc_f, r.fc_o)
    await_native(4, r.qkv_f, r.qkv_o)

    for here, copy in finals:
        @pl.when(jnp.logical_not(here))
        def _():
            copy.wait_send()
    for step in range(nz - 1):
        for way in range(2):
            @pl.when(kv_sends(way, step))
            def _():
                kv_copy(way, step).wait_send()
    for step in range(1, nz):
        for way in range(2):
            @pl.when(z - step >= 0 if way == 0 else z + step < nz)
            def _():
                chain_copy(way, step).wait_send()
    for part in (qkv_s, fc_s, proj_s, out_s, proj_c, fc_c, qkv_c):
        part.finish()
    net.finish()


def block_call(nz, **operands):
    def vm(*shape, kind=BF):
        return pltpu.VMEM(shape, kind)

    outs = dict(
        output=((128, 768), BF), input_grad=((128, 768), BF), qkv_o=((4, 48, 576), BF),
        fc_o=((4, 48, 768), BF), proj_o=((192, 768), BF), out_o=((48, 768), BF), vec_o=((16, 768), F32),
    )
    f = lambda *shape: vm(*shape, kind=F32)
    keys = 512 * nz
    scratch = dict(
        qkv_raw=vm(48, 2304), fc_raw=vm(48, 3072), qkv_pre=vm(4, 48, 576), fc_pre=vm(4, 48, 768),
        vec_f32=f(16, 768), bias_f32=f(8, 256), vec_pre=vm(16, 768),
        pos_row=pltpu.VMEM((1, keys), jnp.int32), pos_col=pltpu.VMEM((keys, 1), jnp.int32),
        w_qkv=vm(768, 576), w_fc=vm(768, 768), w_proj=vm(768, 768), w_out=vm(768, 768), w_outp=vm(1024, 768),
        vec_land_z=vm(nz - 1, 16, 768), vec_u=vm(16, 768), vec_land_p=vm(3, 16, 768), vec=f(16, 768),
        x_all=vm(512, 768), cot_all=vm(512, 768), ln_all=vm(512, 768), lm_all=vm(512, 768),
        qm=vm(3, 512, 128), kv_all=vm(nz, 512, 384), s_buf=f(512, 512), pt=vm(nz * 3, 512, 512),
        m_run=f(3, 1, 512), l_run=f(3, 1, 512), l_inv=f(3, 1, 512), m_at=f(nz * 3, 1, 512), o_t=f(3, 128, 512),
        att_t=f(2, 128, 512), att=vm(512, 256), merged=vm(4, 128, 256),
        resid=f(128, 768), normed_mid=f(128, 768), inverse_mid=f(128, 1), slope=f(512, 768),
        act=vm(512, 768), grad_pre=vm(512, 768), fcb=f(1, 768), vec_g=f(16, 768),
        gm_part=vm(4, 128, 768), gm_c=vm(2, 128, 768), gm_mid=vm(128, 768), gm_y=vm(128, 768),
        br_part=vm(4, 128, 768), br_c=vm(2, 128, 768), br_mid=vm(128, 768), br_y=vm(128, 768),
        gi_part=vm(4, 128, 768), gi_c=vm(2, 128, 768), gi_mid=vm(128, 768), gi_y=vm(128, 768),
        grad_resid=f(128, 768), gb=vm(128, 768), gmer=vm(4, 128, 256), ga=vm(512, 256), gam=vm(3, 512, 128),
        delta=f(3, 1, 512), ds=vm(3, 512, 512), dq_t=f(3, 128, 512), dkv=f(512, 384),
        chain=vm(2 * (nz - 1), 512, 384), chain_land=vm(2 * (nz - 1), 512, 384), gqkv=vm(512, 576),
        qkv_g=vm(768, 576), fc_g=vm(768, 768), proj_g=vm(768, 768), out_g=vm(2, 2, 192, 768),
        qkv_x=vm(nz, 96, 576), fc_x=vm(nz, 96, 768), proj_x=vm(nz, 96, 768),
        qkv_m=vm(nz, 96, 576), fc_m=vm(nz, 96, 768), proj_m=vm(nz, 96, 768),
        qkv_z=vm(nz - 1, 96, 576), fc_z=vm(nz - 1, 96, 768), proj_z=vm(nz - 1, 96, 768),
        qkv_r=vm(96, 576), fc_r=vm(96, 768), proj_r=vm(96, 768), acc=f(96, 768), acc_q=f(96, 576),
        qkv_f=vm(96, 576), fc_f=vm(96, 768), proj_f=vm(96, 768),
        og_c=vm(2, 192, 768), og_1=vm(2, 192, 768), og_y=vm(192, 768), og_2=vm(192, 768),
        og_x=vm(192, 384), og_3=vm(192, 384), og_z=vm(nz - 1, 48, 384),
        vg_p=f(3, 16, 768), vg_1=f(16, 768), vg_z=f(nz - 1, 16, 768), vg_2=f(16, 768), vg_x=f(16, 768),
        send_sem=pltpu.SemaphoreType.DMA((112,)), recv_sem=pltpu.SemaphoreType.DMA((112,)),
        sp_send=pltpu.SemaphoreType.DMA((32,)), sp_recv=pltpu.SemaphoreType.DMA((32,)),
        co_send=pltpu.SemaphoreType.DMA((27,)), co_recv=pltpu.SemaphoreType.DMA((27,)),
        local_sem=pltpu.SemaphoreType.DMA((6,)),
        kv_send=pltpu.SemaphoreType.DMA((2 * nz,)), kv_recv=pltpu.SemaphoreType.DMA((2 * nz,)),
        ch_send=pltpu.SemaphoreType.DMA((2 * nz,)), ch_recv=pltpu.SemaphoreType.DMA((2 * nz,)),
        f_send=pltpu.SemaphoreType.DMA((8,)), f_recv=pltpu.SemaphoreType.DMA((8,)),
    )
    names = [*operands, *outs, *scratch]
    places = {name: pl.BlockSpec(memory_space=pl.ANY) for name in ("x_in", "cot_in", "qkv_in", "fc_in", "out_in", "proj_in")}
    places["order_in"] = pl.BlockSpec(memory_space=pltpu.SMEM)

    def kernel(*refs):
        block_kernel(nz, types.SimpleNamespace(**dict(zip(names, refs, strict=True))))

    got = pl.pallas_call(
        kernel,
        out_shape=tuple(jax.ShapeDtypeStruct(*s) for s in outs.values()),
        in_specs=[places.get(name, VSPEC) for name in operands],
        out_specs=(VSPEC,) * len(outs),
        scratch_shapes=list(scratch.values()),
        compiler_params=pltpu.CompilerParams(
            collective_id=0, has_side_effects=True, vmem_limit_bytes=60 * 2**20
        ),
        name="transformer_block",
    )(*operands.values())
    return dict(zip(outs, got, strict=True))


def hand_over_kernel(nz, output, input_grad, qkv_o, fc_o, proj_o, out_o, vec_o,
                     output_f, input_grad_f, gains_f, biases_f, mid_f, vb_f, qkv_f, out_f, fc_f, fcb_f, proj_f):
    output_f[...] = output[...]
    input_grad_f[...] = input_grad[...]
    gains_f[...] = vec_o[0:2, 0:48]
    biases_f[0:1, :] = vec_o[2:3, 0:48]
    biases_f[1:2, :] = vec_o[6:7, 0:48]
    biases_f[2:4, :] = vec_o[3:5, 0:48]
    mid_f[...] = vec_o[5:6, 0:48]
    vb_f[...] = vec_o[7:8, 0:48]
    fcb_f[...] = vec_o[8:9, 0:192]
    out_f[...] = out_o[...].astype(F32)
    proj_f[...] = proj_o[...].astype(F32)
    for g in range(4):
        for t in range(3):
            qkv_f[:, 768 * t + 192 * g:768 * t + 192 * g + 128] = qkv_o[g, :, 128 * t:128 * t + 128].astype(F32)
        for at, t in ((384, 1), (448, 2), (512, 0)):
            qkv_f[:, 768 * t + 192 * g + 128:768 * t + 192 * g + 192] = qkv_o[g, :, at:at + 64].astype(F32)
        for zz in range(nz):
            fc_f[:, 768 * zz + 192 * g:768 * zz + 192 * g + 192] = fc_o[g, :, 192 * zz:192 * zz + 192].astype(F32)


def hand_over(nz, got):
    shapes = [((128, 768), BF), ((128, 768), BF), ((2, 48), F32), ((4, 48), F32), ((1, 48), F32), ((1, 48), F32),
              ((48, 2304), F32), ((48, 768), F32), ((48, 3072), F32), ((1, 192), F32), ((192, 768), F32)]
    return pl.pallas_call(
        functools.partial(hand_over_kernel, nz),
        out_shape=tuple(jax.ShapeDtypeStruct(*s) for s in shapes),
        in_specs=[VSPEC] * len(got),
        out_specs=(VSPEC,) * len(shapes),
        compiler_params=pltpu.CompilerParams(vmem_limit_bytes=16 * 2**20),
        name="hand_over",
    )(*got.values())


def device_fast(nz, inputs, stretch_order, norm_gains, biases, mid_shift, value_bias, qkv_weight, out_weight, fc_weight, fc_bias, proj_weight, cotangent):
    got = block_call(
        nz,
        x_in=inputs[0],
        cot_in=cotangent[0],
        qkv_in=qkv_weight,
        fc_in=fc_weight,
        out_in=out_weight,
        proj_in=proj_weight,
        gains_in=norm_gains,
        biases_in=biases,
        mid_in=mid_shift[None],
        vb_in=value_bias[None],
        fcb_in=fc_bias[None],
        order_in=stretch_order,
    )
    output, input_grad, gains, rows, mid, vb, qkv, out, fc, fcb, proj = hand_over(nz, got)
    return output[None], input_grad[None], gains, rows, mid[0], vb[0], qkv, out, fc, fcb[0], proj


def solution(mesh):
    placed = (
        P("dp", ("blk", "uly"), None),
        P("dp", None),
        P(None, ("blk", "uly")),
        P(None, ("blk", "uly")),
        P(("blk", "uly")),
        P(("blk", "uly")),
        P(("blk", "uly"), None),
        P(("blk", "uly"), None),
        P(("blk", "uly"), None),
        P(("blk", "uly")),
        P(("blk", "uly"), None),
        P("dp", ("blk", "uly"), None),
    )
    sizes = dict(mesh.shape)
    nz = sizes["blk"]
    fast = sizes["uly"] == 4 and sizes["dp"] == 2 and nz == 4
    chosen = functools.partial(device_fast, nz) if fast else per_device
    return jax.shard_map(
        chosen,
        mesh=mesh,
        in_specs=placed,
        out_specs=(
            P("dp", ("blk", "uly"), None),
            P("dp", ("blk", "uly"), None),
            P(None, ("blk", "uly")),
            P(None, ("blk", "uly")),
            P(("blk", "uly")),
            P(("blk", "uly")),
            P(("blk", "uly"), None),
            P(("blk", "uly"), None),
            P(("blk", "uly"), None),
            P(("blk", "uly")),
            P(("blk", "uly"), None),
        ),
        check_vma=False,
    )
```

```python
import functools
import math
import types

import jax
import jax.numpy as jnp
from jax import lax
from jax.experimental import pallas as pl
from jax.experimental.pallas import tpu as pltpu
from jax.sharding import PartitionSpec as P

HEADS = 12


masked_score = -1e30


def layer_norm(values, gain, shift):
    center = values - jnp.mean(values, -1, keepdims=True)
    inverse = lax.rsqrt(jnp.mean(center * center, -1, keepdims=True) + 1e-05)
    normed = center * inverse
    return (normed * gain + shift, normed, inverse)


def norm_back(grad_out, normed, inverse, gain):
    scaled = grad_out * gain
    mean_plain = jnp.mean(scaled, -1, keepdims=True)
    mean_mixed = jnp.mean(scaled * normed, -1, keepdims=True)
    return inverse * (scaled - mean_plain - normed * mean_mixed)


def sweep(step_fn, carried, parts):
    row_count = parts[0].shape[1]
    sweep_rows = math.gcd(row_count, 1024)

    def turn(inner, turn_number):
        offset = turn_number * sweep_rows
        blocks = tuple((lax.dynamic_slice_in_dim(part, offset, sweep_rows, 1) for part in parts))
        return (step_fn(inner, blocks, offset), None)

    result, _ = lax.scan(turn, carried, jnp.arange(row_count // sweep_rows, dtype=jnp.int32))
    return result


def per_device(
    inputs,
    stretch_order,
    norm_gains,
    biases,
    mid_shift,
    value_bias,
    qkv_weight,
    out_weight,
    fc_weight,
    fc_bias,
    proj_weight,
    cotangent,
):
    fp32 = jnp.float32
    bf16 = jnp.bfloat16
    gain_rows, shifts, mid_gathered, value_shift, w_qkv, w_out, w_fc, b_fc, w_proj = (
        lax.all_gather(norm_gains, ("blk", "uly"), axis=1, tiled=True),
        lax.all_gather(biases, ("blk", "uly"), axis=1, tiled=True),
        lax.all_gather(mid_shift, ("blk", "uly"), axis=0, tiled=True),
        lax.all_gather(value_bias, ("blk", "uly"), axis=0, tiled=True),
        lax.all_gather(qkv_weight, ("blk", "uly"), axis=0, tiled=True),
        lax.all_gather(out_weight, ("blk", "uly"), axis=0, tiled=True),
        lax.all_gather(fc_weight, ("blk", "uly"), axis=0, tiled=True),
        lax.all_gather(fc_bias, ("blk", "uly"), axis=0, tiled=True),
        lax.all_gather(proj_weight, ("blk", "uly"), axis=0, tiled=True),
    )
    gain_rows = gain_rows.astype(fp32)
    shifts = shifts.astype(fp32)
    mid_gathered = mid_gathered.astype(fp32)
    seq_count, row_len, width = inputs.shape
    uly_count = lax.axis_size("uly")
    local_heads = HEADS // uly_count
    head_dim = width // HEADS
    head_span = local_heads * head_dim
    block_rows = uly_count * row_len
    half_rows = row_len // 2
    seq_len = stretch_order.shape[1] * half_rows
    score_scale = head_dim ** (-0.5)
    tokens = inputs.astype(fp32).reshape(seq_count * row_len, width)
    ln_in, normed_in, inverse_in = layer_norm(tokens, gain_rows[0], shifts[0])
    ln_in = ln_in.astype(bf16)
    qkv_shift = jnp.concatenate([shifts[1], jnp.zeros((width,), fp32), value_shift.astype(fp32)])
    qkv = (jnp.dot(ln_in, w_qkv, preferred_element_type=fp32) + qkv_shift).astype(bf16)
    head_data = lax.all_to_all(
        qkv.reshape(seq_count, row_len, 3, uly_count, head_span),
        "uly",
        split_axis=3,
        concat_axis=1,
        tiled=True,
    )
    queries = head_data[:, :, 0, 0].reshape(seq_count, block_rows, local_heads, head_dim)
    key_rows = head_data[:, :, 1, 0]
    value_rows = head_data[:, :, 2, 0]
    positions = (
        stretch_order[:, :, None] * half_rows
        + jnp.arange(half_rows, dtype=jnp.int32)[None, None, :]
    ).reshape(seq_count, seq_len)
    query_pos = lax.dynamic_slice_in_dim(
        positions, lax.axis_index("blk") * block_rows, block_rows, 1
    )

    def score_block(key_part, key_start):
        part_rows = key_part.shape[1]
        key_pos = lax.dynamic_slice_in_dim(positions, key_start, part_rows, 1)
        scores = (
            jnp.einsum(
                "sqhd,skhd->shqk",
                queries,
                key_part.reshape(seq_count, part_rows, local_heads, head_dim),
                preferred_element_type=fp32,
            )
            * score_scale
        )
        causal = query_pos[:, None, :, None] >= key_pos[:, None, None, :]
        return (scores, causal)

    def stats_step(carried, blocks, key_start):
        row_max, row_total = carried
        scores, causal = score_block(blocks[0], key_start)
        new_max = jnp.maximum(row_max, jnp.max(jnp.where(causal, scores, masked_score), -1))
        row_total = row_total * jnp.exp(row_max - new_max) + jnp.sum(
            jnp.where(causal, jnp.exp(scores - new_max[..., None]), 0.0), -1
        )
        return (new_max, row_total)

    def softmax_of(scores, causal, row_max, row_total):
        return jnp.where(causal, jnp.exp(scores - row_max[..., None]) / row_total[..., None], 0.0)

    def make_output_step(row_max, row_total):

        def output_step(acc_out, blocks, key_start):
            scores, causal = score_block(blocks[0], key_start)
            attn_probs = softmax_of(scores, causal, row_max, row_total).astype(bf16)
            part_rows = blocks[1].shape[1]
            value_part = blocks[1].reshape(seq_count, part_rows, local_heads, head_dim)
            return acc_out + jnp.einsum(
                "shqk,skhd->sqhd", attn_probs, value_part, preferred_element_type=fp32
            )

        return output_step

    stats_init = (
        jnp.full((seq_count, local_heads, block_rows), masked_score, fp32),
        jnp.zeros((seq_count, local_heads, block_rows), fp32),
    )
    empty_out = jnp.zeros((seq_count, block_rows, local_heads, head_dim), fp32)
    all_keys, all_values = (
        lax.all_gather(key_rows, "blk", axis=1, tiled=True),
        lax.all_gather(value_rows, "blk", axis=1, tiled=True),
    )
    row_max, row_total = sweep(stats_step, stats_init, (all_keys,))
    attended = sweep(make_output_step(row_max, row_total), empty_out, (all_keys, all_values))
    attended_low = attended.astype(bf16).reshape(seq_count, block_rows, 1, head_span)
    merged = lax.all_to_all(attended_low, "uly", split_axis=1, concat_axis=2, tiled=True).reshape(
        seq_count * row_len, width
    )
    resid = tokens + (jnp.dot(merged, w_out, preferred_element_type=fp32) + shifts[2])
    ln_mid, normed_mid, inverse_mid = layer_norm(resid, gain_rows[1], mid_gathered)
    ln_mid = ln_mid.astype(bf16)
    pre_act = jnp.dot(ln_mid, w_fc, preferred_element_type=fp32) + b_fc.astype(fp32)

    def gelu_piece(pre_values):
        return jax.nn.gelu(pre_values, approximate=True)

    act, gelu_back = jax.vjp(gelu_piece, pre_act)
    act = act.astype(bf16)
    result = resid + (jnp.dot(act, w_proj, preferred_element_type=fp32) + shifts[3])
    grad_low = cotangent.reshape(seq_count * row_len, width)
    grad_out = grad_low.astype(fp32)
    proj_grad = jnp.einsum("ta,tb->ab", act, grad_low, preferred_element_type=fp32)
    proj_shift_grad = jnp.sum(grad_out, 0)
    grad_act = jnp.einsum("tb,ab->ta", grad_low, w_proj, preferred_element_type=fp32)
    grad_pre = gelu_back(grad_act)[0].astype(bf16)
    fc_grad = jnp.einsum("ta,tb->ab", ln_mid, grad_pre, preferred_element_type=fp32)
    fc_shift_grad = jnp.sum(grad_pre.astype(fp32), 0)
    grad_mid = jnp.einsum("tb,ab->ta", grad_pre, w_fc, preferred_element_type=fp32)
    gain_mid_grad = jnp.sum(grad_mid * normed_mid, 0)
    shift_mid_grad = jnp.sum(grad_mid, 0)
    grad_resid = grad_out + norm_back(grad_mid, normed_mid, inverse_mid, gain_rows[1])
    grad_branch = grad_resid.astype(bf16)
    out_grad = jnp.einsum("ta,tb->ab", merged, grad_branch, preferred_element_type=fp32)
    out_shift_grad = jnp.sum(grad_branch.astype(fp32), 0)
    grad_merged = jnp.einsum("tb,ab->ta", grad_branch, w_out, preferred_element_type=fp32).astype(
        bf16
    )
    grad_att = lax.all_to_all(
        grad_merged.reshape(seq_count, row_len, uly_count, head_span),
        "uly",
        split_axis=2,
        concat_axis=1,
        tiled=True,
    )
    grad_att = grad_att.reshape(seq_count, block_rows, local_heads, head_dim)
    delta = jnp.transpose(jnp.sum(grad_att.astype(fp32) * attended, -1), (0, 2, 1))
    back_keys, back_values = (all_keys, all_values)
    sweep_rows = math.gcd(seq_len, 1024)

    def query_terms(offset):
        key_part = lax.dynamic_slice_in_dim(back_keys, offset, sweep_rows, 1)
        value_part = lax.dynamic_slice_in_dim(back_values, offset, sweep_rows, 1)
        scores, causal = score_block(key_part, offset)
        attn_probs = softmax_of(scores, causal, row_max, row_total)
        key_heads = key_part.reshape(seq_count, sweep_rows, local_heads, head_dim)
        value_heads = value_part.reshape(seq_count, sweep_rows, local_heads, head_dim)
        grad_probs = jnp.einsum(
            "sqhd,skhd->shqk", grad_att, value_heads, preferred_element_type=fp32
        )
        grad_scores = (attn_probs * (grad_probs - delta[..., None])).astype(bf16)
        query_term = (
            jnp.einsum("shqk,skhd->sqhd", grad_scores, key_heads, preferred_element_type=fp32)
            * score_scale
        )
        return (query_term, grad_scores, attn_probs.astype(bf16))

    query_init = jnp.zeros((seq_count, block_rows, local_heads, head_dim), fp32)

    def back_step(carried, turn_number):
        grad_query, kv_buffer = carried
        offset = turn_number * sweep_rows
        query_term, grad_scores, probs_low = query_terms(offset)
        grad_key = (
            jnp.einsum("shqk,sqhd->skhd", grad_scores, queries, preferred_element_type=fp32)
            * score_scale
        )
        grad_value = jnp.einsum("shqk,sqhd->skhd", probs_low, grad_att, preferred_element_type=fp32)
        kv_pair = jnp.stack(
            [
                grad_key.reshape(seq_count, sweep_rows, head_span),
                grad_value.reshape(seq_count, sweep_rows, head_span),
            ],
            2,
        )
        kv_buffer = lax.dynamic_update_slice_in_dim(kv_buffer, kv_pair, offset, 1)
        return ((grad_query + query_term, kv_buffer), None)

    back_init = (query_init, jnp.zeros((seq_count, seq_len, 2, head_span), fp32))
    back_done, _ = lax.scan(
        back_step, back_init, jnp.arange(seq_len // sweep_rows, dtype=jnp.int32)
    )
    grad_query, kv_buffer = back_done
    kv_summed = lax.psum_scatter(
        kv_buffer.astype(jnp.bfloat16), "blk", scatter_dimension=1, tiled=True
    ).astype(jnp.float32)
    grad_heads = jnp.concatenate(
        [
            grad_query.reshape(seq_count, block_rows, 1, head_span).astype(bf16),
            kv_summed.astype(bf16),
        ],
        2,
    )
    grad_qkv = lax.all_to_all(
        grad_heads.reshape(seq_count, block_rows, 3, 1, head_span),
        "uly",
        split_axis=1,
        concat_axis=3,
        tiled=True,
    )
    grad_qkv = grad_qkv.reshape(seq_count * row_len, 3 * width)
    qkv_grad = jnp.einsum("ta,tb->ab", ln_in, grad_qkv, preferred_element_type=fp32)
    column_sums = jnp.sum(grad_qkv.astype(fp32), 0)
    grad_in_norm = jnp.einsum("tb,ab->ta", grad_qkv, w_qkv, preferred_element_type=fp32)
    gain_in_grad = jnp.sum(grad_in_norm * normed_in, 0)
    shift_in_grad = jnp.sum(grad_in_norm, 0)
    grad_input = grad_resid + norm_back(grad_in_norm, normed_in, inverse_in, gain_rows[0])
    gains_grad = jnp.stack([gain_in_grad, gain_mid_grad])
    biases_grad = jnp.stack([shift_in_grad, column_sums[:width], out_shift_grad, proj_shift_grad])
    value_grad = column_sums[2 * width :]
    shard_grads = (
        lax.psum_scatter(gains_grad, ("blk", "uly"), scatter_dimension=1, tiled=True),
        lax.psum_scatter(biases_grad, ("blk", "uly"), scatter_dimension=1, tiled=True),
        lax.psum_scatter(shift_mid_grad, ("blk", "uly"), scatter_dimension=0, tiled=True),
        lax.psum_scatter(value_grad, ("blk", "uly"), scatter_dimension=0, tiled=True),
        lax.psum_scatter(qkv_grad, ("blk", "uly"), scatter_dimension=0, tiled=True),
        lax.psum_scatter(out_grad, ("blk", "uly"), scatter_dimension=0, tiled=True),
        lax.psum_scatter(fc_grad, ("blk", "uly"), scatter_dimension=0, tiled=True),
        lax.psum_scatter(fc_shift_grad, ("blk", "uly"), scatter_dimension=0, tiled=True),
        lax.psum_scatter(proj_grad, ("blk", "uly"), scatter_dimension=0, tiled=True),
    )
    shard_grads = (
        lax.psum(shard_grads[0].astype(jnp.bfloat16), "dp").astype(jnp.float32),
        lax.psum(shard_grads[1].astype(jnp.bfloat16), "dp").astype(jnp.float32),
        lax.psum(shard_grads[2].astype(jnp.bfloat16), "dp").astype(jnp.float32),
        lax.psum(shard_grads[3].astype(jnp.bfloat16), "dp").astype(jnp.float32),
        lax.psum(shard_grads[4].astype(jnp.bfloat16), "dp").astype(jnp.float32),
        lax.psum(shard_grads[5].astype(jnp.bfloat16), "dp").astype(jnp.float32),
        lax.psum(shard_grads[6].astype(jnp.bfloat16), "dp").astype(jnp.float32),
        lax.psum(shard_grads[7].astype(jnp.bfloat16), "dp").astype(jnp.float32),
        lax.psum(shard_grads[8].astype(jnp.bfloat16), "dp").astype(jnp.float32),
    )
    output = result.astype(bf16).reshape(seq_count, row_len, width)
    input_grad = grad_input.astype(bf16).reshape(seq_count, row_len, width)
    return (
        output,
        input_grad,
        shard_grads[0],
        shard_grads[1],
        shard_grads[2],
        shard_grads[3],
        shard_grads[4],
        shard_grads[5],
        shard_grads[6],
        shard_grads[7],
        shard_grads[8],
    )


MESH = pl.DeviceIdType.MESH
BF = jnp.bfloat16
F32 = jnp.float32
VSPEC = pl.BlockSpec(memory_space=pltpu.VMEM)
GELU_IN = math.sqrt(2.0 / math.pi)


class Net:
    def __init__(self, send_sem, recv_sem, nz):
        self.send_sem, self.recv_sem = send_sem, recv_sem
        self.count = 0
        self.sent = []
        self.nz = nz
        self.x = lax.axis_index("dp")
        self.z = lax.axis_index("blk")
        self.u = lax.axis_index("uly")

    def send(self, src, dst, dev):
        k = self.count
        self.count += 1
        copy = pltpu.make_async_remote_copy(
            src_ref=src,
            dst_ref=dst,
            send_sem=self.send_sem.at[k],
            recv_sem=self.recv_sem.at[k],
            device_id=dev,
            device_id_type=MESH,
        )
        copy.start()
        self.sent.append(copy)
        return copy

    def plane(self, m):
        return (self.x, self.z, self.u ^ m)

    def other_x(self):
        return (1 - self.x, self.z, self.u)

    def zplus(self, d):
        return lax.rem(self.z + d, self.nz)

    def line(self, d):
        return (self.x, self.zplus(d), self.u)

    def hail(self):
        barrier = pltpu.get_barrier_semaphore()
        near = [self.plane(m) for m in (1, 2, 3)] + [self.other_x()]
        near += [self.line(d) for d in range(1, self.nz)]
        near += [(1 - self.x, self.z, self.u ^ m) for m in (1, 2, 3)]
        for dev in near:
            pl.semaphore_signal(barrier, inc=1, device_id=dev, device_id_type=MESH)
        self.met = len(near)

    def meet(self):
        pl.semaphore_wait(pltpu.get_barrier_semaphore(), self.met)

    def finish(self):
        for copy in self.sent:
            copy.wait_send()


class Line:
    def __init__(self, net, send_sem, recv_sem, base):
        self.net, self.send_sem, self.recv_sem, self.base = net, send_sem, recv_sem, base
        self.z = net.z
        self.inner = jnp.logical_and(net.z >= 1, net.z <= net.nz - 2)
        self.far = net.nz - 1 - net.z

    def copy(self, src, dst, k, target, recv=None):
        target = jnp.clip(target, 0, self.net.nz - 1)
        return pltpu.make_async_remote_copy(
            src_ref=src,
            dst_ref=dst,
            send_sem=self.send_sem.at[self.base + k],
            recv_sem=self.recv_sem.at[self.base + (k if recv is None else recv)],
            device_id=(self.net.x, target, self.net.u),
            device_id_type=MESH,
        )

    def target(self, d):
        return lax.rem(self.z + d, self.net.nz)

    def source(self, d):
        return lax.rem(self.z - d + self.net.nz, self.net.nz)


class Spread(Line):
    def __init__(self, net, send_sem, recv_sem, base, block):
        super().__init__(net, send_sem, recv_sem, base)
        self.block = block

    def direct(self, d):
        return self.copy(self.block(self.z), self.block(self.z), d, self.target(d))

    def start(self):
        for d in (2, 1, 3):
            if d == 2:
                self.direct(d).start()
            else:
                @pl.when(jnp.logical_or(self.inner, self.target(d) != self.far))
                def _():
                    self.direct(d).start()

    def relay_copy(self):
        block = self.block(self.source(2))
        target = jnp.where(self.z == 2, 3, 0)
        return self.copy(block, block, 4, target, jnp.where(self.z == 2, 3, 1))

    def across(self, d):
        block = self.block(self.source(d))
        return pltpu.make_async_remote_copy(
            src_ref=block, dst_ref=block, send_sem=self.send_sem.at[self.base + 4 + d],
            recv_sem=self.recv_sem.at[self.base + 4 + d], device_id=self.net.other_x(), device_id_type=MESH)

    def arrive(self, d):
        block = self.block(self.source(d))
        self.copy(block, block, d, self.z).wait_recv()

    def relay(self):
        self.arrive(2)

        @pl.when(self.inner)
        def _():
            self.relay_copy().start()

        self.across(2).start()

    def rest(self):
        first = jnp.where(self.z == 0, 3, 1)
        for d in (first, 4 - first):
            self.arrive(d)
            self.across(d).start()

    def finish_recv(self):
        for d in (2, 1, 3):
            self.across(d).wait_recv()

    def finish(self):
        self.direct(2).wait_send()
        for d in (1, 3):
            @pl.when(jnp.logical_or(self.inner, self.target(d) != self.far))
            def _():
                self.direct(d).wait_send()
        for d in (1, 2, 3):
            self.across(d).wait_send()

        @pl.when(self.inner)
        def _():
            self.relay_copy().wait_send()


class Collect(Line):
    def __init__(self, net, send_sem, recv_sem, base, theirs, ours, land_x, mine, land_z, relay):
        super().__init__(net, send_sem, recv_sem, base)
        self.theirs, self.ours = theirs, ours
        self.land_x, self.mine, self.land_z, self.relay = land_x, mine, land_z, relay

    def order(self, i):
        pick = lambda table: table[i]
        z = self.z
        return jnp.where(z == 0, 3 - i, jnp.where(z == 3, i, jnp.where(z == 1, pick((0, 2, 3, 1)), pick((3, 1, 0, 2)))))

    def across(self, i):
        zz = self.order(i)
        return pltpu.make_async_remote_copy(
            src_ref=self.theirs(zz), dst_ref=self.land_x.at[zz], send_sem=self.send_sem.at[self.base + 5 + i],
            recv_sem=self.recv_sem.at[self.base + 5 + i], device_id=self.net.other_x(), device_id_type=MESH)

    def start(self):
        for i in range(4):
            self.across(i).start()

    def own(self, i):
        zz = self.order(i)
        self.across(i).wait_recv()
        self.mine[zz] = (self.ours(zz) + self.land_x[zz].astype(F32)).astype(BF)

    def direct(self, zz):
        d = lax.rem(zz - self.z + 4, 4)
        return self.copy(self.mine.at[zz], self.land_z.at[d - 1], d, zz)

    def to_neighbour(self):
        return self.copy(self.mine.at[self.far], self.relay, 4, jnp.where(self.z == 0, 1, 2))

    def part(self, i):
        self.own(i)
        if i == 0:
            @pl.when(self.inner)
            def _():
                self.direct(self.order(0)).start()

            @pl.when(jnp.logical_not(self.inner))
            def _():
                self.to_neighbour().start()
        elif i == 1:
            self.direct(self.order(1)).start()
        elif i == 2:
            @pl.when(jnp.logical_not(self.inner))
            def _():
                self.direct(self.order(2)).start()

    def first(self):
        for i in range(4):
            self.part(i)

    def second(self):
        @pl.when(self.inner)
        def _():
            zz = self.order(2)
            self.copy(self.relay, self.relay, 4, self.z).wait_recv()
            self.mine[zz] = (self.mine[zz].astype(F32) + self.relay[...].astype(F32)).astype(BF)
            self.direct(zz).start()

    def total(self, final):
        skip = jnp.where(self.z == 0, 1, 3)
        final[...] = self.mine[self.z].astype(F32)
        for d in (1, 2, 3):
            @pl.when(jnp.logical_or(self.inner, skip != d))
            def _():
                self.copy(self.land_z.at[d - 1], self.land_z.at[d - 1], d, self.z).wait_recv()
                final[...] += self.land_z[d - 1].astype(F32)

    def finish(self):
        for i in range(4):
            self.across(i).wait_send()

        @pl.when(self.inner)
        def _():
            for i in range(3):
                self.direct(self.order(i)).wait_send()

        @pl.when(jnp.logical_not(self.inner))
        def _():
            self.to_neighbour().wait_send()
            for i in (1, 2):
                self.direct(self.order(i)).wait_send()


def rows_at(start, count):
    return pl.ds(pl.multiple_of(start, 16), count)


def dot_nn(a, b):
    return jnp.dot(a, b, preferred_element_type=F32)


def dot_nt(a, b):
    return lax.dot_general(a, b, (((1,), (1,)), ((), ())), preferred_element_type=F32)


def dot_tn(a, b):
    return lax.dot_general(a, b, (((0,), (0,)), ((), ())), preferred_element_type=F32)


def loop(count, body):
    def step(i, carry):
        body(i)
        return carry

    lax.fori_loop(0, count, step, 0)


def block_kernel(nz, refs):
    r = refs
    net = Net(r.send_sem, r.recv_sem, nz)
    x, z, u = net.x, net.z, net.u
    y, c = u // 2, lax.rem(u, 2)
    own48 = (4 * z + u) * 48
    tile = lambda t: rows_at(128 * t, 128)
    half_cols = lambda which: pl.ds(pl.multiple_of(384 * which, 128), 384)
    lane = lambda shape: lax.broadcasted_iota(jnp.int32, shape, 1)

    x_own, cot_own = r.x_all.at[tile(u)], r.cot_all.at[tile(u)]
    local = [
        pltpu.make_async_copy(r.qkv_in, r.qkv_raw, r.local_sem.at[0]),
        pltpu.make_async_copy(r.fc_in, r.fc_raw, r.local_sem.at[1]),
        pltpu.make_async_copy(r.x_in, x_own, r.local_sem.at[2]),
        pltpu.make_async_copy(r.out_in, r.w_out.at[rows_at(own48, 48)], r.local_sem.at[3]),
        pltpu.make_async_copy(r.proj_in, r.w_proj.at[rows_at(192 * z, 192)], r.local_sem.at[4]),
        pltpu.make_async_copy(r.cot_in, cot_own, r.local_sem.at[5]),
    ]
    local[0].start()
    local[2].start()
    net.hail()
    local[0].wait()
    for g in range(4):
        for t in range(3):
            r.qkv_pre[g, :, 128 * t:128 * t + 128] = r.qkv_raw[:, 768 * t + 192 * g:768 * t + 192 * g + 128]
        for at, t in ((384, 1), (448, 2), (512, 0)):
            r.qkv_pre[g, :, at:at + 64] = r.qkv_raw[:, 768 * t + 192 * g + 128:768 * t + 192 * g + 192]
    r.w_qkv[rows_at(own48, 48), :] = r.qkv_pre[u]
    net.meet()

    def plane_gather_start(own, full):
        return [net.send(own, full.at[tile(u)], net.plane(m)) for m in (2, 1)]

    def plane_gather_forward(sent, full):
        sent[0].wait_recv()
        sent.append(net.send(full.at[tile(u ^ 2)], full.at[tile(u ^ 2)], net.plane(1)))

    in_plane = lambda pre, full: [
        net.send(pre.at[u ^ m], full.at[rows_at(own48, 48)], net.plane(m)) for m in (1, 2, 3)
    ]
    block96 = lambda full: lambda j: full.at[rows_at(192 * j + 96 * x, 96)]
    spread = lambda base, block: Spread(net, r.sp_send, r.sp_recv, base, block)
    qkv_s = spread(0, block96(r.w_qkv))
    fc_s = spread(8, block96(r.w_fc))
    proj_s = spread(16, block96(r.w_proj))
    out_s = spread(24, lambda j: r.w_out.at[rows_at((4 * j + u) * 48, 48), half_cols(x)])
    qkv_p = in_plane(r.qkv_pre, r.w_qkv)
    local[2].wait()
    x_g = plane_gather_start(x_own, r.x_all)
    for i in (3, 1, 4, 5):
        local[i].start()
    vp = r.vec_f32
    vp[...] = jnp.zeros((16, 768), F32)
    vp[0:2, 0:48] = r.gains_in[...].astype(F32)
    vp[2:6, 0:48] = r.biases_in[...].astype(F32)
    vp[6:7, 0:48] = r.mid_in[...].astype(F32)
    vp[7:8, 0:48] = r.vb_in[...].astype(F32)
    bias = r.bias_f32
    bias[...] = jnp.zeros((8, 256), F32)
    bias[0:1, 0:48] = r.biases_in[1:2, :].astype(F32)
    bias[1:2, 0:48] = r.vb_in[...].astype(F32)
    bias[...] = pltpu.roll(bias[...], 48 * u, 1)
    vp[0:8, :] = pltpu.roll(vp[0:8, :], 48 * (4 * z + u), 1)
    vp[8:9, 0:192] = r.fcb_in[...].astype(F32)
    vp[9:10, 0:128] = bias[0:1, 0:128]
    vp[9:10, 256:384] = bias[1:2, 0:128]
    vp[9:10, 448:512] = bias[1:2, 128:192]
    vp[9:10, 512:576] = bias[0:1, 128:192]
    high = vp[8:16, :]
    row8 = lax.broadcasted_iota(jnp.int32, high.shape, 0)
    fcb_row = pltpu.roll(jnp.where(row8 == 0, high, 0.0), 192 * z, 1)
    bias_row = jnp.sum(jnp.where(row8 == 1, high, 0.0), 0, keepdims=True)
    vp[8:16, :] = fcb_row + jnp.where(row8 == 1 + z, bias_row, 0.0)
    r.vec_pre[...] = vp[...].astype(BF)
    vec_z = [net.send(r.vec_pre, r.vec_land_z.at[d - 1], net.line(d)) for d in range(1, nz)]
    for copy in qkv_p:
        copy.wait_recv()
    qkv_s.start()
    local[3].wait()
    out_s.start()
    total = r.vec_pre[...]
    for d in range(nz - 1):
        vec_z[d].wait_recv()
        total = total + r.vec_land_z[d]
    r.vec_u[...] = total
    vec_p = [net.send(r.vec_u, r.vec_land_p.at[m - 1], net.plane(m)) for m in (1, 2, 3)]
    plane_gather_forward(x_g, r.x_all)
    for i in (1, 4, 5):
        local[i].wait()
    for g in range(4):
        for zz in range(nz):
            r.fc_pre[g, :, 192 * zz:192 * zz + 192] = r.fc_raw[:, 768 * zz + 192 * g:768 * zz + 192 * g + 192]
    r.w_fc[rows_at(own48, 48), :] = r.fc_pre[u]
    inner64 = lax.broadcasted_iota(jnp.int32, (64, 1), 0)
    inner64_row = lax.broadcasted_iota(jnp.int32, (1, 64), 1)
    for i in range(8 * nz):
        first = r.order_in[0, i] * 64
        r.pos_col[64 * i:64 * i + 64, :] = first + inner64
        r.pos_row[:, 64 * i:64 * i + 64] = first + inner64_row
    fc_p = in_plane(r.fc_pre, r.w_fc)
    total = r.vec_u[...].astype(F32)
    row = lax.broadcasted_iota(jnp.int32, total.shape, 0)
    for m in range(3):
        vec_p[m].wait_recv()
        total = total + jnp.where(row == 8, 0.0, r.vec_land_p[m].astype(F32))
    r.vec[...] = total
    for copy in x_g[1:]:
        copy.wait_recv()
    gain = lambda i: r.vec[pl.ds(i, 1), :]

    def normalize(values):
        center = values - jnp.mean(values, -1, keepdims=True)
        inverse = lax.rsqrt(jnp.mean(center * center, -1, keepdims=True) + 1e-05)
        return center * inverse, inverse

    def ln_tile(t):
        normed, _ = normalize(r.x_all[tile(t), :].astype(F32))
        r.ln_all[tile(t), :] = (normed * gain(0) + gain(2)).astype(BF)

    loop(4, ln_tile)
    qkv_s.relay()
    qkv_s.rest()
    for copy in fc_p:
        copy.wait_recv()
    fc_s.start()
    cot_g = plane_gather_start(cot_own, r.cot_all)
    r.qm[2] = jnp.zeros((512, 128), BF)
    out_s.relay()
    out_s.rest()
    qkv_s.finish_recv()

    bias_u = jnp.sum(jnp.where(row == 9 + u, r.vec[...], 0.0), 0, keepdims=True)[:, 0:576]

    def qkv_tile(t):
        res = dot_nn(r.ln_all[tile(t), :], r.w_qkv[...]) + bias_u
        res = res.astype(BF)
        q01 = res[:, 0:128].astype(F32) * 0.125
        low = lane(q01.shape) < 64
        r.qm[0, tile(t), :] = jnp.where(low, q01, 0.0).astype(BF)
        r.qm[1, tile(t), :] = jnp.where(low, 0.0, q01).astype(BF)
        r.qm[2, tile(t), 0:64] = (res[:, 512:576].astype(F32) * 0.125).astype(BF)
        r.kv_all[z, tile(t), :] = res[:, 128:512]

    loop(4, qkv_tile)

    third = lambda ch: slice(128 * ch, 128 * ch + 128)

    def kv_copy(way, step, ch):
        block = z - step if way == 0 else z + step
        target = z + 1 if way == 0 else z - 1
        block, target = jnp.clip(block, 0, nz - 1), jnp.clip(target, 0, nz - 1)
        return pltpu.make_async_remote_copy(
            src_ref=r.kv_all.at[block, :, third(ch)], dst_ref=r.kv_all.at[block, :, third(ch)],
            send_sem=r.kv_send.at[(way * nz + step) * 3 + ch], recv_sem=r.kv_recv.at[(way * nz + step) * 3 + ch],
            device_id=(x, target, u), device_id_type=MESH)

    def kv_sends(way, step):
        if way == 0:
            return jnp.logical_and(z - step >= 0, z + 1 < nz)
        return jnp.logical_and(z + step < nz, z >= 1)

    def kv_start(step, ch, way):
        @pl.when(kv_sends(way, step))
        def _():
            kv_copy(way, step, ch).start()

    def attend(j):
        qp = r.pos_row[:, pl.ds(pl.multiple_of(512 * z, 128), 512)]
        for h in range(3):
            kc = 0 if h < 2 else 256
            vc = 128 if h < 2 else 256
            q = r.qm[h]

            def score(kt, top):
                s = dot_nt(r.kv_all[j, rows_at(128 * kt, 128), kc:kc + 128], q)
                kp = r.pos_col[pl.ds(pl.multiple_of(512 * j + 128 * kt, 128), 128), :]
                s = jnp.where(kp <= qp, s, -1e30)
                r.s_buf[rows_at(128 * kt, 128), :] = s
                return jnp.maximum(top, jnp.max(s, 0, keepdims=True))

            old = r.m_run[h]
            top = lax.fori_loop(0, 4, score, old, unroll=True)
            shrink = jnp.exp(old - top)

            def weigh(kt, got):
                p = jnp.exp(r.s_buf[rows_at(128 * kt, 128), :] - top)
                r.pt[j * 3 + h, rows_at(128 * kt, 128), :] = p.astype(BF)
                return got + jnp.sum(p, 0, keepdims=True)

            got = lax.fori_loop(0, 4, weigh, jnp.zeros((1, 512), F32), unroll=True)
            r.m_run[h] = top
            r.m_at[j * 3 + h] = top
            r.l_run[h] = r.l_run[h] * shrink + got
            r.o_t[h] = r.o_t[h] * shrink + dot_tn(r.kv_all[j, :, vc:vc + 128], r.pt[j * 3 + h])

    r.m_run[...] = jnp.full((3, 1, 512), -1e30, F32)
    r.l_run[...] = jnp.zeros((3, 1, 512), F32)
    r.o_t[...] = jnp.zeros((3, 128, 512), F32)
    for ch in range(3):
        for way in range(2):
            kv_start(0, ch, way)
    plane_gather_forward(cot_g, r.cot_all)
    attend(z)
    fc_s.relay()

    for step in range(1, nz):
        for ch in range(3):
            for way in range(2):
                @pl.when(z - step >= 0 if way == 0 else z + step < nz)
                def _():
                    kv_copy(way, step - 1, ch).wait_recv()

                if step < nz - 1:
                    kv_start(step, ch, way)
        if step == 1:
            fc_s.rest()
            out_s.finish_recv()
            out_rows = lambda zz, who: r.w_out.at[rows_at((4 * zz + who) * 48, 48)]
            out_y = [net.send(out_rows(zz, u), out_rows(zz, u), net.plane(2)) for zz in range(nz)]
            out_c = [net.send(out_rows(zz, u), out_rows(zz, u), net.plane(1)) for zz in range(nz)]
        if step == 2:
            for zz, copy in enumerate(out_y):
                copy.wait_recv()
                out_c.append(net.send(out_rows(zz, u ^ 2), out_rows(zz, u ^ 2), net.plane(1)))
        if step == nz - 1:
            proj_s.start()

        def either(way):
            j = jnp.where(way == 0, z - step, z + step)

            @pl.when(jnp.logical_and(j >= 0, j < nz))
            def _():
                attend(j)

        loop(2, either)

    rowi = lax.broadcasted_iota(jnp.int32, (128, 512), 0)
    r.l_inv[...] = 1.0 / r.l_run[...]
    r.att_t[0] = jnp.where(rowi < 64, r.o_t[0] * r.l_inv[0], r.o_t[1] * r.l_inv[1])
    r.att_t[1] = jnp.where(rowi < 64, 0.0, r.o_t[2] * r.l_inv[2])
    r.att[:, 0:128] = jnp.transpose(r.att_t[0]).astype(BF)
    r.att[:, 128:256] = jnp.transpose(r.att_t[1]).astype(BF)
    att_p = [net.send(r.att.at[tile(u ^ m)], r.merged.at[u], net.plane(m)) for m in (2, 3, 1)]
    r.merged[u] = r.att[tile(u), :]

    for copy in out_c:
        copy.wait_recv()
    for g in range(4):
        r.w_outp[256 * g:256 * g + 128, :] = r.w_out[192 * g:192 * g + 128, :]
        r.w_outp[256 * g + 128:256 * g + 192, :] = jnp.zeros((64, 768), BF)
        r.w_outp[256 * g + 192:256 * g + 256, :] = r.w_out[192 * g + 128:192 * g + 192, :]
    for copy in cot_g[1:]:
        copy.wait_recv()
    proj_s.relay()
    for copy in att_p:
        copy.wait_recv()
    resid = x_own[...].astype(F32) + gain(4)
    for g in range(4):
        resid = resid + dot_nn(r.merged[g], r.w_outp[256 * g:256 * g + 256, :])
    r.resid[...] = resid
    normed, inverse = normalize(resid)
    r.normed_mid[...] = normed
    r.inverse_mid[...] = inverse
    r.lm_all[tile(u), :] = (normed * gain(1) + gain(6)).astype(BF)
    lm_own = r.lm_all.at[tile(u)]
    lm_g = [net.send(lm_own, lm_own, net.plane(m)) for m in (2, 1)]
    fc_s.finish_recv()

    r.vec_g[...] = jnp.zeros((16, 768), F32)

    def mlp_front(t):
        rows = tile(t)
        pre = dot_nn(r.lm_all[rows, :], r.w_fc[...]) + gain(8)
        square = pre * pre
        th = jnp.tanh(GELU_IN * (pre * (1.0 + 0.044715 * square)))
        r.act[rows, :] = (0.5 * pre * (1.0 + th)).astype(BF)
        r.slope[rows, :] = 0.5 * (1.0 + th) + (0.5 * GELU_IN) * pre * (1.0 - th * th) * (1.0 + 0.134145 * square)

    def mlp_back(t):
        rows = tile(t)
        gp = (r.slope[rows, :] * dot_nt(r.cot_all[rows, :], r.w_proj[...])).astype(BF)
        r.grad_pre[rows, :] = gp
        r.fcb[...] += jnp.sum(gp.astype(F32), 0, keepdims=True)
        r.gm_part[t] = dot_nt(gp, r.w_fc[...]).astype(BF)

    r.fcb[...] = jnp.zeros((1, 768), F32)
    mlp_front(u)
    lm_g[1].wait_recv()
    mlp_front(u ^ 1)
    plane_gather_forward(lm_g, r.lm_all)

    def reduce_core(i, t, part, land_c):
        return net.send(part.at[t], land_c.at[i], net.plane(1))

    def reduce_y(copy, part, land_c, mid, land_y):
        copy.wait_recv()
        mid[...] = (part[u ^ 2].astype(F32) + land_c[0].astype(F32)).astype(BF)
        return net.send(mid, land_y, net.plane(2))

    def reduce_end(copy_c, copy_y, part, land_c, land_y):
        copy_c.wait_recv()
        copy_y.wait_recv()
        return part[u].astype(F32) + land_c[1].astype(F32) + land_y[...].astype(F32)

    mlp_front(u ^ 2)
    proj_s.rest()
    lm_g[2].wait_recv()
    mlp_front(u ^ 3)
    proj_s.finish_recv()
    mlp_back(u ^ 3)
    gm_c0 = reduce_core(0, u ^ 3, r.gm_part, r.gm_c)
    mlp_back(u ^ 1)
    gm_c1 = reduce_core(1, u ^ 1, r.gm_part, r.gm_c)
    mlp_back(u ^ 2)
    gm_y = reduce_y(gm_c0, r.gm_part, r.gm_c, r.gm_mid, r.gm_y)
    mlp_back(u)
    r.vec_g[...] += jnp.where(row == 10 + u, r.fcb[...], 0.0)

    def branch_tile(t):
        r.br_part[t] = dot_nn(r.act[tile(t), :], r.w_proj[...]).astype(BF)

    def weight_grad(a, b, out, tiles):
        def one(i):
            cols = pl.ds(pl.multiple_of(128 * i, 128), 128)
            out[tile(i), :] = dot_tn(a[:, cols], b[...]).astype(BF)

        loop(tiles, one)

    def collect(base, grad, land_x, mine, land_z, relay):
        return Collect(
            net, r.co_send, r.co_recv, base,
            lambda zz: grad.at[rows_at(192 * zz + 96 * (1 - x), 96)],
            lambda zz: grad[rows_at(192 * zz + 96 * x, 96), :].astype(F32),
            land_x, mine, land_z, relay)

    proj_c = collect(0, r.proj_g, r.proj_x, r.proj_m, r.proj_z, r.proj_r)
    fc_c = collect(9, r.fc_g, r.fc_x, r.fc_m, r.fc_z, r.fc_r)
    qkv_c = collect(18, r.qkv_g, r.qkv_x, r.qkv_m, r.qkv_z, r.qkv_r)

    weight_grad(r.act, r.cot_all, r.proj_g, 6)
    proj_c.start()
    branch_tile(u ^ 3)
    branch_tile(u ^ 1)
    br_c = [reduce_core(0, u ^ 3, r.br_part, r.br_c), reduce_core(1, u ^ 1, r.br_part, r.br_c)]
    branch_tile(u ^ 2)
    branch_tile(u)

    gm = reduce_end(gm_c1, gm_y, r.gm_part, r.gm_c, r.gm_y)
    normed = r.normed_mid[...]
    r.vec_g[1:2, :] = jnp.sum(gm * normed, 0, keepdims=True)
    r.vec_g[5:6, :] = jnp.sum(gm, 0, keepdims=True)

    def norm_grad(grad, normed, inverse, g):
        e = grad * g
        return inverse * (
            e - jnp.mean(e, -1, keepdims=True) - normed * jnp.mean(e * normed, -1, keepdims=True)
        )

    cot = cot_own[...].astype(F32)
    r.vec_g[4:5, :] = jnp.sum(cot, 0, keepdims=True)
    grad_resid = cot + norm_grad(gm, normed, r.inverse_mid[...], gain(1))
    r.grad_resid[...] = grad_resid
    gb = grad_resid.astype(BF)
    r.gb[...] = gb
    r.vec_g[3:4, :] = jnp.sum(gb.astype(F32), 0, keepdims=True)

    def gmer_tile(g):
        r.gmer[g] = dot_nt(r.gb[...], r.w_outp[pl.ds(pl.multiple_of(256 * g, 256), 256), :]).astype(BF)

    loop(4, gmer_tile)
    ga_p = [net.send(r.gmer.at[u ^ m], r.ga.at[tile(u)], net.plane(m)) for m in (2, 3, 1)]
    r.ga[tile(u), :] = r.gmer[u]
    weight_grad(r.lm_all, r.grad_pre, r.fc_g, 6)
    for g in range(4):
        res = dot_tn(r.merged[g], r.gb[...]).astype(BF)
        at = slice(48 * g, 48 * g + 48)
        r.out_g[0, 0, at, :] = res[0:48]
        r.out_g[1, 0, at, :] = res[48:96]
        r.out_g[0, 1, 48 * g:48 * g + 32, :] = res[96:128]
        r.out_g[0, 1, 48 * g + 32:48 * g + 48, :] = res[192:208]
        r.out_g[1, 1, at, :] = res[208:256]
    og_c = net.send(r.out_g.at[1 - c], r.og_c, net.plane(1))
    proj_c.part(0)
    proj_c.part(1)
    early_p = [net.send(r.vec_g, r.vg_p.at[m - 1], net.plane(m)) for m in (1, 2, 3)]
    for copy in ga_p:
        copy.wait_recv()

    low = lane((512, 128)) < 64
    ga01 = r.ga[:, 0:128]
    zero = jnp.zeros((512, 128), BF)
    r.gam[0] = jnp.where(low, ga01.astype(F32), 0.0).astype(BF)
    r.gam[1] = jnp.where(low, 0.0, ga01.astype(F32)).astype(BF)
    r.gam[2] = r.ga[:, 128:256]
    prod = jnp.transpose(ga01.astype(F32)) * r.att_t[0]
    r.delta[0] = jnp.sum(prod[0:64], 0, keepdims=True)
    r.delta[1] = jnp.sum(prod[64:128], 0, keepdims=True)
    prod = jnp.transpose(r.ga[:, 128:256].astype(F32)) * r.att_t[1]
    r.delta[2] = jnp.sum(prod, 0, keepdims=True)
    r.dq_t[...] = jnp.zeros((3, 128, 512), F32)

    def back(j):
        factor = [jnp.exp(r.m_at[j * 3 + h] - r.m_run[h]) * r.l_inv[h] for h in range(3)]

        def keys(kt):
            rows = rows_at(128 * kt, 128)
            for h in range(3):
                vc = 128 if h < 2 else 256
                p = r.pt[j * 3 + h, rows, :].astype(F32) * factor[h]
                dp = dot_nt(r.kv_all[j, rows, vc:vc + 128], r.gam[h])
                r.ds[h, rows, :] = (p * (dp - r.delta[h])).astype(BF)
                r.pt[j * 3 + h, rows, :] = p.astype(BF)

        def sums(kt):
            rows = rows_at(128 * kt, 128)
            pair = lambda of, first, second: dot_nn(of(0), first) + dot_nn(of(1), second)
            ds = lambda h: r.ds[h, rows, :]
            p = lambda h: r.pt[j * 3 + h, rows, :]
            r.dkv[rows, 0:128] = pair(ds, r.qm[0], r.qm[1])
            r.dkv[rows, 128:256] = pair(p, r.gam[0], r.gam[1])
            r.dkv[rows, 256:384] = dot_nn(ds(2), r.qm[2]) + dot_nn(p(2), r.gam[2])

        loop(4, keys)
        loop(4, sums)
        for h in range(3):
            kc = 0 if h < 2 else 256
            r.dq_t[h] += dot_tn(r.kv_all[j, :, kc:kc + 128], r.ds[h])

    def chain_copy(way, step, ch):
        target = jnp.clip(jnp.where(way == 0, z - 1, z + 1), 0, nz - 1)
        at = way * (nz - 1) + step - 1
        return pltpu.make_async_remote_copy(
            src_ref=r.chain.at[at, :, third(ch)], dst_ref=r.chain_land.at[at, :, third(ch)],
            send_sem=r.ch_send.at[at * 3 + ch], recv_sem=r.ch_recv.at[at * 3 + ch],
            device_id=(x, target, u), device_id_type=MESH)

    def chain_step(step):
        def either(way):
            j = jnp.where(way == 0, z - step, z + step)
            behind = jnp.where(way == 0, z + 1, z - 1)

            @pl.when(jnp.logical_and(j >= 0, j < nz))
            def _():
                back(j)
                at = way * (nz - 1) + step - 1
                comes = jnp.logical_and(behind >= 0, behind < nz)
                for ch in range(3):
                    at_ch = third(ch)
                    if step < nz - 1:
                        @pl.when(comes)
                        def _():
                            chain_copy(way, step + 1, ch).wait_recv()
                            r.chain[at, :, at_ch] = (r.dkv[:, at_ch] + r.chain_land[at + 1, :, at_ch].astype(F32)).astype(BF)

                        @pl.when(jnp.logical_not(comes))
                        def _():
                            r.chain[at, :, at_ch] = r.dkv[:, at_ch].astype(BF)
                    else:
                        r.chain[at, :, at_ch] = r.dkv[:, at_ch].astype(BF)
                    chain_copy(way, step, ch).start()

        loop(2, either)

    for step in range(nz - 1, 0, -1):
        chain_step(step)
        if step == nz - 1:
            proj_c.part(2)
            proj_c.part(3)
            fc_c.start()
            total = r.vec_g[...]
            for m in range(3):
                early_p[m].wait_recv()
                total = total + r.vg_p[m]
            r.vg_1[...] = total
            early_z = [net.send(r.vg_1, r.vg_z.at[d - 1], net.line(d)) for d in range(1, nz)]
            br_y = reduce_y(br_c[0], r.br_part, r.br_c, r.br_mid, r.br_y)
            og_c.wait_recv()
            r.og_1[...] = (r.out_g[c].astype(F32) + r.og_c[...].astype(F32)).astype(BF)
            og_y = net.send(r.og_1.at[1 - y], r.og_y, net.plane(2))
        if step == nz - 2:
            proj_c.second()
            r.output[...] = (
                r.resid[...] + gain(5) + reduce_end(br_c[1], br_y, r.br_part, r.br_c, r.br_y)
            ).astype(BF)
            total = r.vg_1[...]
            for d in range(nz - 1):
                early_z[d].wait_recv()
                total = total + r.vg_z[d]
            r.vg_2[...] = total
            early_x = net.send(r.vg_2, r.vg_x, net.other_x())
            fc_c.part(0)
            fc_c.part(1)
            og_y.wait_recv()
            r.og_2[...] = (r.og_1[y].astype(F32) + r.og_y[...].astype(F32)).astype(BF)
            og_x = net.send(r.og_2.at[:, half_cols(1 - x)], r.og_x, net.other_x())
        if step == 1:
            og_x.wait_recv()
            r.og_3[...] = (r.og_2[:, half_cols(x)].astype(F32) + r.og_x[...].astype(F32)).astype(BF)
            og_z = [
                net.send(r.og_3.at[rows_at(48 * net.zplus(d), 48)], r.og_z.at[d - 1], net.line(d))
                for d in range(1, nz)
            ]
            fc_c.part(2)
            fc_c.part(3)
    back(z)

    fc_c.second()
    for ch in range(3):
        @pl.when(z + 1 < nz)
        def _():
            chain_copy(0, 1, ch).wait_recv()
            r.dkv[:, third(ch)] += r.chain_land[0, :, third(ch)].astype(F32)

        @pl.when(z >= 1)
        def _():
            chain_copy(1, 1, ch).wait_recv()
            r.dkv[:, third(ch)] += r.chain_land[nz - 1, :, third(ch)].astype(F32)

    r.gqkv[:, 128:512] = r.dkv[...].astype(BF)
    dq = jnp.transpose(jnp.where(rowi < 64, r.dq_t[0], r.dq_t[1]) * 0.125)
    r.gqkv[:, 0:128] = dq.astype(BF)
    r.gqkv[:, 512:576] = jnp.transpose(r.dq_t[2] * 0.125)[:, 0:64].astype(BF)


    def gin_tile(t):
        r.gi_part[t] = dot_nt(r.gqkv[tile(t), :], r.w_qkv[...]).astype(BF)

    gin_tile(u ^ 3)
    gi_c0 = reduce_core(0, u ^ 3, r.gi_part, r.gi_c)
    gin_tile(u ^ 1)
    gi_c1 = reduce_core(1, u ^ 1, r.gi_part, r.gi_c)
    weight_grad(r.ln_all, r.gqkv, r.qkv_g, 6)
    qkv_c.start()
    gin_tile(u ^ 2)
    gi_y = reduce_y(gi_c0, r.gi_part, r.gi_c, r.gi_mid, r.gi_y)
    gin_tile(u)
    r.late[...] = jnp.zeros((8, 768), F32)
    row_l = row[0:8]
    r.late[:, 0:576] = jnp.where(row_l[:, 0:576] == 2 + u, jnp.sum(r.gqkv[...].astype(F32), 0, keepdims=True), 0.0)
    qkv_c.first()
    proj_c.total(r.acc)
    r.proj_f[...] = r.acc[...].astype(BF)
    mine = rows_at(96 * x, 96)
    r.proj_o[mine, :] = r.proj_f[...]
    proj_last = net.send(r.proj_f, r.proj_o.at[mine], net.other_x())

    finals = []

    def hand_out(base, final, native):
        for xx in range(2):
            for cc in range(2):
                target_x = x ^ xx
                target_u = 2 * x + cc
                here = jnp.logical_and(xx == 0, target_u == u)
                k = base + 2 * xx + cc
                copy = pltpu.make_async_remote_copy(
                    src_ref=final.at[pl.ds(48 * cc, 48)], dst_ref=native.at[u], send_sem=r.f_send.at[k],
                    recv_sem=r.f_recv.at[base + u], device_id=(target_x, z, target_u), device_id_type=MESH)

                @pl.when(jnp.logical_not(here))
                def _():
                    copy.start()

                @pl.when(here)
                def _():
                    native[u] = final[pl.ds(48 * cc, 48), :]

                finals.append((here, copy))

    def await_native(base, final, native):
        for who in range(4):
            copy = pltpu.make_async_remote_copy(
                src_ref=final.at[pl.ds(0, 48)], dst_ref=native.at[who], send_sem=r.f_send.at[base],
                recv_sem=r.f_recv.at[base + who], device_id=(1 - x, z, u), device_id_type=MESH)

            @pl.when(jnp.logical_not(jnp.logical_and(x == y, u == who)))
            def _():
                copy.wait_recv()

    gin = reduce_end(gi_c1, gi_y, r.gi_part, r.gi_c, r.gi_y)
    normed, inverse = normalize(x_own[...].astype(F32))
    r.late[0:1, :] = jnp.sum(gin * normed, 0, keepdims=True)
    r.late[1:2, :] = jnp.sum(gin, 0, keepdims=True)
    late_p = [net.send(r.late, r.late_p.at[m - 1], net.plane(m)) for m in (2, 3, 1)]
    late_p += [net.send(r.late, r.late_p.at[3 + m], (1 - x, z, u ^ m)) for m in range(4)]
    r.input_grad[...] = (r.grad_resid[...] + norm_grad(gin, normed, inverse, gain(0))).astype(BF)
    qkv_c.second()
    fc_c.total(r.acc)
    r.fc_f[...] = r.acc[...].astype(BF)
    hand_out(0, r.fc_f, r.fc_o)
    total = r.late[...]
    for copy in late_p:
        copy.wait_recv()
    for m in range(7):
        total = total + r.late_p[m]
    r.late_1[...] = total
    late_z = [net.send(r.late_1, r.late_z.at[d - 1], net.line(d)) for d in range(1, nz)]
    total = r.og_3[rows_at(48 * z, 48), :].astype(F32)
    for d in range(nz - 1):
        og_z[d].wait_recv()
        total = total + r.og_z[d].astype(F32)
    r.out_o[:, half_cols(x)] = total.astype(BF)
    og_last = net.send(r.out_o.at[:, half_cols(x)], r.out_o.at[:, half_cols(x)], net.other_x())
    qkv_c.total(r.acc_q)
    r.qkv_f[...] = r.acc_q[...].astype(BF)
    hand_out(4, r.qkv_f, r.qkv_o)
    early_x.wait_recv()
    early = r.vg_2[...] + r.vg_x[...]
    late = r.late_1[...]
    for d in range(nz - 1):
        late_z[d].wait_recv()
        late = late + r.late_z[d]
    heads = jnp.sum(jnp.where(row_l == 2 + z, late, 0.0), 0, keepdims=True)
    hidden = jnp.sum(jnp.where(row == 10 + u, early, 0.0), 0, keepdims=True)
    total = early[0:8] + jnp.where(row_l == 0, late, 0.0) + jnp.where(row_l == 2, late[1:2], 0.0)
    bias[0:1, 0:128] = heads[:, 0:128]
    bias[0:1, 128:192] = heads[:, 512:576]
    bias[1:2, 0:128] = heads[:, 256:384]
    bias[1:2, 128:192] = heads[:, 448:512]
    mine8 = pltpu.roll(total, 768 - 48 * (4 * z + u), 1)
    vp[0:8, :] = mine8
    both = pltpu.roll(bias[...], 256 - 48 * u, 1)
    vp[6:8, 0:256] = both[0:2]
    vp[8:16, :] = pltpu.roll(jnp.broadcast_to(hidden, (8, 768)), 768 - 192 * z, 1)
    r.vec_o[...] = vp[...]
    proj_last.wait_recv()
    og_last.wait_recv()
    await_native(0, r.fc_f, r.fc_o)
    await_native(4, r.qkv_f, r.qkv_o)

    for here, copy in finals:
        @pl.when(jnp.logical_not(here))
        def _():
            copy.wait_send()
    for step in range(nz - 1):
        for way in range(2):
            @pl.when(kv_sends(way, step))
            def _():
                for ch in range(3):
                    kv_copy(way, step, ch).wait_send()
    for step in range(1, nz):
        for way in range(2):
            @pl.when(z - step >= 0 if way == 0 else z + step < nz)
            def _():
                for ch in range(3):
                    chain_copy(way, step, ch).wait_send()
    for part in (qkv_s, fc_s, proj_s, out_s, proj_c, fc_c, qkv_c):
        part.finish()
    net.finish()


def block_call(nz, **operands):
    def vm(*shape, kind=BF):
        return pltpu.VMEM(shape, kind)

    outs = dict(
        output=((128, 768), BF), input_grad=((128, 768), BF), qkv_o=((4, 48, 576), BF),
        fc_o=((4, 48, 768), BF), proj_o=((192, 768), BF), out_o=((48, 768), BF), vec_o=((16, 768), F32),
    )
    f = lambda *shape: vm(*shape, kind=F32)
    keys = 512 * nz
    scratch = dict(
        qkv_raw=vm(48, 2304), fc_raw=vm(48, 3072), qkv_pre=vm(4, 48, 576), fc_pre=vm(4, 48, 768),
        vec_f32=f(16, 768), bias_f32=f(8, 256), vec_pre=vm(16, 768),
        pos_row=pltpu.VMEM((1, keys), jnp.int32), pos_col=pltpu.VMEM((keys, 1), jnp.int32),
        w_qkv=vm(768, 576), w_fc=vm(768, 768), w_proj=vm(768, 768), w_out=vm(768, 768), w_outp=vm(1024, 768),
        vec_land_z=vm(nz - 1, 16, 768), vec_u=vm(16, 768), vec_land_p=vm(3, 16, 768), vec=f(16, 768),
        x_all=vm(512, 768), cot_all=vm(512, 768), ln_all=vm(512, 768), lm_all=vm(512, 768),
        qm=vm(3, 512, 128), kv_all=vm(nz, 512, 384), s_buf=f(512, 512), pt=vm(nz * 3, 512, 512),
        m_run=f(3, 1, 512), l_run=f(3, 1, 512), l_inv=f(3, 1, 512), m_at=f(nz * 3, 1, 512), o_t=f(3, 128, 512),
        att_t=f(2, 128, 512), att=vm(512, 256), merged=vm(4, 128, 256),
        resid=f(128, 768), normed_mid=f(128, 768), inverse_mid=f(128, 1), slope=f(512, 768),
        act=vm(512, 768), grad_pre=vm(512, 768), fcb=f(1, 768), vec_g=f(16, 768),
        gm_part=vm(4, 128, 768), gm_c=vm(2, 128, 768), gm_mid=vm(128, 768), gm_y=vm(128, 768),
        br_part=vm(4, 128, 768), br_c=vm(2, 128, 768), br_mid=vm(128, 768), br_y=vm(128, 768),
        gi_part=vm(4, 128, 768), gi_c=vm(2, 128, 768), gi_mid=vm(128, 768), gi_y=vm(128, 768),
        grad_resid=f(128, 768), gb=vm(128, 768), gmer=vm(4, 128, 256), ga=vm(512, 256), gam=vm(3, 512, 128),
        delta=f(3, 1, 512), ds=vm(3, 512, 512), dq_t=f(3, 128, 512), dkv=f(512, 384),
        chain=vm(2 * (nz - 1), 512, 384), chain_land=vm(2 * (nz - 1), 512, 384), gqkv=vm(512, 576),
        qkv_g=vm(768, 576), fc_g=vm(768, 768), proj_g=vm(768, 768), out_g=vm(2, 2, 192, 768),
        qkv_x=vm(nz, 96, 576), fc_x=vm(nz, 96, 768), proj_x=vm(nz, 96, 768),
        qkv_m=vm(nz, 96, 576), fc_m=vm(nz, 96, 768), proj_m=vm(nz, 96, 768),
        qkv_z=vm(nz - 1, 96, 576), fc_z=vm(nz - 1, 96, 768), proj_z=vm(nz - 1, 96, 768),
        qkv_r=vm(96, 576), fc_r=vm(96, 768), proj_r=vm(96, 768), acc=f(96, 768), acc_q=f(96, 576),
        qkv_f=vm(96, 576), fc_f=vm(96, 768), proj_f=vm(96, 768),
        og_c=vm(2, 192, 768), og_1=vm(2, 192, 768), og_y=vm(192, 768), og_2=vm(192, 768),
        og_x=vm(192, 384), og_3=vm(192, 384), og_z=vm(nz - 1, 48, 384),
        late=f(8, 768), late_p=f(7, 8, 768), late_1=f(8, 768), late_z=f(nz - 1, 8, 768),
        vg_p=f(3, 16, 768), vg_1=f(16, 768), vg_z=f(nz - 1, 16, 768), vg_2=f(16, 768), vg_x=f(16, 768),
        send_sem=pltpu.SemaphoreType.DMA((112,)), recv_sem=pltpu.SemaphoreType.DMA((112,)),
        sp_send=pltpu.SemaphoreType.DMA((32,)), sp_recv=pltpu.SemaphoreType.DMA((32,)),
        co_send=pltpu.SemaphoreType.DMA((27,)), co_recv=pltpu.SemaphoreType.DMA((27,)),
        local_sem=pltpu.SemaphoreType.DMA((6,)),
        kv_send=pltpu.SemaphoreType.DMA((6 * nz,)), kv_recv=pltpu.SemaphoreType.DMA((6 * nz,)),
        ch_send=pltpu.SemaphoreType.DMA((6 * nz,)), ch_recv=pltpu.SemaphoreType.DMA((6 * nz,)),
        f_send=pltpu.SemaphoreType.DMA((8,)), f_recv=pltpu.SemaphoreType.DMA((8,)),
    )
    names = [*operands, *outs, *scratch]
    places = {name: pl.BlockSpec(memory_space=pl.ANY) for name in ("x_in", "cot_in", "qkv_in", "fc_in", "out_in", "proj_in")}
    places["order_in"] = pl.BlockSpec(memory_space=pltpu.SMEM)

    def kernel(*refs):
        block_kernel(nz, types.SimpleNamespace(**dict(zip(names, refs, strict=True))))

    got = pl.pallas_call(
        kernel,
        out_shape=tuple(jax.ShapeDtypeStruct(*s) for s in outs.values()),
        in_specs=[places.get(name, VSPEC) for name in operands],
        out_specs=(VSPEC,) * len(outs),
        scratch_shapes=list(scratch.values()),
        compiler_params=pltpu.CompilerParams(
            collective_id=0, has_side_effects=True, vmem_limit_bytes=60 * 2**20
        ),
        name="transformer_block",
    )(*operands.values())
    return dict(zip(outs, got, strict=True))


def hand_over_kernel(nz, output, input_grad, qkv_o, fc_o, proj_o, out_o, vec_o,
                     output_f, input_grad_f, gains_f, biases_f, mid_f, vb_f, qkv_f, out_f, fc_f, fcb_f, proj_f):
    output_f[...] = output[...]
    input_grad_f[...] = input_grad[...]
    gains_f[...] = vec_o[0:2, 0:48]
    biases_f[0:1, :] = vec_o[2:3, 0:48]
    biases_f[1:2, :] = vec_o[6:7, 0:48]
    biases_f[2:4, :] = vec_o[3:5, 0:48]
    mid_f[...] = vec_o[5:6, 0:48]
    vb_f[...] = vec_o[7:8, 0:48]
    fcb_f[...] = vec_o[8:9, 0:192]
    out_f[...] = out_o[...].astype(F32)
    proj_f[...] = proj_o[...].astype(F32)
    for g in range(4):
        for t in range(3):
            qkv_f[:, 768 * t + 192 * g:768 * t + 192 * g + 128] = qkv_o[g, :, 128 * t:128 * t + 128].astype(F32)
        for at, t in ((384, 1), (448, 2), (512, 0)):
            qkv_f[:, 768 * t + 192 * g + 128:768 * t + 192 * g + 192] = qkv_o[g, :, at:at + 64].astype(F32)
        for zz in range(nz):
            fc_f[:, 768 * zz + 192 * g:768 * zz + 192 * g + 192] = fc_o[g, :, 192 * zz:192 * zz + 192].astype(F32)


def hand_over(nz, got):
    shapes = [((128, 768), BF), ((128, 768), BF), ((2, 48), F32), ((4, 48), F32), ((1, 48), F32), ((1, 48), F32),
              ((48, 2304), F32), ((48, 768), F32), ((48, 3072), F32), ((1, 192), F32), ((192, 768), F32)]
    return pl.pallas_call(
        functools.partial(hand_over_kernel, nz),
        out_shape=tuple(jax.ShapeDtypeStruct(*s) for s in shapes),
        in_specs=[VSPEC] * len(got),
        out_specs=(VSPEC,) * len(shapes),
        compiler_params=pltpu.CompilerParams(vmem_limit_bytes=60 * 2**20),
        name="hand_over",
    )(*got.values())


def device_fast(nz, inputs, stretch_order, norm_gains, biases, mid_shift, value_bias, qkv_weight, out_weight, fc_weight, fc_bias, proj_weight, cotangent):
    got = block_call(
        nz,
        x_in=inputs[0],
        cot_in=cotangent[0],
        qkv_in=qkv_weight,
        fc_in=fc_weight,
        out_in=out_weight,
        proj_in=proj_weight,
        gains_in=norm_gains,
        biases_in=biases,
        mid_in=mid_shift[None],
        vb_in=value_bias[None],
        fcb_in=fc_bias[None],
        order_in=stretch_order,
    )
    output, input_grad, gains, rows, mid, vb, qkv, out, fc, fcb, proj = hand_over(nz, got)
    return output[None], input_grad[None], gains, rows, mid[0], vb[0], qkv, out, fc, fcb[0], proj


def solution(mesh):
    placed = (
        P("dp", ("blk", "uly"), None),
        P("dp", None),
        P(None, ("blk", "uly")),
        P(None, ("blk", "uly")),
        P(("blk", "uly")),
        P(("blk", "uly")),
        P(("blk", "uly"), None),
        P(("blk", "uly"), None),
        P(("blk", "uly"), None),
        P(("blk", "uly")),
        P(("blk", "uly"), None),
        P("dp", ("blk", "uly"), None),
    )
    sizes = dict(mesh.shape)
    nz = sizes["blk"]
    fast = sizes["uly"] == 4 and sizes["dp"] == 2 and nz == 4
    chosen = functools.partial(device_fast, nz) if fast else per_device
    return jax.shard_map(
        chosen,
        mesh=mesh,
        in_specs=placed,
        out_specs=(
            P("dp", ("blk", "uly"), None),
            P("dp", ("blk", "uly"), None),
            P(None, ("blk", "uly")),
            P(None, ("blk", "uly")),
            P(("blk", "uly")),
            P(("blk", "uly")),
            P(("blk", "uly"), None),
            P(("blk", "uly"), None),
            P(("blk", "uly"), None),
            P(("blk", "uly")),
            P(("blk", "uly"), None),
        ),
        check_vma=False,
    )
```

```python
import functools
import math
import types

import jax
import jax.numpy as jnp
from jax import lax
from jax.experimental import pallas as pl
from jax.experimental.pallas import tpu as pltpu
from jax.sharding import PartitionSpec as P

HEADS = 12


masked_score = -1e30


def layer_norm(values, gain, shift):
    center = values - jnp.mean(values, -1, keepdims=True)
    inverse = lax.rsqrt(jnp.mean(center * center, -1, keepdims=True) + 1e-05)
    normed = center * inverse
    return (normed * gain + shift, normed, inverse)


def norm_back(grad_out, normed, inverse, gain):
    scaled = grad_out * gain
    mean_plain = jnp.mean(scaled, -1, keepdims=True)
    mean_mixed = jnp.mean(scaled * normed, -1, keepdims=True)
    return inverse * (scaled - mean_plain - normed * mean_mixed)


def sweep(step_fn, carried, parts):
    row_count = parts[0].shape[1]
    sweep_rows = math.gcd(row_count, 1024)

    def turn(inner, turn_number):
        offset = turn_number * sweep_rows
        blocks = tuple((lax.dynamic_slice_in_dim(part, offset, sweep_rows, 1) for part in parts))
        return (step_fn(inner, blocks, offset), None)

    result, _ = lax.scan(turn, carried, jnp.arange(row_count // sweep_rows, dtype=jnp.int32))
    return result


def per_device(
    inputs,
    stretch_order,
    norm_gains,
    biases,
    mid_shift,
    value_bias,
    qkv_weight,
    out_weight,
    fc_weight,
    fc_bias,
    proj_weight,
    cotangent,
):
    fp32 = jnp.float32
    bf16 = jnp.bfloat16
    gain_rows, shifts, mid_gathered, value_shift, w_qkv, w_out, w_fc, b_fc, w_proj = (
        lax.all_gather(norm_gains, ("blk", "uly"), axis=1, tiled=True),
        lax.all_gather(biases, ("blk", "uly"), axis=1, tiled=True),
        lax.all_gather(mid_shift, ("blk", "uly"), axis=0, tiled=True),
        lax.all_gather(value_bias, ("blk", "uly"), axis=0, tiled=True),
        lax.all_gather(qkv_weight, ("blk", "uly"), axis=0, tiled=True),
        lax.all_gather(out_weight, ("blk", "uly"), axis=0, tiled=True),
        lax.all_gather(fc_weight, ("blk", "uly"), axis=0, tiled=True),
        lax.all_gather(fc_bias, ("blk", "uly"), axis=0, tiled=True),
        lax.all_gather(proj_weight, ("blk", "uly"), axis=0, tiled=True),
    )
    gain_rows = gain_rows.astype(fp32)
    shifts = shifts.astype(fp32)
    mid_gathered = mid_gathered.astype(fp32)
    seq_count, row_len, width = inputs.shape
    uly_count = lax.axis_size("uly")
    local_heads = HEADS // uly_count
    head_dim = width // HEADS
    head_span = local_heads * head_dim
    block_rows = uly_count * row_len
    half_rows = row_len // 2
    seq_len = stretch_order.shape[1] * half_rows
    score_scale = head_dim ** (-0.5)
    tokens = inputs.astype(fp32).reshape(seq_count * row_len, width)
    ln_in, normed_in, inverse_in = layer_norm(tokens, gain_rows[0], shifts[0])
    ln_in = ln_in.astype(bf16)
    qkv_shift = jnp.concatenate([shifts[1], jnp.zeros((width,), fp32), value_shift.astype(fp32)])
    qkv = (jnp.dot(ln_in, w_qkv, preferred_element_type=fp32) + qkv_shift).astype(bf16)
    head_data = lax.all_to_all(
        qkv.reshape(seq_count, row_len, 3, uly_count, head_span),
        "uly",
        split_axis=3,
        concat_axis=1,
        tiled=True,
    )
    queries = head_data[:, :, 0, 0].reshape(seq_count, block_rows, local_heads, head_dim)
    key_rows = head_data[:, :, 1, 0]
    value_rows = head_data[:, :, 2, 0]
    positions = (
        stretch_order[:, :, None] * half_rows
        + jnp.arange(half_rows, dtype=jnp.int32)[None, None, :]
    ).reshape(seq_count, seq_len)
    query_pos = lax.dynamic_slice_in_dim(
        positions, lax.axis_index("blk") * block_rows, block_rows, 1
    )

    def score_block(key_part, key_start):
        part_rows = key_part.shape[1]
        key_pos = lax.dynamic_slice_in_dim(positions, key_start, part_rows, 1)
        scores = (
            jnp.einsum(
                "sqhd,skhd->shqk",
                queries,
                key_part.reshape(seq_count, part_rows, local_heads, head_dim),
                preferred_element_type=fp32,
            )
            * score_scale
        )
        causal = query_pos[:, None, :, None] >= key_pos[:, None, None, :]
        return (scores, causal)

    def stats_step(carried, blocks, key_start):
        row_max, row_total = carried
        scores, causal = score_block(blocks[0], key_start)
        new_max = jnp.maximum(row_max, jnp.max(jnp.where(causal, scores, masked_score), -1))
        row_total = row_total * jnp.exp(row_max - new_max) + jnp.sum(
            jnp.where(causal, jnp.exp(scores - new_max[..., None]), 0.0), -1
        )
        return (new_max, row_total)

    def softmax_of(scores, causal, row_max, row_total):
        return jnp.where(causal, jnp.exp(scores - row_max[..., None]) / row_total[..., None], 0.0)

    def make_output_step(row_max, row_total):

        def output_step(acc_out, blocks, key_start):
            scores, causal = score_block(blocks[0], key_start)
            attn_probs = softmax_of(scores, causal, row_max, row_total).astype(bf16)
            part_rows = blocks[1].shape[1]
            value_part = blocks[1].reshape(seq_count, part_rows, local_heads, head_dim)
            return acc_out + jnp.einsum(
                "shqk,skhd->sqhd", attn_probs, value_part, preferred_element_type=fp32
            )

        return output_step

    stats_init = (
        jnp.full((seq_count, local_heads, block_rows), masked_score, fp32),
        jnp.zeros((seq_count, local_heads, block_rows), fp32),
    )
    empty_out = jnp.zeros((seq_count, block_rows, local_heads, head_dim), fp32)
    all_keys, all_values = (
        lax.all_gather(key_rows, "blk", axis=1, tiled=True),
        lax.all_gather(value_rows, "blk", axis=1, tiled=True),
    )
    row_max, row_total = sweep(stats_step, stats_init, (all_keys,))
    attended = sweep(make_output_step(row_max, row_total), empty_out, (all_keys, all_values))
    attended_low = attended.astype(bf16).reshape(seq_count, block_rows, 1, head_span)
    merged = lax.all_to_all(attended_low, "uly", split_axis=1, concat_axis=2, tiled=True).reshape(
        seq_count * row_len, width
    )
    resid = tokens + (jnp.dot(merged, w_out, preferred_element_type=fp32) + shifts[2])
    ln_mid, normed_mid, inverse_mid = layer_norm(resid, gain_rows[1], mid_gathered)
    ln_mid = ln_mid.astype(bf16)
    pre_act = jnp.dot(ln_mid, w_fc, preferred_element_type=fp32) + b_fc.astype(fp32)

    def gelu_piece(pre_values):
        return jax.nn.gelu(pre_values, approximate=True)

    act, gelu_back = jax.vjp(gelu_piece, pre_act)
    act = act.astype(bf16)
    result = resid + (jnp.dot(act, w_proj, preferred_element_type=fp32) + shifts[3])
    grad_low = cotangent.reshape(seq_count * row_len, width)
    grad_out = grad_low.astype(fp32)
    proj_grad = jnp.einsum("ta,tb->ab", act, grad_low, preferred_element_type=fp32)
    proj_shift_grad = jnp.sum(grad_out, 0)
    grad_act = jnp.einsum("tb,ab->ta", grad_low, w_proj, preferred_element_type=fp32)
    grad_pre = gelu_back(grad_act)[0].astype(bf16)
    fc_grad = jnp.einsum("ta,tb->ab", ln_mid, grad_pre, preferred_element_type=fp32)
    fc_shift_grad = jnp.sum(grad_pre.astype(fp32), 0)
    grad_mid = jnp.einsum("tb,ab->ta", grad_pre, w_fc, preferred_element_type=fp32)
    gain_mid_grad = jnp.sum(grad_mid * normed_mid, 0)
    shift_mid_grad = jnp.sum(grad_mid, 0)
    grad_resid = grad_out + norm_back(grad_mid, normed_mid, inverse_mid, gain_rows[1])
    grad_branch = grad_resid.astype(bf16)
    out_grad = jnp.einsum("ta,tb->ab", merged, grad_branch, preferred_element_type=fp32)
    out_shift_grad = jnp.sum(grad_branch.astype(fp32), 0)
    grad_merged = jnp.einsum("tb,ab->ta", grad_branch, w_out, preferred_element_type=fp32).astype(
        bf16
    )
    grad_att = lax.all_to_all(
        grad_merged.reshape(seq_count, row_len, uly_count, head_span),
        "uly",
        split_axis=2,
        concat_axis=1,
        tiled=True,
    )
    grad_att = grad_att.reshape(seq_count, block_rows, local_heads, head_dim)
    delta = jnp.transpose(jnp.sum(grad_att.astype(fp32) * attended, -1), (0, 2, 1))
    back_keys, back_values = (all_keys, all_values)
    sweep_rows = math.gcd(seq_len, 1024)

    def query_terms(offset):
        key_part = lax.dynamic_slice_in_dim(back_keys, offset, sweep_rows, 1)
        value_part = lax.dynamic_slice_in_dim(back_values, offset, sweep_rows, 1)
        scores, causal = score_block(key_part, offset)
        attn_probs = softmax_of(scores, causal, row_max, row_total)
        key_heads = key_part.reshape(seq_count, sweep_rows, local_heads, head_dim)
        value_heads = value_part.reshape(seq_count, sweep_rows, local_heads, head_dim)
        grad_probs = jnp.einsum(
            "sqhd,skhd->shqk", grad_att, value_heads, preferred_element_type=fp32
        )
        grad_scores = (attn_probs * (grad_probs - delta[..., None])).astype(bf16)
        query_term = (
            jnp.einsum("shqk,skhd->sqhd", grad_scores, key_heads, preferred_element_type=fp32)
            * score_scale
        )
        return (query_term, grad_scores, attn_probs.astype(bf16))

    query_init = jnp.zeros((seq_count, block_rows, local_heads, head_dim), fp32)

    def back_step(carried, turn_number):
        grad_query, kv_buffer = carried
        offset = turn_number * sweep_rows
        query_term, grad_scores, probs_low = query_terms(offset)
        grad_key = (
            jnp.einsum("shqk,sqhd->skhd", grad_scores, queries, preferred_element_type=fp32)
            * score_scale
        )
        grad_value = jnp.einsum("shqk,sqhd->skhd", probs_low, grad_att, preferred_element_type=fp32)
        kv_pair = jnp.stack(
            [
                grad_key.reshape(seq_count, sweep_rows, head_span),
                grad_value.reshape(seq_count, sweep_rows, head_span),
            ],
            2,
        )
        kv_buffer = lax.dynamic_update_slice_in_dim(kv_buffer, kv_pair, offset, 1)
        return ((grad_query + query_term, kv_buffer), None)

    back_init = (query_init, jnp.zeros((seq_count, seq_len, 2, head_span), fp32))
    back_done, _ = lax.scan(
        back_step, back_init, jnp.arange(seq_len // sweep_rows, dtype=jnp.int32)
    )
    grad_query, kv_buffer = back_done
    kv_summed = lax.psum_scatter(
        kv_buffer.astype(jnp.bfloat16), "blk", scatter_dimension=1, tiled=True
    ).astype(jnp.float32)
    grad_heads = jnp.concatenate(
        [
            grad_query.reshape(seq_count, block_rows, 1, head_span).astype(bf16),
            kv_summed.astype(bf16),
        ],
        2,
    )
    grad_qkv = lax.all_to_all(
        grad_heads.reshape(seq_count, block_rows, 3, 1, head_span),
        "uly",
        split_axis=1,
        concat_axis=3,
        tiled=True,
    )
    grad_qkv = grad_qkv.reshape(seq_count * row_len, 3 * width)
    qkv_grad = jnp.einsum("ta,tb->ab", ln_in, grad_qkv, preferred_element_type=fp32)
    column_sums = jnp.sum(grad_qkv.astype(fp32), 0)
    grad_in_norm = jnp.einsum("tb,ab->ta", grad_qkv, w_qkv, preferred_element_type=fp32)
    gain_in_grad = jnp.sum(grad_in_norm * normed_in, 0)
    shift_in_grad = jnp.sum(grad_in_norm, 0)
    grad_input = grad_resid + norm_back(grad_in_norm, normed_in, inverse_in, gain_rows[0])
    gains_grad = jnp.stack([gain_in_grad, gain_mid_grad])
    biases_grad = jnp.stack([shift_in_grad, column_sums[:width], out_shift_grad, proj_shift_grad])
    value_grad = column_sums[2 * width :]
    shard_grads = (
        lax.psum_scatter(gains_grad, ("blk", "uly"), scatter_dimension=1, tiled=True),
        lax.psum_scatter(biases_grad, ("blk", "uly"), scatter_dimension=1, tiled=True),
        lax.psum_scatter(shift_mid_grad, ("blk", "uly"), scatter_dimension=0, tiled=True),
        lax.psum_scatter(value_grad, ("blk", "uly"), scatter_dimension=0, tiled=True),
        lax.psum_scatter(qkv_grad, ("blk", "uly"), scatter_dimension=0, tiled=True),
        lax.psum_scatter(out_grad, ("blk", "uly"), scatter_dimension=0, tiled=True),
        lax.psum_scatter(fc_grad, ("blk", "uly"), scatter_dimension=0, tiled=True),
        lax.psum_scatter(fc_shift_grad, ("blk", "uly"), scatter_dimension=0, tiled=True),
        lax.psum_scatter(proj_grad, ("blk", "uly"), scatter_dimension=0, tiled=True),
    )
    shard_grads = (
        lax.psum(shard_grads[0].astype(jnp.bfloat16), "dp").astype(jnp.float32),
        lax.psum(shard_grads[1].astype(jnp.bfloat16), "dp").astype(jnp.float32),
        lax.psum(shard_grads[2].astype(jnp.bfloat16), "dp").astype(jnp.float32),
        lax.psum(shard_grads[3].astype(jnp.bfloat16), "dp").astype(jnp.float32),
        lax.psum(shard_grads[4].astype(jnp.bfloat16), "dp").astype(jnp.float32),
        lax.psum(shard_grads[5].astype(jnp.bfloat16), "dp").astype(jnp.float32),
        lax.psum(shard_grads[6].astype(jnp.bfloat16), "dp").astype(jnp.float32),
        lax.psum(shard_grads[7].astype(jnp.bfloat16), "dp").astype(jnp.float32),
        lax.psum(shard_grads[8].astype(jnp.bfloat16), "dp").astype(jnp.float32),
    )
    output = result.astype(bf16).reshape(seq_count, row_len, width)
    input_grad = grad_input.astype(bf16).reshape(seq_count, row_len, width)
    return (
        output,
        input_grad,
        shard_grads[0],
        shard_grads[1],
        shard_grads[2],
        shard_grads[3],
        shard_grads[4],
        shard_grads[5],
        shard_grads[6],
        shard_grads[7],
        shard_grads[8],
    )


MESH = pl.DeviceIdType.MESH
BF = jnp.bfloat16
F32 = jnp.float32
VSPEC = pl.BlockSpec(memory_space=pltpu.VMEM)
GELU_IN = math.sqrt(2.0 / math.pi)


class Net:
    def __init__(self, send_sem, recv_sem, nz):
        self.send_sem, self.recv_sem = send_sem, recv_sem
        self.count = 0
        self.sent = []
        self.nz = nz
        self.x = lax.axis_index("dp")
        self.z = lax.axis_index("blk")
        self.u = lax.axis_index("uly")

    def send(self, src, dst, dev):
        k = self.count
        self.count += 1
        copy = pltpu.make_async_remote_copy(
            src_ref=src,
            dst_ref=dst,
            send_sem=self.send_sem.at[k],
            recv_sem=self.recv_sem.at[k],
            device_id=dev,
            device_id_type=MESH,
        )
        copy.start()
        self.sent.append(copy)
        return copy

    def plane(self, m):
        return (self.x, self.z, self.u ^ m)

    def other_x(self):
        return (1 - self.x, self.z, self.u)

    def zplus(self, d):
        return lax.rem(self.z + d, self.nz)

    def line(self, d):
        return (self.x, self.zplus(d), self.u)

    def hail(self):
        barrier = pltpu.get_barrier_semaphore()
        near = [self.plane(m) for m in (1, 2, 3)] + [self.other_x()]
        near += [self.line(d) for d in range(1, self.nz)]
        near += [(1 - self.x, self.z, self.u ^ m) for m in (1, 2, 3)]
        for dev in near:
            pl.semaphore_signal(barrier, inc=1, device_id=dev, device_id_type=MESH)
        self.met = len(near)

    def meet(self):
        pl.semaphore_wait(pltpu.get_barrier_semaphore(), self.met)

    def finish(self):
        for copy in self.sent:
            copy.wait_send()


class Line:
    def __init__(self, net, send_sem, recv_sem, base):
        self.net, self.send_sem, self.recv_sem, self.base = net, send_sem, recv_sem, base
        self.z = net.z
        self.inner = jnp.logical_and(net.z >= 1, net.z <= net.nz - 2)
        self.far = net.nz - 1 - net.z

    def copy(self, src, dst, k, target, recv=None):
        target = jnp.clip(target, 0, self.net.nz - 1)
        return pltpu.make_async_remote_copy(
            src_ref=src,
            dst_ref=dst,
            send_sem=self.send_sem.at[self.base + k],
            recv_sem=self.recv_sem.at[self.base + (k if recv is None else recv)],
            device_id=(self.net.x, target, self.net.u),
            device_id_type=MESH,
        )

    def target(self, d):
        return lax.rem(self.z + d, self.net.nz)

    def source(self, d):
        return lax.rem(self.z - d + self.net.nz, self.net.nz)


class Spread(Line):
    def __init__(self, net, send_sem, recv_sem, base, block):
        super().__init__(net, send_sem, recv_sem, base)
        self.block = block

    def direct(self, d):
        return self.copy(self.block(self.z), self.block(self.z), d, self.target(d))

    def start(self):
        for d in (2, 1, 3):
            if d == 2:
                self.direct(d).start()
            else:
                @pl.when(jnp.logical_or(self.inner, self.target(d) != self.far))
                def _():
                    self.direct(d).start()

    def relay_copy(self):
        block = self.block(self.source(2))
        target = jnp.where(self.z == 2, 3, 0)
        return self.copy(block, block, 4, target, jnp.where(self.z == 2, 3, 1))

    def across(self, d):
        block = self.block(self.source(d))
        return pltpu.make_async_remote_copy(
            src_ref=block, dst_ref=block, send_sem=self.send_sem.at[self.base + 4 + d],
            recv_sem=self.recv_sem.at[self.base + 4 + d], device_id=self.net.other_x(), device_id_type=MESH)

    def arrive(self, d):
        block = self.block(self.source(d))
        self.copy(block, block, d, self.z).wait_recv()

    def relay(self):
        self.arrive(2)

        @pl.when(self.inner)
        def _():
            self.relay_copy().start()

        self.across(2).start()

    def rest(self):
        first = jnp.where(self.z == 0, 3, 1)
        for d in (first, 4 - first):
            self.arrive(d)
            self.across(d).start()

    def finish_recv(self):
        for d in (2, 1, 3):
            self.across(d).wait_recv()

    def finish(self):
        self.direct(2).wait_send()
        for d in (1, 3):
            @pl.when(jnp.logical_or(self.inner, self.target(d) != self.far))
            def _():
                self.direct(d).wait_send()
        for d in (1, 2, 3):
            self.across(d).wait_send()

        @pl.when(self.inner)
        def _():
            self.relay_copy().wait_send()


class Collect(Line):
    def __init__(self, net, send_sem, recv_sem, base, theirs, ours, land_x, mine, land_z, relay):
        super().__init__(net, send_sem, recv_sem, base)
        self.theirs, self.ours = theirs, ours
        self.land_x, self.mine, self.land_z, self.relay = land_x, mine, land_z, relay

    def order(self, i):
        pick = lambda table: table[i]
        z = self.z
        return jnp.where(z == 0, 3 - i, jnp.where(z == 3, i, jnp.where(z == 1, pick((0, 2, 3, 1)), pick((3, 1, 0, 2)))))

    def across(self, i):
        zz = self.order(i)
        return pltpu.make_async_remote_copy(
            src_ref=self.theirs(zz), dst_ref=self.land_x.at[zz], send_sem=self.send_sem.at[self.base + 5 + i],
            recv_sem=self.recv_sem.at[self.base + 5 + i], device_id=self.net.other_x(), device_id_type=MESH)

    def start(self):
        for i in range(4):
            self.across(i).start()

    def own(self, i):
        zz = self.order(i)
        self.across(i).wait_recv()
        self.mine[zz] = (self.ours(zz) + self.land_x[zz].astype(F32)).astype(BF)

    def direct(self, zz):
        d = lax.rem(zz - self.z + 4, 4)
        return self.copy(self.mine.at[zz], self.land_z.at[d - 1], d, zz)

    def to_neighbour(self):
        return self.copy(self.mine.at[self.far], self.relay, 4, jnp.where(self.z == 0, 1, 2))

    def part(self, i):
        self.own(i)
        if i == 0:
            @pl.when(self.inner)
            def _():
                self.direct(self.order(0)).start()

            @pl.when(jnp.logical_not(self.inner))
            def _():
                self.to_neighbour().start()
        elif i == 1:
            self.direct(self.order(1)).start()
        elif i == 2:
            @pl.when(jnp.logical_not(self.inner))
            def _():
                self.direct(self.order(2)).start()

    def first(self):
        for i in range(4):
            self.part(i)

    def second(self):
        @pl.when(self.inner)
        def _():
            zz = self.order(2)
            self.copy(self.relay, self.relay, 4, self.z).wait_recv()
            self.mine[zz] = (self.mine[zz].astype(F32) + self.relay[...].astype(F32)).astype(BF)
            self.direct(zz).start()

    def total(self, final):
        skip = jnp.where(self.z == 0, 1, 3)
        final[...] = self.mine[self.z].astype(F32)
        for d in (1, 2, 3):
            @pl.when(jnp.logical_or(self.inner, skip != d))
            def _():
                self.copy(self.land_z.at[d - 1], self.land_z.at[d - 1], d, self.z).wait_recv()
                final[...] += self.land_z[d - 1].astype(F32)

    def finish(self):
        for i in range(4):
            self.across(i).wait_send()

        @pl.when(self.inner)
        def _():
            for i in range(3):
                self.direct(self.order(i)).wait_send()

        @pl.when(jnp.logical_not(self.inner))
        def _():
            self.to_neighbour().wait_send()
            for i in (1, 2):
                self.direct(self.order(i)).wait_send()


def rows_at(start, count):
    return pl.ds(pl.multiple_of(start, 16), count)


def dot_nn(a, b):
    return jnp.dot(a, b, preferred_element_type=F32)


def dot_nt(a, b):
    return lax.dot_general(a, b, (((1,), (1,)), ((), ())), preferred_element_type=F32)


def dot_tn(a, b):
    return lax.dot_general(a, b, (((0,), (0,)), ((), ())), preferred_element_type=F32)


def loop(count, body):
    def step(i, carry):
        body(i)
        return carry

    lax.fori_loop(0, count, step, 0)


def block_kernel(nz, refs):
    r = refs
    net = Net(r.send_sem, r.recv_sem, nz)
    x, z, u = net.x, net.z, net.u
    y, c = u // 2, lax.rem(u, 2)
    own48 = (4 * z + u) * 48
    tile = lambda t: rows_at(128 * t, 128)
    half_cols = lambda which: pl.ds(pl.multiple_of(384 * which, 128), 384)
    lane = lambda shape: lax.broadcasted_iota(jnp.int32, shape, 1)

    x_own, cot_own = r.x_all.at[tile(u)], r.cot_all.at[tile(u)]
    local = [
        pltpu.make_async_copy(r.qkv_in, r.qkv_raw, r.local_sem.at[0]),
        pltpu.make_async_copy(r.fc_in, r.fc_raw, r.local_sem.at[1]),
        pltpu.make_async_copy(r.x_in, x_own, r.local_sem.at[2]),
        pltpu.make_async_copy(r.out_in, r.w_out.at[rows_at(own48, 48)], r.local_sem.at[3]),
        pltpu.make_async_copy(r.proj_in, r.w_proj.at[rows_at(192 * z, 192)], r.local_sem.at[4]),
        pltpu.make_async_copy(r.cot_in, cot_own, r.local_sem.at[5]),
    ]
    local[0].start()
    local[2].start()
    net.hail()
    local[0].wait()
    for g in range(4):
        for t in range(3):
            r.qkv_pre[g, :, 128 * t:128 * t + 128] = r.qkv_raw[:, 768 * t + 192 * g:768 * t + 192 * g + 128]
        for at, t in ((384, 1), (448, 2), (512, 0)):
            r.qkv_pre[g, :, at:at + 64] = r.qkv_raw[:, 768 * t + 192 * g + 128:768 * t + 192 * g + 192]
    r.w_qkv[rows_at(own48, 48), :] = r.qkv_pre[u]
    net.meet()

    def plane_gather_start(own, full):
        return [net.send(own, full.at[tile(u)], net.plane(m)) for m in (2, 1)]

    def plane_gather_forward(sent, full):
        sent[0].wait_recv()
        sent.append(net.send(full.at[tile(u ^ 2)], full.at[tile(u ^ 2)], net.plane(1)))

    in_plane = lambda pre, full: [
        net.send(pre.at[u ^ m], full.at[rows_at(own48, 48)], net.plane(m)) for m in (1, 2, 3)
    ]
    block96 = lambda full: lambda j: full.at[rows_at(192 * j + 96 * x, 96)]
    spread = lambda base, block: Spread(net, r.sp_send, r.sp_recv, base, block)
    qkv_s = spread(0, block96(r.w_qkv))
    fc_s = spread(8, block96(r.w_fc))
    proj_s = spread(16, block96(r.w_proj))
    out_s = spread(24, lambda j: r.w_out.at[rows_at((4 * j + u) * 48, 48), half_cols(x)])
    qkv_p = in_plane(r.qkv_pre, r.w_qkv)
    local[2].wait()
    x_g = plane_gather_start(x_own, r.x_all)
    for i in (3, 1, 4, 5):
        local[i].start()
    vp = r.vec_f32
    vp[...] = jnp.zeros((16, 768), F32)
    vp[0:2, 0:48] = r.gains_in[...].astype(F32)
    vp[2:6, 0:48] = r.biases_in[...].astype(F32)
    vp[6:7, 0:48] = r.mid_in[...].astype(F32)
    vp[7:8, 0:48] = r.vb_in[...].astype(F32)
    bias = r.bias_f32
    bias[...] = jnp.zeros((8, 256), F32)
    bias[0:1, 0:48] = r.biases_in[1:2, :].astype(F32)
    bias[1:2, 0:48] = r.vb_in[...].astype(F32)
    bias[...] = pltpu.roll(bias[...], 48 * u, 1)
    vp[0:8, :] = pltpu.roll(vp[0:8, :], 48 * (4 * z + u), 1)
    vp[8:9, 0:192] = r.fcb_in[...].astype(F32)
    vp[9:10, 0:128] = bias[0:1, 0:128]
    vp[9:10, 256:384] = bias[1:2, 0:128]
    vp[9:10, 448:512] = bias[1:2, 128:192]
    vp[9:10, 512:576] = bias[0:1, 128:192]
    high = vp[8:16, :]
    row8 = lax.broadcasted_iota(jnp.int32, high.shape, 0)
    fcb_row = pltpu.roll(jnp.where(row8 == 0, high, 0.0), 192 * z, 1)
    bias_row = jnp.sum(jnp.where(row8 == 1, high, 0.0), 0, keepdims=True)
    vp[8:16, :] = fcb_row + jnp.where(row8 == 1 + z, bias_row, 0.0)
    r.vec_pre[...] = vp[...].astype(BF)
    vec_z = [net.send(r.vec_pre, r.vec_land_z.at[d - 1], net.line(d)) for d in range(1, nz)]
    for copy in qkv_p:
        copy.wait_recv()
    qkv_s.start()
    local[3].wait()
    out_s.start()
    total = r.vec_pre[...]
    for d in range(nz - 1):
        vec_z[d].wait_recv()
        total = total + r.vec_land_z[d]
    r.vec_u[...] = total
    vec_p = [net.send(r.vec_u, r.vec_land_p.at[m - 1], net.plane(m)) for m in (1, 2, 3)]
    plane_gather_forward(x_g, r.x_all)
    for i in (1, 4, 5):
        local[i].wait()
    for g in range(4):
        for zz in range(nz):
            r.fc_pre[g, :, 192 * zz:192 * zz + 192] = r.fc_raw[:, 768 * zz + 192 * g:768 * zz + 192 * g + 192]
    r.w_fc[rows_at(own48, 48), :] = r.fc_pre[u]
    inner64 = lax.broadcasted_iota(jnp.int32, (64, 1), 0)
    inner64_row = lax.broadcasted_iota(jnp.int32, (1, 64), 1)
    for i in range(8 * nz):
        first = r.order_in[0, i] * 64
        r.pos_col[64 * i:64 * i + 64, :] = first + inner64
        r.pos_row[:, 64 * i:64 * i + 64] = first + inner64_row
    fc_p = in_plane(r.fc_pre, r.w_fc)
    total = r.vec_u[...].astype(F32)
    row = lax.broadcasted_iota(jnp.int32, total.shape, 0)
    for m in range(3):
        vec_p[m].wait_recv()
        total = total + jnp.where(row == 8, 0.0, r.vec_land_p[m].astype(F32))
    r.vec[...] = total
    for copy in x_g[1:]:
        copy.wait_recv()
    gain = lambda i: r.vec[pl.ds(i, 1), :]

    def normalize(values):
        center = values - jnp.mean(values, -1, keepdims=True)
        inverse = lax.rsqrt(jnp.mean(center * center, -1, keepdims=True) + 1e-05)
        return center * inverse, inverse

    def ln_tile(t):
        normed, _ = normalize(r.x_all[tile(t), :].astype(F32))
        r.ln_all[tile(t), :] = (normed * gain(0) + gain(2)).astype(BF)

    loop(4, ln_tile)
    qkv_s.relay()
    qkv_s.rest()
    for copy in fc_p:
        copy.wait_recv()
    fc_s.start()
    cot_g = plane_gather_start(cot_own, r.cot_all)
    r.qm[2] = jnp.zeros((512, 128), BF)
    out_s.relay()
    out_s.rest()
    qkv_s.finish_recv()

    bias_u = jnp.sum(jnp.where(row == 9 + u, r.vec[...], 0.0), 0, keepdims=True)[:, 0:576]

    def qkv_tile(t):
        res = dot_nn(r.ln_all[tile(t), :], r.w_qkv[...]) + bias_u
        res = res.astype(BF)
        q01 = res[:, 0:128].astype(F32) * 0.125
        low = lane(q01.shape) < 64
        r.qm[0, tile(t), :] = jnp.where(low, q01, 0.0).astype(BF)
        r.qm[1, tile(t), :] = jnp.where(low, 0.0, q01).astype(BF)
        r.qm[2, tile(t), 0:64] = (res[:, 512:576].astype(F32) * 0.125).astype(BF)
        r.kv_all[z, tile(t), :] = res[:, 128:512]

    loop(4, qkv_tile)

    third = lambda ch: slice(128 * ch, 128 * ch + 128)

    def kv_copy(way, step, ch):
        block = z - step if way == 0 else z + step
        target = z + 1 if way == 0 else z - 1
        block, target = jnp.clip(block, 0, nz - 1), jnp.clip(target, 0, nz - 1)
        return pltpu.make_async_remote_copy(
            src_ref=r.kv_all.at[block, :, third(ch)], dst_ref=r.kv_all.at[block, :, third(ch)],
            send_sem=r.kv_send.at[(way * nz + step) * 3 + ch], recv_sem=r.kv_recv.at[(way * nz + step) * 3 + ch],
            device_id=(x, target, u), device_id_type=MESH)

    def kv_sends(way, step):
        if way == 0:
            return jnp.logical_and(z - step >= 0, z + 1 < nz)
        return jnp.logical_and(z + step < nz, z >= 1)

    def kv_start(step, ch, way):
        @pl.when(kv_sends(way, step))
        def _():
            kv_copy(way, step, ch).start()

    def attend(j):
        qp = r.pos_row[:, pl.ds(pl.multiple_of(512 * z, 128), 512)]
        for h in range(3):
            kc = 0 if h < 2 else 256
            vc = 128 if h < 2 else 256
            q = r.qm[h]

            def score(kt, top):
                s = dot_nt(r.kv_all[j, rows_at(128 * kt, 128), kc:kc + 128], q)
                kp = r.pos_col[pl.ds(pl.multiple_of(512 * j + 128 * kt, 128), 128), :]
                s = jnp.where(kp <= qp, s, -1e30)
                r.s_buf[rows_at(128 * kt, 128), :] = s
                return jnp.maximum(top, jnp.max(s, 0, keepdims=True))

            old = r.m_run[h]
            top = lax.fori_loop(0, 4, score, old, unroll=True)
            shrink = jnp.exp(old - top)

            def weigh(kt, got):
                p = jnp.exp(r.s_buf[rows_at(128 * kt, 128), :] - top)
                r.pt[j * 3 + h, rows_at(128 * kt, 128), :] = p.astype(BF)
                return got + jnp.sum(p, 0, keepdims=True)

            got = lax.fori_loop(0, 4, weigh, jnp.zeros((1, 512), F32), unroll=True)
            r.m_run[h] = top
            r.m_at[j * 3 + h] = top
            r.l_run[h] = r.l_run[h] * shrink + got
            r.o_t[h] = r.o_t[h] * shrink + dot_tn(r.kv_all[j, :, vc:vc + 128], r.pt[j * 3 + h])

    r.m_run[...] = jnp.full((3, 1, 512), -1e30, F32)
    r.l_run[...] = jnp.zeros((3, 1, 512), F32)
    r.o_t[...] = jnp.zeros((3, 128, 512), F32)
    for ch in range(3):
        for way in range(2):
            kv_start(0, ch, way)
    plane_gather_forward(cot_g, r.cot_all)
    attend(z)
    fc_s.relay()

    for step in range(1, nz):
        for ch in range(3):
            for way in range(2):
                @pl.when(z - step >= 0 if way == 0 else z + step < nz)
                def _():
                    kv_copy(way, step - 1, ch).wait_recv()

                if step < nz - 1:
                    kv_start(step, ch, way)
        if step == 1:
            fc_s.rest()
            out_s.finish_recv()
            out_rows = lambda zz, who: r.w_out.at[rows_at((4 * zz + who) * 48, 48)]
            out_y = [net.send(out_rows(zz, u), out_rows(zz, u), net.plane(2)) for zz in range(nz)]
            out_c = [net.send(out_rows(zz, u), out_rows(zz, u), net.plane(1)) for zz in range(nz)]
        if step == 2:
            for zz, copy in enumerate(out_y):
                copy.wait_recv()
                out_c.append(net.send(out_rows(zz, u ^ 2), out_rows(zz, u ^ 2), net.plane(1)))
        if step == nz - 1:
            proj_s.start()

        def either(way):
            j = jnp.where(way == 0, z - step, z + step)

            @pl.when(jnp.logical_and(j >= 0, j < nz))
            def _():
                attend(j)

        loop(2, either)

    rowi = lax.broadcasted_iota(jnp.int32, (128, 512), 0)
    r.l_inv[...] = 1.0 / r.l_run[...]
    r.att_t[0] = jnp.where(rowi < 64, r.o_t[0] * r.l_inv[0], r.o_t[1] * r.l_inv[1])
    r.att_t[1] = jnp.where(rowi < 64, 0.0, r.o_t[2] * r.l_inv[2])
    r.att[:, 0:128] = jnp.transpose(r.att_t[0]).astype(BF)
    r.att[:, 128:256] = jnp.transpose(r.att_t[1]).astype(BF)
    att_p = [net.send(r.att.at[tile(u ^ m)], r.merged.at[u], net.plane(m)) for m in (2, 3, 1)]
    r.merged[u] = r.att[tile(u), :]

    for copy in out_c:
        copy.wait_recv()
    for g in range(4):
        r.w_outp[256 * g:256 * g + 128, :] = r.w_out[192 * g:192 * g + 128, :]
        r.w_outp[256 * g + 128:256 * g + 192, :] = jnp.zeros((64, 768), BF)
        r.w_outp[256 * g + 192:256 * g + 256, :] = r.w_out[192 * g + 128:192 * g + 192, :]
    for copy in cot_g[1:]:
        copy.wait_recv()
    proj_s.relay()
    for copy in att_p:
        copy.wait_recv()
    resid = x_own[...].astype(F32) + gain(4)
    for g in range(4):
        resid = resid + dot_nn(r.merged[g], r.w_outp[256 * g:256 * g + 256, :])
    r.resid[...] = resid
    normed, inverse = normalize(resid)
    r.normed_mid[...] = normed
    r.inverse_mid[...] = inverse
    r.lm_all[tile(u), :] = (normed * gain(1) + gain(6)).astype(BF)
    lm_own = r.lm_all.at[tile(u)]
    lm_g = [net.send(lm_own, lm_own, net.plane(m)) for m in (2, 1)]
    fc_s.finish_recv()

    r.vec_g[...] = jnp.zeros((16, 768), F32)

    def mlp_front(t):
        rows = tile(t)
        pre = dot_nn(r.lm_all[rows, :], r.w_fc[...]) + gain(8)
        square = pre * pre
        th = jnp.tanh(GELU_IN * (pre * (1.0 + 0.044715 * square)))
        r.act[rows, :] = (0.5 * pre * (1.0 + th)).astype(BF)
        r.slope[rows, :] = 0.5 * (1.0 + th) + (0.5 * GELU_IN) * pre * (1.0 - th * th) * (1.0 + 0.134145 * square)

    def mlp_back(t):
        rows = tile(t)
        gp = (r.slope[rows, :] * dot_nt(r.cot_all[rows, :], r.w_proj[...])).astype(BF)
        r.grad_pre[rows, :] = gp
        r.fcb[...] += jnp.sum(gp.astype(F32), 0, keepdims=True)
        r.gm_part[t] = dot_nt(gp, r.w_fc[...]).astype(BF)

    r.fcb[...] = jnp.zeros((1, 768), F32)
    mlp_front(u)
    lm_g[1].wait_recv()
    mlp_front(u ^ 1)
    plane_gather_forward(lm_g, r.lm_all)

    def reduce_core(i, t, part, land_c):
        return net.send(part.at[t], land_c.at[i], net.plane(1))

    def reduce_y(copy, part, land_c, mid, land_y):
        copy.wait_recv()
        mid[...] = (part[u ^ 2].astype(F32) + land_c[0].astype(F32)).astype(BF)
        return net.send(mid, land_y, net.plane(2))

    def reduce_end(copy_c, copy_y, part, land_c, land_y):
        copy_c.wait_recv()
        copy_y.wait_recv()
        return part[u].astype(F32) + land_c[1].astype(F32) + land_y[...].astype(F32)

    mlp_front(u ^ 2)
    proj_s.rest()
    lm_g[2].wait_recv()
    mlp_front(u ^ 3)
    proj_s.finish_recv()
    mlp_back(u ^ 3)
    gm_c0 = reduce_core(0, u ^ 3, r.gm_part, r.gm_c)
    mlp_back(u ^ 1)
    gm_c1 = reduce_core(1, u ^ 1, r.gm_part, r.gm_c)
    mlp_back(u ^ 2)
    gm_y = reduce_y(gm_c0, r.gm_part, r.gm_c, r.gm_mid, r.gm_y)
    mlp_back(u)
    r.vec_g[...] += jnp.where(row == 10 + u, r.fcb[...], 0.0)

    def branch_tile(t):
        r.br_part[t] = dot_nn(r.act[tile(t), :], r.w_proj[...]).astype(BF)

    def weight_grad(a, b, out, tiles):
        def one(i):
            cols = pl.ds(pl.multiple_of(128 * i, 128), 128)
            out[tile(i), :] = dot_tn(a[:, cols], b[...]).astype(BF)

        loop(tiles, one)

    def collect(base, grad, land_x, mine, land_z, relay):
        return Collect(
            net, r.co_send, r.co_recv, base,
            lambda zz: grad.at[rows_at(192 * zz + 96 * (1 - x), 96)],
            lambda zz: grad[rows_at(192 * zz + 96 * x, 96), :].astype(F32),
            land_x, mine, land_z, relay)

    proj_c = collect(0, r.proj_g, r.proj_x, r.proj_m, r.proj_z, r.proj_r)
    fc_c = collect(9, r.fc_g, r.fc_x, r.fc_m, r.fc_z, r.fc_r)
    qkv_c = collect(18, r.qkv_g, r.qkv_x, r.qkv_m, r.qkv_z, r.qkv_r)

    weight_grad(r.act, r.cot_all, r.proj_g, 6)
    proj_c.start()
    branch_tile(u ^ 3)
    branch_tile(u ^ 1)
    br_c = [reduce_core(0, u ^ 3, r.br_part, r.br_c), reduce_core(1, u ^ 1, r.br_part, r.br_c)]
    branch_tile(u ^ 2)
    branch_tile(u)

    gm = reduce_end(gm_c1, gm_y, r.gm_part, r.gm_c, r.gm_y)
    normed = r.normed_mid[...]
    r.vec_g[1:2, :] = jnp.sum(gm * normed, 0, keepdims=True)
    r.vec_g[5:6, :] = jnp.sum(gm, 0, keepdims=True)

    def norm_grad(grad, normed, inverse, g):
        e = grad * g
        return inverse * (
            e - jnp.mean(e, -1, keepdims=True) - normed * jnp.mean(e * normed, -1, keepdims=True)
        )

    cot = cot_own[...].astype(F32)
    r.vec_g[4:5, :] = jnp.sum(cot, 0, keepdims=True)
    grad_resid = cot + norm_grad(gm, normed, r.inverse_mid[...], gain(1))
    r.grad_resid[...] = grad_resid
    gb = grad_resid.astype(BF)
    r.gb[...] = gb
    r.vec_g[3:4, :] = jnp.sum(gb.astype(F32), 0, keepdims=True)

    def gmer_tile(g):
        r.gmer[g] = dot_nt(r.gb[...], r.w_outp[pl.ds(pl.multiple_of(256 * g, 256), 256), :]).astype(BF)

    loop(4, gmer_tile)
    ga_p = [net.send(r.gmer.at[u ^ m], r.ga.at[tile(u)], net.plane(m)) for m in (2, 3, 1)]
    r.ga[tile(u), :] = r.gmer[u]
    weight_grad(r.lm_all, r.grad_pre, r.fc_g, 6)
    for g in range(4):
        res = dot_tn(r.merged[g], r.gb[...]).astype(BF)
        at = slice(48 * g, 48 * g + 48)
        r.out_g[0, 0, at, :] = res[0:48]
        r.out_g[1, 0, at, :] = res[48:96]
        r.out_g[0, 1, 48 * g:48 * g + 32, :] = res[96:128]
        r.out_g[0, 1, 48 * g + 32:48 * g + 48, :] = res[192:208]
        r.out_g[1, 1, at, :] = res[208:256]
    og_c = net.send(r.out_g.at[1 - c], r.og_c, net.plane(1))
    proj_c.part(0)
    proj_c.part(1)
    for copy in ga_p:
        copy.wait_recv()

    low = lane((512, 128)) < 64
    ga01 = r.ga[:, 0:128]
    zero = jnp.zeros((512, 128), BF)
    r.gam[0] = jnp.where(low, ga01.astype(F32), 0.0).astype(BF)
    r.gam[1] = jnp.where(low, 0.0, ga01.astype(F32)).astype(BF)
    r.gam[2] = r.ga[:, 128:256]
    prod = jnp.transpose(ga01.astype(F32)) * r.att_t[0]
    r.delta[0] = jnp.sum(prod[0:64], 0, keepdims=True)
    r.delta[1] = jnp.sum(prod[64:128], 0, keepdims=True)
    prod = jnp.transpose(r.ga[:, 128:256].astype(F32)) * r.att_t[1]
    r.delta[2] = jnp.sum(prod, 0, keepdims=True)
    r.dq_t[...] = jnp.zeros((3, 128, 512), F32)

    def back(j):
        factor = [jnp.exp(r.m_at[j * 3 + h] - r.m_run[h]) * r.l_inv[h] for h in range(3)]

        def keys(kt):
            rows = rows_at(128 * kt, 128)
            for h in range(3):
                vc = 128 if h < 2 else 256
                p = r.pt[j * 3 + h, rows, :].astype(F32) * factor[h]
                dp = dot_nt(r.kv_all[j, rows, vc:vc + 128], r.gam[h])
                r.ds[h, rows, :] = (p * (dp - r.delta[h])).astype(BF)
                r.pt[j * 3 + h, rows, :] = p.astype(BF)

        def sums(kt):
            rows = rows_at(128 * kt, 128)
            pair = lambda of, first, second: dot_nn(of(0), first) + dot_nn(of(1), second)
            ds = lambda h: r.ds[h, rows, :]
            p = lambda h: r.pt[j * 3 + h, rows, :]
            r.dkv[rows, 0:128] = pair(ds, r.qm[0], r.qm[1])
            r.dkv[rows, 128:256] = pair(p, r.gam[0], r.gam[1])
            r.dkv[rows, 256:384] = dot_nn(ds(2), r.qm[2]) + dot_nn(p(2), r.gam[2])

        loop(4, keys)
        loop(4, sums)
        for h in range(3):
            kc = 0 if h < 2 else 256
            r.dq_t[h] += dot_tn(r.kv_all[j, :, kc:kc + 128], r.ds[h])

    def chain_copy(way, step, ch):
        target = jnp.clip(jnp.where(way == 0, z - 1, z + 1), 0, nz - 1)
        at = way * (nz - 1) + step - 1
        return pltpu.make_async_remote_copy(
            src_ref=r.chain.at[at, :, third(ch)], dst_ref=r.chain_land.at[at, :, third(ch)],
            send_sem=r.ch_send.at[at * 3 + ch], recv_sem=r.ch_recv.at[at * 3 + ch],
            device_id=(x, target, u), device_id_type=MESH)

    def chain_step(step):
        def either(way):
            j = jnp.where(way == 0, z - step, z + step)
            behind = jnp.where(way == 0, z + 1, z - 1)

            @pl.when(jnp.logical_and(j >= 0, j < nz))
            def _():
                back(j)
                at = way * (nz - 1) + step - 1
                comes = jnp.logical_and(behind >= 0, behind < nz)
                for ch in range(3):
                    at_ch = third(ch)
                    if step < nz - 1:
                        @pl.when(comes)
                        def _():
                            chain_copy(way, step + 1, ch).wait_recv()
                            r.chain[at, :, at_ch] = (r.dkv[:, at_ch] + r.chain_land[at + 1, :, at_ch].astype(F32)).astype(BF)

                        @pl.when(jnp.logical_not(comes))
                        def _():
                            r.chain[at, :, at_ch] = r.dkv[:, at_ch].astype(BF)
                    else:
                        r.chain[at, :, at_ch] = r.dkv[:, at_ch].astype(BF)
                    chain_copy(way, step, ch).start()

        loop(2, either)

    for step in range(nz - 1, 0, -1):
        chain_step(step)
        if step == nz - 1:
            proj_c.part(2)
            proj_c.part(3)
            fc_c.start()
            early_p = [net.send(r.vec_g, r.vg_p.at[m - 1], net.plane(m)) for m in (1, 2, 3)]
            br_y = reduce_y(br_c[0], r.br_part, r.br_c, r.br_mid, r.br_y)
            og_c.wait_recv()
            r.og_1[...] = (r.out_g[c].astype(F32) + r.og_c[...].astype(F32)).astype(BF)
            og_y = net.send(r.og_1.at[1 - y], r.og_y, net.plane(2))
        if step == nz - 2:
            proj_c.second()
            r.output[...] = (
                r.resid[...] + gain(5) + reduce_end(br_c[1], br_y, r.br_part, r.br_c, r.br_y)
            ).astype(BF)
            total = r.vec_g[...]
            for m in range(3):
                early_p[m].wait_recv()
                total = total + r.vg_p[m]
            r.vg_1[...] = total
            early_z = [net.send(r.vg_1, r.vg_z.at[d - 1], net.line(d)) for d in range(1, nz)]
            fc_c.part(0)
            fc_c.part(1)
            og_y.wait_recv()
            r.og_2[...] = (r.og_1[y].astype(F32) + r.og_y[...].astype(F32)).astype(BF)
            og_x = net.send(r.og_2.at[:, half_cols(1 - x)], r.og_x, net.other_x())
        if step == 1:
            og_x.wait_recv()
            r.og_3[...] = (r.og_2[:, half_cols(x)].astype(F32) + r.og_x[...].astype(F32)).astype(BF)
            og_z = [
                net.send(r.og_3.at[rows_at(48 * net.zplus(d), 48)], r.og_z.at[d - 1], net.line(d))
                for d in range(1, nz)
            ]
            total = r.vg_1[...]
            for d in range(nz - 1):
                early_z[d].wait_recv()
                total = total + r.vg_z[d]
            r.vg_2[...] = total
            early_x = net.send(r.vg_2, r.vg_x, net.other_x())
            fc_c.part(2)
            fc_c.part(3)
    back(z)

    fc_c.second()
    for ch in range(3):
        @pl.when(z + 1 < nz)
        def _():
            chain_copy(0, 1, ch).wait_recv()
            r.dkv[:, third(ch)] += r.chain_land[0, :, third(ch)].astype(F32)

        @pl.when(z >= 1)
        def _():
            chain_copy(1, 1, ch).wait_recv()
            r.dkv[:, third(ch)] += r.chain_land[nz - 1, :, third(ch)].astype(F32)

    r.gqkv[:, 128:512] = r.dkv[...].astype(BF)
    dq = jnp.transpose(jnp.where(rowi < 64, r.dq_t[0], r.dq_t[1]) * 0.125)
    r.gqkv[:, 0:128] = dq.astype(BF)
    r.gqkv[:, 512:576] = jnp.transpose(r.dq_t[2] * 0.125)[:, 0:64].astype(BF)


    def gin_tile(t):
        r.gi_part[t] = dot_nt(r.gqkv[tile(t), :], r.w_qkv[...]).astype(BF)

    weight_grad(r.ln_all, r.gqkv, r.qkv_g, 6)
    qkv_c.start()
    gin_tile(u ^ 3)
    gi_c0 = reduce_core(0, u ^ 3, r.gi_part, r.gi_c)
    gin_tile(u ^ 1)
    gi_c1 = reduce_core(1, u ^ 1, r.gi_part, r.gi_c)
    gin_tile(u ^ 2)
    gi_y = reduce_y(gi_c0, r.gi_part, r.gi_c, r.gi_mid, r.gi_y)
    gin_tile(u)
    r.late[...] = jnp.zeros((8, 768), F32)
    row_l = row[0:8]
    r.late[:, 0:576] = jnp.where(row_l[:, 0:576] == 2 + u, jnp.sum(r.gqkv[...].astype(F32), 0, keepdims=True), 0.0)
    qkv_c.first()
    proj_c.total(r.acc)
    r.proj_f[...] = r.acc[...].astype(BF)
    mine = rows_at(96 * x, 96)
    r.proj_o[mine, :] = r.proj_f[...]
    proj_last = net.send(r.proj_f, r.proj_o.at[mine], net.other_x())

    finals = []

    def hand_out(base, final, native):
        for xx in range(2):
            for cc in range(2):
                target_x = x ^ xx
                target_u = 2 * x + cc
                here = jnp.logical_and(xx == 0, target_u == u)
                k = base + 2 * xx + cc
                copy = pltpu.make_async_remote_copy(
                    src_ref=final.at[pl.ds(48 * cc, 48)], dst_ref=native.at[u], send_sem=r.f_send.at[k],
                    recv_sem=r.f_recv.at[base + u], device_id=(target_x, z, target_u), device_id_type=MESH)

                @pl.when(jnp.logical_not(here))
                def _():
                    copy.start()

                @pl.when(here)
                def _():
                    native[u] = final[pl.ds(48 * cc, 48), :]

                finals.append((here, copy))

    def await_native(base, final, native):
        for who in range(4):
            copy = pltpu.make_async_remote_copy(
                src_ref=final.at[pl.ds(0, 48)], dst_ref=native.at[who], send_sem=r.f_send.at[base],
                recv_sem=r.f_recv.at[base + who], device_id=(1 - x, z, u), device_id_type=MESH)

            @pl.when(jnp.logical_not(jnp.logical_and(x == y, u == who)))
            def _():
                copy.wait_recv()

    gin = reduce_end(gi_c1, gi_y, r.gi_part, r.gi_c, r.gi_y)
    normed, inverse = normalize(x_own[...].astype(F32))
    r.late[0:1, :] = jnp.sum(gin * normed, 0, keepdims=True)
    r.late[1:2, :] = jnp.sum(gin, 0, keepdims=True)
    late_p = [net.send(r.late, r.late_p.at[m - 1], net.plane(m)) for m in (2, 3, 1)]
    late_p += [net.send(r.late, r.late_p.at[3 + m], (1 - x, z, u ^ m)) for m in range(4)]
    r.input_grad[...] = (r.grad_resid[...] + norm_grad(gin, normed, inverse, gain(0))).astype(BF)
    qkv_c.second()
    fc_c.total(r.acc)
    r.fc_f[...] = r.acc[...].astype(BF)
    hand_out(0, r.fc_f, r.fc_o)
    total = r.late[...]
    for copy in late_p:
        copy.wait_recv()
    for m in range(7):
        total = total + r.late_p[m]
    r.late_1[...] = total
    late_z = [net.send(r.late_1, r.late_z.at[d - 1], net.line(d)) for d in range(1, nz)]
    total = r.og_3[rows_at(48 * z, 48), :].astype(F32)
    for d in range(nz - 1):
        og_z[d].wait_recv()
        total = total + r.og_z[d].astype(F32)
    r.out_o[:, half_cols(x)] = total.astype(BF)
    og_last = net.send(r.out_o.at[:, half_cols(x)], r.out_o.at[:, half_cols(x)], net.other_x())
    qkv_c.total(r.acc_q)
    r.qkv_f[...] = r.acc_q[...].astype(BF)
    hand_out(4, r.qkv_f, r.qkv_o)
    early_x.wait_recv()
    early = r.vg_2[...] + r.vg_x[...]
    late = r.late_1[...]
    for d in range(nz - 1):
        late_z[d].wait_recv()
        late = late + r.late_z[d]
    heads = jnp.sum(jnp.where(row_l == 2 + z, late, 0.0), 0, keepdims=True)
    hidden = jnp.sum(jnp.where(row == 10 + u, early, 0.0), 0, keepdims=True)
    total = early[0:8] + jnp.where(row_l == 0, late, 0.0) + jnp.where(row_l == 2, late[1:2], 0.0)
    bias[0:1, 0:128] = heads[:, 0:128]
    bias[0:1, 128:192] = heads[:, 512:576]
    bias[1:2, 0:128] = heads[:, 256:384]
    bias[1:2, 128:192] = heads[:, 448:512]
    mine8 = pltpu.roll(total, 768 - 48 * (4 * z + u), 1)
    vp[0:8, :] = mine8
    both = pltpu.roll(bias[...], 256 - 48 * u, 1)
    vp[6:8, 0:256] = both[0:2]
    vp[8:16, :] = pltpu.roll(jnp.broadcast_to(hidden, (8, 768)), 768 - 192 * z, 1)
    r.vec_o[...] = vp[...]
    proj_last.wait_recv()
    og_last.wait_recv()
    await_native(0, r.fc_f, r.fc_o)
    await_native(4, r.qkv_f, r.qkv_o)

    for here, copy in finals:
        @pl.when(jnp.logical_not(here))
        def _():
            copy.wait_send()
    for step in range(nz - 1):
        for way in range(2):
            @pl.when(kv_sends(way, step))
            def _():
                for ch in range(3):
                    kv_copy(way, step, ch).wait_send()
    for step in range(1, nz):
        for way in range(2):
            @pl.when(z - step >= 0 if way == 0 else z + step < nz)
            def _():
                for ch in range(3):
                    chain_copy(way, step, ch).wait_send()
    for part in (qkv_s, fc_s, proj_s, out_s, proj_c, fc_c, qkv_c):
        part.finish()
    net.finish()


def block_call(nz, **operands):
    def vm(*shape, kind=BF):
        return pltpu.VMEM(shape, kind)

    outs = dict(
        output=((128, 768), BF), input_grad=((128, 768), BF), qkv_o=((4, 48, 576), BF),
        fc_o=((4, 48, 768), BF), proj_o=((192, 768), BF), out_o=((48, 768), BF), vec_o=((16, 768), F32),
    )
    f = lambda *shape: vm(*shape, kind=F32)
    keys = 512 * nz
    scratch = dict(
        qkv_raw=vm(48, 2304), fc_raw=vm(48, 3072), qkv_pre=vm(4, 48, 576), fc_pre=vm(4, 48, 768),
        vec_f32=f(16, 768), bias_f32=f(8, 256), vec_pre=vm(16, 768),
        pos_row=pltpu.VMEM((1, keys), jnp.int32), pos_col=pltpu.VMEM((keys, 1), jnp.int32),
        w_qkv=vm(768, 576), w_fc=vm(768, 768), w_proj=vm(768, 768), w_out=vm(768, 768), w_outp=vm(1024, 768),
        vec_land_z=vm(nz - 1, 16, 768), vec_u=vm(16, 768), vec_land_p=vm(3, 16, 768), vec=f(16, 768),
        x_all=vm(512, 768), cot_all=vm(512, 768), ln_all=vm(512, 768), lm_all=vm(512, 768),
        qm=vm(3, 512, 128), kv_all=vm(nz, 512, 384), s_buf=f(512, 512), pt=vm(nz * 3, 512, 512),
        m_run=f(3, 1, 512), l_run=f(3, 1, 512), l_inv=f(3, 1, 512), m_at=f(nz * 3, 1, 512), o_t=f(3, 128, 512),
        att_t=f(2, 128, 512), att=vm(512, 256), merged=vm(4, 128, 256),
        resid=f(128, 768), normed_mid=f(128, 768), inverse_mid=f(128, 1), slope=f(512, 768),
        act=vm(512, 768), grad_pre=vm(512, 768), fcb=f(1, 768), vec_g=f(16, 768),
        gm_part=vm(4, 128, 768), gm_c=vm(2, 128, 768), gm_mid=vm(128, 768), gm_y=vm(128, 768),
        br_part=vm(4, 128, 768), br_c=vm(2, 128, 768), br_mid=vm(128, 768), br_y=vm(128, 768),
        gi_part=vm(4, 128, 768), gi_c=vm(2, 128, 768), gi_mid=vm(128, 768), gi_y=vm(128, 768),
        grad_resid=f(128, 768), gb=vm(128, 768), gmer=vm(4, 128, 256), ga=vm(512, 256), gam=vm(3, 512, 128),
        delta=f(3, 1, 512), ds=vm(3, 512, 512), dq_t=f(3, 128, 512), dkv=f(512, 384),
        chain=vm(2 * (nz - 1), 512, 384), chain_land=vm(2 * (nz - 1), 512, 384), gqkv=vm(512, 576),
        qkv_g=vm(768, 576), fc_g=vm(768, 768), proj_g=vm(768, 768), out_g=vm(2, 2, 192, 768),
        qkv_x=vm(nz, 96, 576), fc_x=vm(nz, 96, 768), proj_x=vm(nz, 96, 768),
        qkv_m=vm(nz, 96, 576), fc_m=vm(nz, 96, 768), proj_m=vm(nz, 96, 768),
        qkv_z=vm(nz - 1, 96, 576), fc_z=vm(nz - 1, 96, 768), proj_z=vm(nz - 1, 96, 768),
        qkv_r=vm(96, 576), fc_r=vm(96, 768), proj_r=vm(96, 768), acc=f(96, 768), acc_q=f(96, 576),
        qkv_f=vm(96, 576), fc_f=vm(96, 768), proj_f=vm(96, 768),
        og_c=vm(2, 192, 768), og_1=vm(2, 192, 768), og_y=vm(192, 768), og_2=vm(192, 768),
        og_x=vm(192, 384), og_3=vm(192, 384), og_z=vm(nz - 1, 48, 384),
        late=f(8, 768), late_p=f(7, 8, 768), late_1=f(8, 768), late_z=f(nz - 1, 8, 768),
        vg_p=f(3, 16, 768), vg_1=f(16, 768), vg_z=f(nz - 1, 16, 768), vg_2=f(16, 768), vg_x=f(16, 768),
        send_sem=pltpu.SemaphoreType.DMA((112,)), recv_sem=pltpu.SemaphoreType.DMA((112,)),
        sp_send=pltpu.SemaphoreType.DMA((32,)), sp_recv=pltpu.SemaphoreType.DMA((32,)),
        co_send=pltpu.SemaphoreType.DMA((27,)), co_recv=pltpu.SemaphoreType.DMA((27,)),
        local_sem=pltpu.SemaphoreType.DMA((6,)),
        kv_send=pltpu.SemaphoreType.DMA((6 * nz,)), kv_recv=pltpu.SemaphoreType.DMA((6 * nz,)),
        ch_send=pltpu.SemaphoreType.DMA((6 * nz,)), ch_recv=pltpu.SemaphoreType.DMA((6 * nz,)),
        f_send=pltpu.SemaphoreType.DMA((8,)), f_recv=pltpu.SemaphoreType.DMA((8,)),
    )
    names = [*operands, *outs, *scratch]
    places = {name: pl.BlockSpec(memory_space=pl.ANY) for name in ("x_in", "cot_in", "qkv_in", "fc_in", "out_in", "proj_in")}
    places["order_in"] = pl.BlockSpec(memory_space=pltpu.SMEM)

    def kernel(*refs):
        block_kernel(nz, types.SimpleNamespace(**dict(zip(names, refs, strict=True))))

    got = pl.pallas_call(
        kernel,
        out_shape=tuple(jax.ShapeDtypeStruct(*s) for s in outs.values()),
        in_specs=[places.get(name, VSPEC) for name in operands],
        out_specs=(VSPEC,) * len(outs),
        scratch_shapes=list(scratch.values()),
        compiler_params=pltpu.CompilerParams(
            collective_id=0, has_side_effects=True, vmem_limit_bytes=60 * 2**20
        ),
        name="transformer_block",
    )(*operands.values())
    return dict(zip(outs, got, strict=True))


def hand_over_kernel(nz, output, input_grad, qkv_o, fc_o, proj_o, out_o, vec_o,
                     output_f, input_grad_f, gains_f, biases_f, mid_f, vb_f, qkv_f, out_f, fc_f, fcb_f, proj_f):
    output_f[...] = output[...]
    input_grad_f[...] = input_grad[...]
    gains_f[...] = vec_o[0:2, 0:48]
    biases_f[0:1, :] = vec_o[2:3, 0:48]
    biases_f[1:2, :] = vec_o[6:7, 0:48]
    biases_f[2:4, :] = vec_o[3:5, 0:48]
    mid_f[...] = vec_o[5:6, 0:48]
    vb_f[...] = vec_o[7:8, 0:48]
    fcb_f[...] = vec_o[8:9, 0:192]
    out_f[...] = out_o[...].astype(F32)
    proj_f[...] = proj_o[...].astype(F32)
    for g in range(4):
        for t in range(3):
            qkv_f[:, 768 * t + 192 * g:768 * t + 192 * g + 128] = qkv_o[g, :, 128 * t:128 * t + 128].astype(F32)
        for at, t in ((384, 1), (448, 2), (512, 0)):
            qkv_f[:, 768 * t + 192 * g + 128:768 * t + 192 * g + 192] = qkv_o[g, :, at:at + 64].astype(F32)
        for zz in range(nz):
            fc_f[:, 768 * zz + 192 * g:768 * zz + 192 * g + 192] = fc_o[g, :, 192 * zz:192 * zz + 192].astype(F32)


def hand_over(nz, got):
    shapes = [((128, 768), BF), ((128, 768), BF), ((2, 48), F32), ((4, 48), F32), ((1, 48), F32), ((1, 48), F32),
              ((48, 2304), F32), ((48, 768), F32), ((48, 3072), F32), ((1, 192), F32), ((192, 768), F32)]
    return pl.pallas_call(
        functools.partial(hand_over_kernel, nz),
        out_shape=tuple(jax.ShapeDtypeStruct(*s) for s in shapes),
        in_specs=[VSPEC] * len(got),
        out_specs=(VSPEC,) * len(shapes),
        compiler_params=pltpu.CompilerParams(vmem_limit_bytes=60 * 2**20),
        name="hand_over",
    )(*got.values())


def device_fast(nz, inputs, stretch_order, norm_gains, biases, mid_shift, value_bias, qkv_weight, out_weight, fc_weight, fc_bias, proj_weight, cotangent):
    got = block_call(
        nz,
        x_in=inputs[0],
        cot_in=cotangent[0],
        qkv_in=qkv_weight,
        fc_in=fc_weight,
        out_in=out_weight,
        proj_in=proj_weight,
        gains_in=norm_gains,
        biases_in=biases,
        mid_in=mid_shift[None],
        vb_in=value_bias[None],
        fcb_in=fc_bias[None],
        order_in=stretch_order,
    )
    output, input_grad, gains, rows, mid, vb, qkv, out, fc, fcb, proj = hand_over(nz, got)
    return output[None], input_grad[None], gains, rows, mid[0], vb[0], qkv, out, fc, fcb[0], proj


def solution(mesh):
    placed = (
        P("dp", ("blk", "uly"), None),
        P("dp", None),
        P(None, ("blk", "uly")),
        P(None, ("blk", "uly")),
        P(("blk", "uly")),
        P(("blk", "uly")),
        P(("blk", "uly"), None),
        P(("blk", "uly"), None),
        P(("blk", "uly"), None),
        P(("blk", "uly")),
        P(("blk", "uly"), None),
        P("dp", ("blk", "uly"), None),
    )
    sizes = dict(mesh.shape)
    nz = sizes["blk"]
    fast = sizes["uly"] == 4 and sizes["dp"] == 2 and nz == 4
    chosen = functools.partial(device_fast, nz) if fast else per_device
    return jax.shard_map(
        chosen,
        mesh=mesh,
        in_specs=placed,
        out_specs=(
            P("dp", ("blk", "uly"), None),
            P("dp", ("blk", "uly"), None),
            P(None, ("blk", "uly")),
            P(None, ("blk", "uly")),
            P(("blk", "uly")),
            P(("blk", "uly")),
            P(("blk", "uly"), None),
            P(("blk", "uly"), None),
            P(("blk", "uly"), None),
            P(("blk", "uly")),
            P(("blk", "uly"), None),
        ),
        check_vma=False,
    )
```

```python
import functools
import math
import types

import jax
import jax.numpy as jnp
from jax import lax
from jax.experimental import pallas as pl
from jax.experimental.pallas import tpu as pltpu
from jax.sharding import PartitionSpec as P

HEADS = 12


masked_score = -1e30


def layer_norm(values, gain, shift):
    center = values - jnp.mean(values, -1, keepdims=True)
    inverse = lax.rsqrt(jnp.mean(center * center, -1, keepdims=True) + 1e-05)
    normed = center * inverse
    return (normed * gain + shift, normed, inverse)


def norm_back(grad_out, normed, inverse, gain):
    scaled = grad_out * gain
    mean_plain = jnp.mean(scaled, -1, keepdims=True)
    mean_mixed = jnp.mean(scaled * normed, -1, keepdims=True)
    return inverse * (scaled - mean_plain - normed * mean_mixed)


def sweep(step_fn, carried, parts):
    row_count = parts[0].shape[1]
    sweep_rows = math.gcd(row_count, 1024)

    def turn(inner, turn_number):
        offset = turn_number * sweep_rows
        blocks = tuple((lax.dynamic_slice_in_dim(part, offset, sweep_rows, 1) for part in parts))
        return (step_fn(inner, blocks, offset), None)

    result, _ = lax.scan(turn, carried, jnp.arange(row_count // sweep_rows, dtype=jnp.int32))
    return result


def per_device(
    inputs,
    stretch_order,
    norm_gains,
    biases,
    mid_shift,
    value_bias,
    qkv_weight,
    out_weight,
    fc_weight,
    fc_bias,
    proj_weight,
    cotangent,
):
    fp32 = jnp.float32
    bf16 = jnp.bfloat16
    gain_rows, shifts, mid_gathered, value_shift, w_qkv, w_out, w_fc, b_fc, w_proj = (
        lax.all_gather(norm_gains, ("blk", "uly"), axis=1, tiled=True),
        lax.all_gather(biases, ("blk", "uly"), axis=1, tiled=True),
        lax.all_gather(mid_shift, ("blk", "uly"), axis=0, tiled=True),
        lax.all_gather(value_bias, ("blk", "uly"), axis=0, tiled=True),
        lax.all_gather(qkv_weight, ("blk", "uly"), axis=0, tiled=True),
        lax.all_gather(out_weight, ("blk", "uly"), axis=0, tiled=True),
        lax.all_gather(fc_weight, ("blk", "uly"), axis=0, tiled=True),
        lax.all_gather(fc_bias, ("blk", "uly"), axis=0, tiled=True),
        lax.all_gather(proj_weight, ("blk", "uly"), axis=0, tiled=True),
    )
    gain_rows = gain_rows.astype(fp32)
    shifts = shifts.astype(fp32)
    mid_gathered = mid_gathered.astype(fp32)
    seq_count, row_len, width = inputs.shape
    uly_count = lax.axis_size("uly")
    local_heads = HEADS // uly_count
    head_dim = width // HEADS
    head_span = local_heads * head_dim
    block_rows = uly_count * row_len
    half_rows = row_len // 2
    seq_len = stretch_order.shape[1] * half_rows
    score_scale = head_dim ** (-0.5)
    tokens = inputs.astype(fp32).reshape(seq_count * row_len, width)
    ln_in, normed_in, inverse_in = layer_norm(tokens, gain_rows[0], shifts[0])
    ln_in = ln_in.astype(bf16)
    qkv_shift = jnp.concatenate([shifts[1], jnp.zeros((width,), fp32), value_shift.astype(fp32)])
    qkv = (jnp.dot(ln_in, w_qkv, preferred_element_type=fp32) + qkv_shift).astype(bf16)
    head_data = lax.all_to_all(
        qkv.reshape(seq_count, row_len, 3, uly_count, head_span),
        "uly",
        split_axis=3,
        concat_axis=1,
        tiled=True,
    )
    queries = head_data[:, :, 0, 0].reshape(seq_count, block_rows, local_heads, head_dim)
    key_rows = head_data[:, :, 1, 0]
    value_rows = head_data[:, :, 2, 0]
    positions = (
        stretch_order[:, :, None] * half_rows
        + jnp.arange(half_rows, dtype=jnp.int32)[None, None, :]
    ).reshape(seq_count, seq_len)
    query_pos = lax.dynamic_slice_in_dim(
        positions, lax.axis_index("blk") * block_rows, block_rows, 1
    )

    def score_block(key_part, key_start):
        part_rows = key_part.shape[1]
        key_pos = lax.dynamic_slice_in_dim(positions, key_start, part_rows, 1)
        scores = (
            jnp.einsum(
                "sqhd,skhd->shqk",
                queries,
                key_part.reshape(seq_count, part_rows, local_heads, head_dim),
                preferred_element_type=fp32,
            )
            * score_scale
        )
        causal = query_pos[:, None, :, None] >= key_pos[:, None, None, :]
        return (scores, causal)

    def stats_step(carried, blocks, key_start):
        row_max, row_total = carried
        scores, causal = score_block(blocks[0], key_start)
        new_max = jnp.maximum(row_max, jnp.max(jnp.where(causal, scores, masked_score), -1))
        row_total = row_total * jnp.exp(row_max - new_max) + jnp.sum(
            jnp.where(causal, jnp.exp(scores - new_max[..., None]), 0.0), -1
        )
        return (new_max, row_total)

    def softmax_of(scores, causal, row_max, row_total):
        return jnp.where(causal, jnp.exp(scores - row_max[..., None]) / row_total[..., None], 0.0)

    def make_output_step(row_max, row_total):

        def output_step(acc_out, blocks, key_start):
            scores, causal = score_block(blocks[0], key_start)
            attn_probs = softmax_of(scores, causal, row_max, row_total).astype(bf16)
            part_rows = blocks[1].shape[1]
            value_part = blocks[1].reshape(seq_count, part_rows, local_heads, head_dim)
            return acc_out + jnp.einsum(
                "shqk,skhd->sqhd", attn_probs, value_part, preferred_element_type=fp32
            )

        return output_step

    stats_init = (
        jnp.full((seq_count, local_heads, block_rows), masked_score, fp32),
        jnp.zeros((seq_count, local_heads, block_rows), fp32),
    )
    empty_out = jnp.zeros((seq_count, block_rows, local_heads, head_dim), fp32)
    all_keys, all_values = (
        lax.all_gather(key_rows, "blk", axis=1, tiled=True),
        lax.all_gather(value_rows, "blk", axis=1, tiled=True),
    )
    row_max, row_total = sweep(stats_step, stats_init, (all_keys,))
    attended = sweep(make_output_step(row_max, row_total), empty_out, (all_keys, all_values))
    attended_low = attended.astype(bf16).reshape(seq_count, block_rows, 1, head_span)
    merged = lax.all_to_all(attended_low, "uly", split_axis=1, concat_axis=2, tiled=True).reshape(
        seq_count * row_len, width
    )
    resid = tokens + (jnp.dot(merged, w_out, preferred_element_type=fp32) + shifts[2])
    ln_mid, normed_mid, inverse_mid = layer_norm(resid, gain_rows[1], mid_gathered)
    ln_mid = ln_mid.astype(bf16)
    pre_act = jnp.dot(ln_mid, w_fc, preferred_element_type=fp32) + b_fc.astype(fp32)

    def gelu_piece(pre_values):
        return jax.nn.gelu(pre_values, approximate=True)

    act, gelu_back = jax.vjp(gelu_piece, pre_act)
    act = act.astype(bf16)
    result = resid + (jnp.dot(act, w_proj, preferred_element_type=fp32) + shifts[3])
    grad_low = cotangent.reshape(seq_count * row_len, width)
    grad_out = grad_low.astype(fp32)
    proj_grad = jnp.einsum("ta,tb->ab", act, grad_low, preferred_element_type=fp32)
    proj_shift_grad = jnp.sum(grad_out, 0)
    grad_act = jnp.einsum("tb,ab->ta", grad_low, w_proj, preferred_element_type=fp32)
    grad_pre = gelu_back(grad_act)[0].astype(bf16)
    fc_grad = jnp.einsum("ta,tb->ab", ln_mid, grad_pre, preferred_element_type=fp32)
    fc_shift_grad = jnp.sum(grad_pre.astype(fp32), 0)
    grad_mid = jnp.einsum("tb,ab->ta", grad_pre, w_fc, preferred_element_type=fp32)
    gain_mid_grad = jnp.sum(grad_mid * normed_mid, 0)
    shift_mid_grad = jnp.sum(grad_mid, 0)
    grad_resid = grad_out + norm_back(grad_mid, normed_mid, inverse_mid, gain_rows[1])
    grad_branch = grad_resid.astype(bf16)
    out_grad = jnp.einsum("ta,tb->ab", merged, grad_branch, preferred_element_type=fp32)
    out_shift_grad = jnp.sum(grad_branch.astype(fp32), 0)
    grad_merged = jnp.einsum("tb,ab->ta", grad_branch, w_out, preferred_element_type=fp32).astype(
        bf16
    )
    grad_att = lax.all_to_all(
        grad_merged.reshape(seq_count, row_len, uly_count, head_span),
        "uly",
        split_axis=2,
        concat_axis=1,
        tiled=True,
    )
    grad_att = grad_att.reshape(seq_count, block_rows, local_heads, head_dim)
    delta = jnp.transpose(jnp.sum(grad_att.astype(fp32) * attended, -1), (0, 2, 1))
    back_keys, back_values = (all_keys, all_values)
    sweep_rows = math.gcd(seq_len, 1024)

    def query_terms(offset):
        key_part = lax.dynamic_slice_in_dim(back_keys, offset, sweep_rows, 1)
        value_part = lax.dynamic_slice_in_dim(back_values, offset, sweep_rows, 1)
        scores, causal = score_block(key_part, offset)
        attn_probs = softmax_of(scores, causal, row_max, row_total)
        key_heads = key_part.reshape(seq_count, sweep_rows, local_heads, head_dim)
        value_heads = value_part.reshape(seq_count, sweep_rows, local_heads, head_dim)
        grad_probs = jnp.einsum(
            "sqhd,skhd->shqk", grad_att, value_heads, preferred_element_type=fp32
        )
        grad_scores = (attn_probs * (grad_probs - delta[..., None])).astype(bf16)
        query_term = (
            jnp.einsum("shqk,skhd->sqhd", grad_scores, key_heads, preferred_element_type=fp32)
            * score_scale
        )
        return (query_term, grad_scores, attn_probs.astype(bf16))

    query_init = jnp.zeros((seq_count, block_rows, local_heads, head_dim), fp32)

    def back_step(carried, turn_number):
        grad_query, kv_buffer = carried
        offset = turn_number * sweep_rows
        query_term, grad_scores, probs_low = query_terms(offset)
        grad_key = (
            jnp.einsum("shqk,sqhd->skhd", grad_scores, queries, preferred_element_type=fp32)
            * score_scale
        )
        grad_value = jnp.einsum("shqk,sqhd->skhd", probs_low, grad_att, preferred_element_type=fp32)
        kv_pair = jnp.stack(
            [
                grad_key.reshape(seq_count, sweep_rows, head_span),
                grad_value.reshape(seq_count, sweep_rows, head_span),
            ],
            2,
        )
        kv_buffer = lax.dynamic_update_slice_in_dim(kv_buffer, kv_pair, offset, 1)
        return ((grad_query + query_term, kv_buffer), None)

    back_init = (query_init, jnp.zeros((seq_count, seq_len, 2, head_span), fp32))
    back_done, _ = lax.scan(
        back_step, back_init, jnp.arange(seq_len // sweep_rows, dtype=jnp.int32)
    )
    grad_query, kv_buffer = back_done
    kv_summed = lax.psum_scatter(
        kv_buffer.astype(jnp.bfloat16), "blk", scatter_dimension=1, tiled=True
    ).astype(jnp.float32)
    grad_heads = jnp.concatenate(
        [
            grad_query.reshape(seq_count, block_rows, 1, head_span).astype(bf16),
            kv_summed.astype(bf16),
        ],
        2,
    )
    grad_qkv = lax.all_to_all(
        grad_heads.reshape(seq_count, block_rows, 3, 1, head_span),
        "uly",
        split_axis=1,
        concat_axis=3,
        tiled=True,
    )
    grad_qkv = grad_qkv.reshape(seq_count * row_len, 3 * width)
    qkv_grad = jnp.einsum("ta,tb->ab", ln_in, grad_qkv, preferred_element_type=fp32)
    column_sums = jnp.sum(grad_qkv.astype(fp32), 0)
    grad_in_norm = jnp.einsum("tb,ab->ta", grad_qkv, w_qkv, preferred_element_type=fp32)
    gain_in_grad = jnp.sum(grad_in_norm * normed_in, 0)
    shift_in_grad = jnp.sum(grad_in_norm, 0)
    grad_input = grad_resid + norm_back(grad_in_norm, normed_in, inverse_in, gain_rows[0])
    gains_grad = jnp.stack([gain_in_grad, gain_mid_grad])
    biases_grad = jnp.stack([shift_in_grad, column_sums[:width], out_shift_grad, proj_shift_grad])
    value_grad = column_sums[2 * width :]
    shard_grads = (
        lax.psum_scatter(gains_grad, ("blk", "uly"), scatter_dimension=1, tiled=True),
        lax.psum_scatter(biases_grad, ("blk", "uly"), scatter_dimension=1, tiled=True),
        lax.psum_scatter(shift_mid_grad, ("blk", "uly"), scatter_dimension=0, tiled=True),
        lax.psum_scatter(value_grad, ("blk", "uly"), scatter_dimension=0, tiled=True),
        lax.psum_scatter(qkv_grad, ("blk", "uly"), scatter_dimension=0, tiled=True),
        lax.psum_scatter(out_grad, ("blk", "uly"), scatter_dimension=0, tiled=True),
        lax.psum_scatter(fc_grad, ("blk", "uly"), scatter_dimension=0, tiled=True),
        lax.psum_scatter(fc_shift_grad, ("blk", "uly"), scatter_dimension=0, tiled=True),
        lax.psum_scatter(proj_grad, ("blk", "uly"), scatter_dimension=0, tiled=True),
    )
    shard_grads = (
        lax.psum(shard_grads[0].astype(jnp.bfloat16), "dp").astype(jnp.float32),
        lax.psum(shard_grads[1].astype(jnp.bfloat16), "dp").astype(jnp.float32),
        lax.psum(shard_grads[2].astype(jnp.bfloat16), "dp").astype(jnp.float32),
        lax.psum(shard_grads[3].astype(jnp.bfloat16), "dp").astype(jnp.float32),
        lax.psum(shard_grads[4].astype(jnp.bfloat16), "dp").astype(jnp.float32),
        lax.psum(shard_grads[5].astype(jnp.bfloat16), "dp").astype(jnp.float32),
        lax.psum(shard_grads[6].astype(jnp.bfloat16), "dp").astype(jnp.float32),
        lax.psum(shard_grads[7].astype(jnp.bfloat16), "dp").astype(jnp.float32),
        lax.psum(shard_grads[8].astype(jnp.bfloat16), "dp").astype(jnp.float32),
    )
    output = result.astype(bf16).reshape(seq_count, row_len, width)
    input_grad = grad_input.astype(bf16).reshape(seq_count, row_len, width)
    return (
        output,
        input_grad,
        shard_grads[0],
        shard_grads[1],
        shard_grads[2],
        shard_grads[3],
        shard_grads[4],
        shard_grads[5],
        shard_grads[6],
        shard_grads[7],
        shard_grads[8],
    )


MESH = pl.DeviceIdType.MESH
BF = jnp.bfloat16
F32 = jnp.float32
VSPEC = pl.BlockSpec(memory_space=pltpu.VMEM)
GELU_IN = math.sqrt(2.0 / math.pi)


class Net:
    def __init__(self, send_sem, recv_sem, nz):
        self.send_sem, self.recv_sem = send_sem, recv_sem
        self.count = 0
        self.sent = []
        self.nz = nz
        self.x = lax.axis_index("dp")
        self.z = lax.axis_index("blk")
        self.u = lax.axis_index("uly")

    def send(self, src, dst, dev):
        k = self.count
        self.count += 1
        copy = pltpu.make_async_remote_copy(
            src_ref=src,
            dst_ref=dst,
            send_sem=self.send_sem.at[k],
            recv_sem=self.recv_sem.at[k],
            device_id=dev,
            device_id_type=MESH,
        )
        copy.start()
        self.sent.append(copy)
        return copy

    def plane(self, m):
        return (self.x, self.z, self.u ^ m)

    def other_x(self):
        return (1 - self.x, self.z, self.u)

    def zplus(self, d):
        return lax.rem(self.z + d, self.nz)

    def line(self, d):
        return (self.x, self.zplus(d), self.u)

    def hail(self):
        barrier = pltpu.get_barrier_semaphore()
        near = [self.plane(m) for m in (1, 2, 3)] + [self.other_x()]
        near += [self.line(d) for d in range(1, self.nz)]
        near += [(1 - self.x, self.z, self.u ^ m) for m in (1, 2, 3)]
        for dev in near:
            pl.semaphore_signal(barrier, inc=1, device_id=dev, device_id_type=MESH)
        self.met = len(near)

    def meet(self):
        pl.semaphore_wait(pltpu.get_barrier_semaphore(), self.met)

    def finish(self):
        for copy in self.sent:
            copy.wait_send()


class Line:
    def __init__(self, net, send_sem, recv_sem, base):
        self.net, self.send_sem, self.recv_sem, self.base = net, send_sem, recv_sem, base
        self.z = net.z
        self.inner = jnp.logical_and(net.z >= 1, net.z <= net.nz - 2)
        self.far = net.nz - 1 - net.z

    def copy(self, src, dst, k, target, recv=None):
        target = jnp.clip(target, 0, self.net.nz - 1)
        return pltpu.make_async_remote_copy(
            src_ref=src,
            dst_ref=dst,
            send_sem=self.send_sem.at[self.base + k],
            recv_sem=self.recv_sem.at[self.base + (k if recv is None else recv)],
            device_id=(self.net.x, target, self.net.u),
            device_id_type=MESH,
        )

    def target(self, d):
        return lax.rem(self.z + d, self.net.nz)

    def source(self, d):
        return lax.rem(self.z - d + self.net.nz, self.net.nz)


class Spread(Line):
    def __init__(self, net, send_sem, recv_sem, base, block):
        super().__init__(net, send_sem, recv_sem, base)
        self.block = block

    def direct(self, d):
        return self.copy(self.block(self.z), self.block(self.z), d, self.target(d))

    def start(self):
        for d in (2, 1, 3):
            if d == 2:
                self.direct(d).start()
            else:
                @pl.when(jnp.logical_or(self.inner, self.target(d) != self.far))
                def _():
                    self.direct(d).start()

    def relay_copy(self):
        block = self.block(self.source(2))
        target = jnp.where(self.z == 2, 3, 0)
        return self.copy(block, block, 4, target, jnp.where(self.z == 2, 3, 1))

    def across(self, d):
        block = self.block(self.source(d))
        return pltpu.make_async_remote_copy(
            src_ref=block, dst_ref=block, send_sem=self.send_sem.at[self.base + 4 + d],
            recv_sem=self.recv_sem.at[self.base + 4 + d], device_id=self.net.other_x(), device_id_type=MESH)

    def arrive(self, d):
        block = self.block(self.source(d))
        self.copy(block, block, d, self.z).wait_recv()

    def relay(self):
        self.arrive(2)

        @pl.when(self.inner)
        def _():
            self.relay_copy().start()

        self.across(2).start()

    def rest(self):
        first = jnp.where(self.z == 0, 3, 1)
        for d in (first, 4 - first):
            self.arrive(d)
            self.across(d).start()

    def finish_recv(self):
        for d in (2, 1, 3):
            self.across(d).wait_recv()

    def finish(self):
        self.direct(2).wait_send()
        for d in (1, 3):
            @pl.when(jnp.logical_or(self.inner, self.target(d) != self.far))
            def _():
                self.direct(d).wait_send()
        for d in (1, 2, 3):
            self.across(d).wait_send()

        @pl.when(self.inner)
        def _():
            self.relay_copy().wait_send()


class Collect(Line):
    def __init__(self, net, send_sem, recv_sem, base, theirs, ours, land_x, mine, land_z, relay):
        super().__init__(net, send_sem, recv_sem, base)
        self.theirs, self.ours = theirs, ours
        self.land_x, self.mine, self.land_z, self.relay = land_x, mine, land_z, relay

    def order(self, i):
        pick = lambda table: table[i]
        z = self.z
        return jnp.where(z == 0, 3 - i, jnp.where(z == 3, i, jnp.where(z == 1, pick((0, 2, 3, 1)), pick((3, 1, 0, 2)))))

    def across(self, i):
        zz = self.order(i)
        return pltpu.make_async_remote_copy(
            src_ref=self.theirs(zz), dst_ref=self.land_x.at[zz], send_sem=self.send_sem.at[self.base + 5 + i],
            recv_sem=self.recv_sem.at[self.base + 5 + i], device_id=self.net.other_x(), device_id_type=MESH)

    def start(self):
        for i in range(4):
            self.across(i).start()

    def own(self, i):
        zz = self.order(i)
        self.across(i).wait_recv()
        self.mine[zz] = (self.ours(zz) + self.land_x[zz].astype(F32)).astype(BF)

    def direct(self, zz):
        d = lax.rem(zz - self.z + 4, 4)
        return self.copy(self.mine.at[zz], self.land_z.at[d - 1], d, zz)

    def to_neighbour(self):
        return self.copy(self.mine.at[self.far], self.relay, 4, jnp.where(self.z == 0, 1, 2))

    def part(self, i):
        self.own(i)
        if i == 0:
            @pl.when(self.inner)
            def _():
                self.direct(self.order(0)).start()

            @pl.when(jnp.logical_not(self.inner))
            def _():
                self.to_neighbour().start()
        elif i == 1:
            self.direct(self.order(1)).start()
        elif i == 2:
            @pl.when(jnp.logical_not(self.inner))
            def _():
                self.direct(self.order(2)).start()

    def first(self):
        for i in range(4):
            self.part(i)

    def second(self):
        @pl.when(self.inner)
        def _():
            zz = self.order(2)
            self.copy(self.relay, self.relay, 4, self.z).wait_recv()
            self.mine[zz] = (self.mine[zz].astype(F32) + self.relay[...].astype(F32)).astype(BF)
            self.direct(zz).start()

    def total(self, final):
        skip = jnp.where(self.z == 0, 1, 3)
        final[...] = self.mine[self.z].astype(F32)
        for d in (1, 2, 3):
            @pl.when(jnp.logical_or(self.inner, skip != d))
            def _():
                self.copy(self.land_z.at[d - 1], self.land_z.at[d - 1], d, self.z).wait_recv()
                final[...] += self.land_z[d - 1].astype(F32)

    def finish(self):
        for i in range(4):
            self.across(i).wait_send()

        @pl.when(self.inner)
        def _():
            for i in range(3):
                self.direct(self.order(i)).wait_send()

        @pl.when(jnp.logical_not(self.inner))
        def _():
            self.to_neighbour().wait_send()
            for i in (1, 2):
                self.direct(self.order(i)).wait_send()


def rows_at(start, count):
    return pl.ds(pl.multiple_of(start, 16), count)


def dot_nn(a, b):
    return jnp.dot(a, b, preferred_element_type=F32)


def dot_nt(a, b):
    return lax.dot_general(a, b, (((1,), (1,)), ((), ())), preferred_element_type=F32)


def dot_tn(a, b):
    return lax.dot_general(a, b, (((0,), (0,)), ((), ())), preferred_element_type=F32)


def loop(count, body):
    def step(i, carry):
        body(i)
        return carry

    lax.fori_loop(0, count, step, 0)


def block_kernel(nz, refs):
    r = refs
    net = Net(r.send_sem, r.recv_sem, nz)
    x, z, u = net.x, net.z, net.u
    y, c = u // 2, lax.rem(u, 2)
    own48 = (4 * z + u) * 48
    tile = lambda t: rows_at(128 * t, 128)
    half_cols = lambda which: pl.ds(pl.multiple_of(384 * which, 128), 384)
    lane = lambda shape: lax.broadcasted_iota(jnp.int32, shape, 1)

    x_own, cot_own = r.x_all.at[tile(u)], r.cot_all.at[tile(u)]
    local = [
        pltpu.make_async_copy(r.qkv_in, r.qkv_raw, r.local_sem.at[0]),
        pltpu.make_async_copy(r.fc_in, r.fc_raw, r.local_sem.at[1]),
        pltpu.make_async_copy(r.x_in, x_own, r.local_sem.at[2]),
        pltpu.make_async_copy(r.out_in, r.w_out.at[rows_at(own48, 48)], r.local_sem.at[3]),
        pltpu.make_async_copy(r.proj_in, r.w_proj.at[rows_at(192 * z, 192)], r.local_sem.at[4]),
        pltpu.make_async_copy(r.cot_in, cot_own, r.local_sem.at[5]),
    ]
    local[0].start()
    local[2].start()
    net.hail()
    local[0].wait()
    for g in range(4):
        for t in range(3):
            r.qkv_pre[g, :, 128 * t:128 * t + 128] = r.qkv_raw[:, 768 * t + 192 * g:768 * t + 192 * g + 128]
        for at, t in ((384, 1), (448, 2), (512, 0)):
            r.qkv_pre[g, :, at:at + 64] = r.qkv_raw[:, 768 * t + 192 * g + 128:768 * t + 192 * g + 192]
    r.w_qkv[rows_at(own48, 48), :] = r.qkv_pre[u]
    net.meet()

    def plane_gather_start(own, full):
        return [net.send(own, full.at[tile(u)], net.plane(m)) for m in (2, 1)]

    def plane_gather_forward(sent, full):
        sent[0].wait_recv()
        sent.append(net.send(full.at[tile(u ^ 2)], full.at[tile(u ^ 2)], net.plane(1)))

    in_plane = lambda pre, full: [
        net.send(pre.at[u ^ m], full.at[rows_at(own48, 48)], net.plane(m)) for m in (1, 2, 3)
    ]
    block96 = lambda full: lambda j: full.at[rows_at(192 * j + 96 * x, 96)]
    spread = lambda base, block: Spread(net, r.sp_send, r.sp_recv, base, block)
    qkv_s = spread(0, block96(r.w_qkv))
    fc_s = spread(8, block96(r.w_fc))
    proj_s = spread(16, block96(r.w_proj))
    out_s = spread(24, lambda j: r.w_out.at[rows_at((4 * j + u) * 48, 48), half_cols(x)])
    qkv_p = in_plane(r.qkv_pre, r.w_qkv)
    local[2].wait()
    x_g = plane_gather_start(x_own, r.x_all)
    for i in (3, 1, 4, 5):
        local[i].start()
    vp = r.vec_f32
    vp[...] = jnp.zeros((16, 768), F32)
    vp[0:2, 0:48] = r.gains_in[...].astype(F32)
    vp[2:6, 0:48] = r.biases_in[...].astype(F32)
    vp[6:7, 0:48] = r.mid_in[...].astype(F32)
    vp[7:8, 0:48] = r.vb_in[...].astype(F32)
    bias = r.bias_f32
    bias[...] = jnp.zeros((8, 256), F32)
    bias[0:1, 0:48] = r.biases_in[1:2, :].astype(F32)
    bias[1:2, 0:48] = r.vb_in[...].astype(F32)
    bias[...] = pltpu.roll(bias[...], 48 * u, 1)
    vp[0:8, :] = pltpu.roll(vp[0:8, :], 48 * (4 * z + u), 1)
    vp[8:9, 0:192] = r.fcb_in[...].astype(F32)
    vp[9:10, 0:128] = bias[0:1, 0:128]
    vp[9:10, 256:384] = bias[1:2, 0:128]
    vp[9:10, 448:512] = bias[1:2, 128:192]
    vp[9:10, 512:576] = bias[0:1, 128:192]
    high = vp[8:16, :]
    row8 = lax.broadcasted_iota(jnp.int32, high.shape, 0)
    fcb_row = pltpu.roll(jnp.where(row8 == 0, high, 0.0), 192 * z, 1)
    bias_row = jnp.sum(jnp.where(row8 == 1, high, 0.0), 0, keepdims=True)
    vp[8:16, :] = fcb_row + jnp.where(row8 == 1 + z, bias_row, 0.0)
    r.vec_pre[...] = vp[...].astype(BF)
    vec_z = [net.send(r.vec_pre, r.vec_land_z.at[d - 1], net.line(d)) for d in range(1, nz)]
    for copy in qkv_p:
        copy.wait_recv()
    qkv_s.start()
    local[3].wait()
    out_s.start()
    total = r.vec_pre[...]
    for d in range(nz - 1):
        vec_z[d].wait_recv()
        total = total + r.vec_land_z[d]
    r.vec_u[...] = total
    vec_p = [net.send(r.vec_u, r.vec_land_p.at[m - 1], net.plane(m)) for m in (1, 2, 3)]
    plane_gather_forward(x_g, r.x_all)
    for i in (1, 4, 5):
        local[i].wait()
    for g in range(4):
        for zz in range(nz):
            r.fc_pre[g, :, 192 * zz:192 * zz + 192] = r.fc_raw[:, 768 * zz + 192 * g:768 * zz + 192 * g + 192]
    r.w_fc[rows_at(own48, 48), :] = r.fc_pre[u]
    inner64 = lax.broadcasted_iota(jnp.int32, (64, 1), 0)
    inner64_row = lax.broadcasted_iota(jnp.int32, (1, 64), 1)
    for i in range(8 * nz):
        first = r.order_in[0, i] * 64
        r.pos_col[64 * i:64 * i + 64, :] = first + inner64
        r.pos_row[:, 64 * i:64 * i + 64] = first + inner64_row
    fc_p = in_plane(r.fc_pre, r.w_fc)
    total = r.vec_u[...].astype(F32)
    row = lax.broadcasted_iota(jnp.int32, total.shape, 0)
    for m in range(3):
        vec_p[m].wait_recv()
        total = total + jnp.where(row == 8, 0.0, r.vec_land_p[m].astype(F32))
    r.vec[...] = total
    for copy in x_g[1:]:
        copy.wait_recv()
    gain = lambda i: r.vec[pl.ds(i, 1), :]

    def normalize(values):
        center = values - jnp.mean(values, -1, keepdims=True)
        inverse = lax.rsqrt(jnp.mean(center * center, -1, keepdims=True) + 1e-05)
        return center * inverse, inverse

    def ln_tile(t):
        normed, _ = normalize(r.x_all[tile(t), :].astype(F32))
        r.ln_all[tile(t), :] = (normed * gain(0) + gain(2)).astype(BF)

    loop(4, ln_tile)
    qkv_s.relay()
    qkv_s.rest()
    for copy in fc_p:
        copy.wait_recv()
    fc_s.start()
    cot_g = plane_gather_start(cot_own, r.cot_all)
    r.qm[2] = jnp.zeros((512, 128), BF)
    out_s.relay()
    out_s.rest()
    qkv_s.finish_recv()

    bias_u = jnp.sum(jnp.where(row == 9 + u, r.vec[...], 0.0), 0, keepdims=True)[:, 0:576]

    def qkv_tile(t):
        res = dot_nn(r.ln_all[tile(t), :], r.w_qkv[...]) + bias_u
        res = res.astype(BF)
        q01 = res[:, 0:128].astype(F32) * 0.125
        low = lane(q01.shape) < 64
        r.qm[0, tile(t), :] = jnp.where(low, q01, 0.0).astype(BF)
        r.qm[1, tile(t), :] = jnp.where(low, 0.0, q01).astype(BF)
        r.qm[2, tile(t), 0:64] = (res[:, 512:576].astype(F32) * 0.125).astype(BF)
        r.kv_all[z, tile(t), :] = res[:, 128:512]

    loop(4, qkv_tile)

    third = lambda ch: slice(128 * ch, 128 * ch + 128)

    def kv_copy(way, step, ch):
        block = z - step if way == 0 else z + step
        target = z + 1 if way == 0 else z - 1
        block, target = jnp.clip(block, 0, nz - 1), jnp.clip(target, 0, nz - 1)
        return pltpu.make_async_remote_copy(
            src_ref=r.kv_all.at[block, :, third(ch)], dst_ref=r.kv_all.at[block, :, third(ch)],
            send_sem=r.kv_send.at[(way * nz + step) * 3 + ch], recv_sem=r.kv_recv.at[(way * nz + step) * 3 + ch],
            device_id=(x, target, u), device_id_type=MESH)

    def kv_sends(way, step):
        if way == 0:
            return jnp.logical_and(z - step >= 0, z + 1 < nz)
        return jnp.logical_and(z + step < nz, z >= 1)

    def kv_start(step, ch, way):
        @pl.when(kv_sends(way, step))
        def _():
            kv_copy(way, step, ch).start()

    def attend(j):
        qp = r.pos_row[:, pl.ds(pl.multiple_of(512 * z, 128), 512)]
        for h in range(3):
            kc = 0 if h < 2 else 256
            vc = 128 if h < 2 else 256
            q = r.qm[h]

            def score(kt, top):
                s = dot_nt(r.kv_all[j, rows_at(128 * kt, 128), kc:kc + 128], q)
                kp = r.pos_col[pl.ds(pl.multiple_of(512 * j + 128 * kt, 128), 128), :]
                s = jnp.where(kp <= qp, s, -1e30)
                r.s_buf[rows_at(128 * kt, 128), :] = s
                return jnp.maximum(top, jnp.max(s, 0, keepdims=True))

            old = r.m_run[h]
            top = lax.fori_loop(0, 4, score, old, unroll=True)
            shrink = jnp.exp(old - top)

            def weigh(kt, got):
                p = jnp.exp(r.s_buf[rows_at(128 * kt, 128), :] - top)
                r.pt[j * 3 + h, rows_at(128 * kt, 128), :] = p.astype(BF)
                return got + jnp.sum(p, 0, keepdims=True)

            got = lax.fori_loop(0, 4, weigh, jnp.zeros((1, 512), F32), unroll=True)
            r.m_run[h] = top
            r.m_at[j * 3 + h] = top
            r.l_run[h] = r.l_run[h] * shrink + got
            r.o_t[h] = r.o_t[h] * shrink + dot_tn(r.kv_all[j, :, vc:vc + 128], r.pt[j * 3 + h])

    r.m_run[...] = jnp.full((3, 1, 512), -1e30, F32)
    r.l_run[...] = jnp.zeros((3, 1, 512), F32)
    r.o_t[...] = jnp.zeros((3, 128, 512), F32)
    for ch in range(3):
        for way in range(2):
            kv_start(0, ch, way)
    plane_gather_forward(cot_g, r.cot_all)
    attend(z)
    fc_s.relay()

    for step in range(1, nz):
        for ch in range(3):
            for way in range(2):
                @pl.when(z - step >= 0 if way == 0 else z + step < nz)
                def _():
                    kv_copy(way, step - 1, ch).wait_recv()

                if step < nz - 1:
                    kv_start(step, ch, way)
        if step == 1:
            fc_s.rest()
            out_s.finish_recv()
            out_rows = lambda zz, who: r.w_out.at[rows_at((4 * zz + who) * 48, 48)]
            out_y = [net.send(out_rows(zz, u), out_rows(zz, u), net.plane(2)) for zz in range(nz)]
            out_c = [net.send(out_rows(zz, u), out_rows(zz, u), net.plane(1)) for zz in range(nz)]
        if step == 2:
            for zz, copy in enumerate(out_y):
                copy.wait_recv()
                out_c.append(net.send(out_rows(zz, u ^ 2), out_rows(zz, u ^ 2), net.plane(1)))
        if step == nz - 1:
            proj_s.start()

        def either(way):
            j = jnp.where(way == 0, z - step, z + step)

            @pl.when(jnp.logical_and(j >= 0, j < nz))
            def _():
                attend(j)

        loop(2, either)

    rowi = lax.broadcasted_iota(jnp.int32, (128, 512), 0)
    r.l_inv[...] = 1.0 / r.l_run[...]
    r.att_t[0] = jnp.where(rowi < 64, r.o_t[0] * r.l_inv[0], r.o_t[1] * r.l_inv[1])
    r.att_t[1] = jnp.where(rowi < 64, 0.0, r.o_t[2] * r.l_inv[2])
    r.att[:, 0:128] = jnp.transpose(r.att_t[0]).astype(BF)
    r.att[:, 128:256] = jnp.transpose(r.att_t[1]).astype(BF)
    att_p = [net.send(r.att.at[tile(u ^ m)], r.merged.at[u], net.plane(m)) for m in (2, 3, 1)]
    r.merged[u] = r.att[tile(u), :]

    for copy in out_c:
        copy.wait_recv()
    for g in range(4):
        r.w_outp[256 * g:256 * g + 128, :] = r.w_out[192 * g:192 * g + 128, :]
        r.w_outp[256 * g + 128:256 * g + 192, :] = jnp.zeros((64, 768), BF)
        r.w_outp[256 * g + 192:256 * g + 256, :] = r.w_out[192 * g + 128:192 * g + 192, :]
    for copy in cot_g[1:]:
        copy.wait_recv()
    proj_s.relay()
    for copy in att_p:
        copy.wait_recv()
    resid = x_own[...].astype(F32) + gain(4)
    for g in range(4):
        resid = resid + dot_nn(r.merged[g], r.w_outp[256 * g:256 * g + 256, :])
    r.resid[...] = resid
    normed, inverse = normalize(resid)
    r.normed_mid[...] = normed
    r.inverse_mid[...] = inverse
    r.lm_all[tile(u), :] = (normed * gain(1) + gain(6)).astype(BF)
    lm_own = r.lm_all.at[tile(u)]
    lm_g = [net.send(lm_own, lm_own, net.plane(m)) for m in (2, 1)]
    fc_s.finish_recv()

    r.vec_g[...] = jnp.zeros((16, 768), F32)

    def mlp_front(t):
        rows = tile(t)
        pre = dot_nn(r.lm_all[rows, :], r.w_fc[...]) + gain(8)
        square = pre * pre
        th = jnp.tanh(GELU_IN * (pre * (1.0 + 0.044715 * square)))
        r.act[rows, :] = (0.5 * pre * (1.0 + th)).astype(BF)
        r.slope[rows, :] = 0.5 * (1.0 + th) + (0.5 * GELU_IN) * pre * (1.0 - th * th) * (1.0 + 0.134145 * square)

    def mlp_back(t):
        rows = tile(t)
        gp = (r.slope[rows, :] * dot_nt(r.cot_all[rows, :], r.w_proj[...])).astype(BF)
        r.grad_pre[rows, :] = gp
        r.fcb[...] += jnp.sum(gp.astype(F32), 0, keepdims=True)
        r.gm_part[t] = dot_nt(gp, r.w_fc[...]).astype(BF)

    r.fcb[...] = jnp.zeros((1, 768), F32)
    mlp_front(u)
    lm_g[1].wait_recv()
    mlp_front(u ^ 1)
    plane_gather_forward(lm_g, r.lm_all)

    def reduce_core(i, t, part, land_c):
        return net.send(part.at[t], land_c.at[i], net.plane(1))

    def reduce_y(copy, part, land_c, mid, land_y):
        copy.wait_recv()
        mid[...] = (part[u ^ 2].astype(F32) + land_c[0].astype(F32)).astype(BF)
        return net.send(mid, land_y, net.plane(2))

    def reduce_end(copy_c, copy_y, part, land_c, land_y):
        copy_c.wait_recv()
        copy_y.wait_recv()
        return part[u].astype(F32) + land_c[1].astype(F32) + land_y[...].astype(F32)

    mlp_front(u ^ 2)
    proj_s.rest()
    lm_g[2].wait_recv()
    mlp_front(u ^ 3)
    proj_s.finish_recv()
    mlp_back(u ^ 3)
    gm_c0 = reduce_core(0, u ^ 3, r.gm_part, r.gm_c)
    mlp_back(u ^ 1)
    gm_c1 = reduce_core(1, u ^ 1, r.gm_part, r.gm_c)
    mlp_back(u ^ 2)
    gm_y = reduce_y(gm_c0, r.gm_part, r.gm_c, r.gm_mid, r.gm_y)
    mlp_back(u)
    r.vec_g[...] += jnp.where(row == 10 + u, r.fcb[...], 0.0)

    def branch_tile(t):
        r.br_part[t] = dot_nn(r.act[tile(t), :], r.w_proj[...]).astype(BF)

    def weight_grad(a, b, out, tiles):
        def one(i):
            cols = pl.ds(pl.multiple_of(128 * i, 128), 128)
            out[tile(i), :] = dot_tn(a[:, cols], b[...]).astype(BF)

        loop(tiles, one)

    def collect(base, grad, land_x, mine, land_z, relay):
        return Collect(
            net, r.co_send, r.co_recv, base,
            lambda zz: grad.at[rows_at(192 * zz + 96 * (1 - x), 96)],
            lambda zz: grad[rows_at(192 * zz + 96 * x, 96), :].astype(F32),
            land_x, mine, land_z, relay)

    proj_c = collect(0, r.proj_g, r.proj_x, r.proj_m, r.proj_z, r.proj_r)
    fc_c = collect(9, r.fc_g, r.fc_x, r.fc_m, r.fc_z, r.fc_r)
    qkv_c = collect(18, r.qkv_g, r.qkv_x, r.qkv_m, r.qkv_z, r.qkv_r)

    weight_grad(r.act, r.cot_all, r.proj_g, 6)
    proj_c.start()
    branch_tile(u ^ 3)
    branch_tile(u ^ 1)
    br_c = [reduce_core(0, u ^ 3, r.br_part, r.br_c), reduce_core(1, u ^ 1, r.br_part, r.br_c)]
    branch_tile(u ^ 2)
    branch_tile(u)

    gm = reduce_end(gm_c1, gm_y, r.gm_part, r.gm_c, r.gm_y)
    normed = r.normed_mid[...]
    r.vec_g[1:2, :] = jnp.sum(gm * normed, 0, keepdims=True)
    r.vec_g[5:6, :] = jnp.sum(gm, 0, keepdims=True)

    def norm_grad(grad, normed, inverse, g):
        e = grad * g
        return inverse * (
            e - jnp.mean(e, -1, keepdims=True) - normed * jnp.mean(e * normed, -1, keepdims=True)
        )

    cot = cot_own[...].astype(F32)
    r.vec_g[4:5, :] = jnp.sum(cot, 0, keepdims=True)
    grad_resid = cot + norm_grad(gm, normed, r.inverse_mid[...], gain(1))
    r.grad_resid[...] = grad_resid
    gb = grad_resid.astype(BF)
    r.gb[...] = gb
    r.vec_g[3:4, :] = jnp.sum(gb.astype(F32), 0, keepdims=True)

    def gmer_tile(g):
        r.gmer[g] = dot_nt(r.gb[...], r.w_outp[pl.ds(pl.multiple_of(256 * g, 256), 256), :]).astype(BF)

    loop(4, gmer_tile)
    ga_p = [net.send(r.gmer.at[u ^ m], r.ga.at[tile(u)], net.plane(m)) for m in (2, 3, 1)]
    r.ga[tile(u), :] = r.gmer[u]
    weight_grad(r.lm_all, r.grad_pre, r.fc_g, 6)
    for g in range(4):
        res = dot_tn(r.merged[g], r.gb[...]).astype(BF)
        at = slice(48 * g, 48 * g + 48)
        r.out_g[0, 0, at, :] = res[0:48]
        r.out_g[1, 0, at, :] = res[48:96]
        r.out_g[0, 1, 48 * g:48 * g + 32, :] = res[96:128]
        r.out_g[0, 1, 48 * g + 32:48 * g + 48, :] = res[192:208]
        r.out_g[1, 1, at, :] = res[208:256]
    og_c = net.send(r.out_g.at[1 - c], r.og_c, net.plane(1))
    proj_c.part(0)
    proj_c.part(1)
    for copy in ga_p:
        copy.wait_recv()

    low = lane((512, 128)) < 64
    ga01 = r.ga[:, 0:128]
    zero = jnp.zeros((512, 128), BF)
    r.gam[0] = jnp.where(low, ga01.astype(F32), 0.0).astype(BF)
    r.gam[1] = jnp.where(low, 0.0, ga01.astype(F32)).astype(BF)
    r.gam[2] = r.ga[:, 128:256]
    prod = jnp.transpose(ga01.astype(F32)) * r.att_t[0]
    r.delta[0] = jnp.sum(prod[0:64], 0, keepdims=True)
    r.delta[1] = jnp.sum(prod[64:128], 0, keepdims=True)
    prod = jnp.transpose(r.ga[:, 128:256].astype(F32)) * r.att_t[1]
    r.delta[2] = jnp.sum(prod, 0, keepdims=True)
    r.dq_t[...] = jnp.zeros((3, 128, 512), F32)

    def back(j):
        factor = [jnp.exp(r.m_at[j * 3 + h] - r.m_run[h]) * r.l_inv[h] for h in range(3)]

        def keys(kt):
            rows = rows_at(128 * kt, 128)
            for h in range(3):
                vc = 128 if h < 2 else 256
                p = r.pt[j * 3 + h, rows, :].astype(F32) * factor[h]
                dp = dot_nt(r.kv_all[j, rows, vc:vc + 128], r.gam[h])
                r.ds[h, rows, :] = (p * (dp - r.delta[h])).astype(BF)
                r.pt[j * 3 + h, rows, :] = p.astype(BF)

        def sums(kt):
            rows = rows_at(128 * kt, 128)
            pair = lambda of, first, second: dot_nn(of(0), first) + dot_nn(of(1), second)
            ds = lambda h: r.ds[h, rows, :]
            p = lambda h: r.pt[j * 3 + h, rows, :]
            r.dkv[rows, 0:128] = pair(ds, r.qm[0], r.qm[1])
            r.dkv[rows, 128:256] = pair(p, r.gam[0], r.gam[1])
            r.dkv[rows, 256:384] = dot_nn(ds(2), r.qm[2]) + dot_nn(p(2), r.gam[2])

        lax.fori_loop(0, 4, lambda i, c: (keys(i), c)[1], 0, unroll=True)
        lax.fori_loop(0, 4, lambda i, c: (sums(i), c)[1], 0, unroll=True)
        for h in range(3):
            kc = 0 if h < 2 else 256
            r.dq_t[h] += dot_tn(r.kv_all[j, :, kc:kc + 128], r.ds[h])

    def chain_copy(way, step, ch):
        target = jnp.clip(jnp.where(way == 0, z - 1, z + 1), 0, nz - 1)
        at = way * (nz - 1) + step - 1
        return pltpu.make_async_remote_copy(
            src_ref=r.chain.at[at, :, third(ch)], dst_ref=r.chain_land.at[at, :, third(ch)],
            send_sem=r.ch_send.at[at * 3 + ch], recv_sem=r.ch_recv.at[at * 3 + ch],
            device_id=(x, target, u), device_id_type=MESH)

    def chain_step(step):
        def either(way):
            j = jnp.where(way == 0, z - step, z + step)
            behind = jnp.where(way == 0, z + 1, z - 1)

            @pl.when(jnp.logical_and(j >= 0, j < nz))
            def _():
                back(j)
                at = way * (nz - 1) + step - 1
                comes = jnp.logical_and(behind >= 0, behind < nz)
                for ch in range(3):
                    at_ch = third(ch)
                    if step < nz - 1:
                        @pl.when(comes)
                        def _():
                            chain_copy(way, step + 1, ch).wait_recv()
                            r.chain[at, :, at_ch] = (r.dkv[:, at_ch] + r.chain_land[at + 1, :, at_ch].astype(F32)).astype(BF)

                        @pl.when(jnp.logical_not(comes))
                        def _():
                            r.chain[at, :, at_ch] = r.dkv[:, at_ch].astype(BF)
                    else:
                        r.chain[at, :, at_ch] = r.dkv[:, at_ch].astype(BF)
                    chain_copy(way, step, ch).start()

        loop(2, either)

    for step in range(nz - 1, 0, -1):
        chain_step(step)
        if step == nz - 1:
            proj_c.part(2)
            proj_c.part(3)
            fc_c.start()
            early_p = [net.send(r.vec_g, r.vg_p.at[m - 1], net.plane(m)) for m in (1, 2, 3)]
            og_c.wait_recv()
            r.og_1[...] = (r.out_g[c].astype(F32) + r.og_c[...].astype(F32)).astype(BF)
            og_y = net.send(r.og_1.at[1 - y], r.og_y, net.plane(2))
        if step == nz - 2:
            proj_c.second()
            br_y = reduce_y(br_c[0], r.br_part, r.br_c, r.br_mid, r.br_y)
            total = r.vec_g[...]
            for m in range(3):
                early_p[m].wait_recv()
                total = total + r.vg_p[m]
            r.vg_1[...] = total
            early_z = [net.send(r.vg_1, r.vg_z.at[d - 1], net.line(d)) for d in range(1, nz)]
            fc_c.part(0)
            fc_c.part(1)
            og_y.wait_recv()
            r.og_2[...] = (r.og_1[y].astype(F32) + r.og_y[...].astype(F32)).astype(BF)
            og_x = net.send(r.og_2.at[:, half_cols(1 - x)], r.og_x, net.other_x())
        if step == 1:
            og_x.wait_recv()
            r.og_3[...] = (r.og_2[:, half_cols(x)].astype(F32) + r.og_x[...].astype(F32)).astype(BF)
            og_z = [
                net.send(r.og_3.at[rows_at(48 * net.zplus(d), 48)], r.og_z.at[d - 1], net.line(d))
                for d in range(1, nz)
            ]
            total = r.vg_1[...]
            for d in range(nz - 1):
                early_z[d].wait_recv()
                total = total + r.vg_z[d]
            r.vg_2[...] = total
            early_x = net.send(r.vg_2, r.vg_x, net.other_x())
            r.output[...] = (
                r.resid[...] + gain(5) + reduce_end(br_c[1], br_y, r.br_part, r.br_c, r.br_y)
            ).astype(BF)
            fc_c.part(2)
            fc_c.part(3)
    back(z)

    fc_c.second()
    for ch in range(3):
        @pl.when(z + 1 < nz)
        def _():
            chain_copy(0, 1, ch).wait_recv()
            r.dkv[:, third(ch)] += r.chain_land[0, :, third(ch)].astype(F32)

        @pl.when(z >= 1)
        def _():
            chain_copy(1, 1, ch).wait_recv()
            r.dkv[:, third(ch)] += r.chain_land[nz - 1, :, third(ch)].astype(F32)

    r.gqkv[:, 128:512] = r.dkv[...].astype(BF)
    dq = jnp.transpose(jnp.where(rowi < 64, r.dq_t[0], r.dq_t[1]) * 0.125)
    r.gqkv[:, 0:128] = dq.astype(BF)
    r.gqkv[:, 512:576] = jnp.transpose(r.dq_t[2] * 0.125)[:, 0:64].astype(BF)


    def gin_tile(t):
        r.gi_part[t] = dot_nt(r.gqkv[tile(t), :], r.w_qkv[...]).astype(BF)

    weight_grad(r.ln_all, r.gqkv, r.qkv_g, 6)
    qkv_c.start()
    gin_tile(u ^ 3)
    gi_c0 = reduce_core(0, u ^ 3, r.gi_part, r.gi_c)
    gin_tile(u ^ 1)
    gi_c1 = reduce_core(1, u ^ 1, r.gi_part, r.gi_c)
    gin_tile(u ^ 2)
    gi_y = reduce_y(gi_c0, r.gi_part, r.gi_c, r.gi_mid, r.gi_y)
    gin_tile(u)
    r.late[...] = jnp.zeros((8, 768), F32)
    row_l = row[0:8]
    r.late[:, 0:576] = jnp.where(row_l[:, 0:576] == 2 + u, jnp.sum(r.gqkv[...].astype(F32), 0, keepdims=True), 0.0)
    qkv_c.first()
    proj_c.total(r.acc)
    r.proj_f[...] = r.acc[...].astype(BF)
    mine = rows_at(96 * x, 96)
    r.proj_o[mine, :] = r.proj_f[...]
    proj_last = net.send(r.proj_f, r.proj_o.at[mine], net.other_x())

    finals = []

    def hand_out(base, final, native):
        for xx in range(2):
            for cc in range(2):
                target_x = x ^ xx
                target_u = 2 * x + cc
                here = jnp.logical_and(xx == 0, target_u == u)
                k = base + 2 * xx + cc
                copy = pltpu.make_async_remote_copy(
                    src_ref=final.at[pl.ds(48 * cc, 48)], dst_ref=native.at[u], send_sem=r.f_send.at[k],
                    recv_sem=r.f_recv.at[base + u], device_id=(target_x, z, target_u), device_id_type=MESH)

                @pl.when(jnp.logical_not(here))
                def _():
                    copy.start()

                @pl.when(here)
                def _():
                    native[u] = final[pl.ds(48 * cc, 48), :]

                finals.append((here, copy))

    def await_native(base, final, native):
        for who in range(4):
            copy = pltpu.make_async_remote_copy(
                src_ref=final.at[pl.ds(0, 48)], dst_ref=native.at[who], send_sem=r.f_send.at[base],
                recv_sem=r.f_recv.at[base + who], device_id=(1 - x, z, u), device_id_type=MESH)

            @pl.when(jnp.logical_not(jnp.logical_and(x == y, u == who)))
            def _():
                copy.wait_recv()

    gin = reduce_end(gi_c1, gi_y, r.gi_part, r.gi_c, r.gi_y)
    normed, inverse = normalize(x_own[...].astype(F32))
    r.late[0:1, :] = jnp.sum(gin * normed, 0, keepdims=True)
    r.late[1:2, :] = jnp.sum(gin, 0, keepdims=True)
    late_p = [net.send(r.late, r.late_p.at[m - 1], net.plane(m)) for m in (2, 3, 1)]
    late_p += [net.send(r.late, r.late_p.at[3 + m], (1 - x, z, u ^ m)) for m in range(4)]
    r.input_grad[...] = (r.grad_resid[...] + norm_grad(gin, normed, inverse, gain(0))).astype(BF)
    qkv_c.second()
    fc_c.total(r.acc)
    r.fc_f[...] = r.acc[...].astype(BF)
    hand_out(0, r.fc_f, r.fc_o)
    total = r.late[...]
    for copy in late_p:
        copy.wait_recv()
    for m in range(7):
        total = total + r.late_p[m]
    r.late_1[...] = total
    late_z = [net.send(r.late_1, r.late_z.at[d - 1], net.line(d)) for d in range(1, nz)]
    total = r.og_3[rows_at(48 * z, 48), :].astype(F32)
    for d in range(nz - 1):
        og_z[d].wait_recv()
        total = total + r.og_z[d].astype(F32)
    r.out_o[:, half_cols(x)] = total.astype(BF)
    og_last = net.send(r.out_o.at[:, half_cols(x)], r.out_o.at[:, half_cols(x)], net.other_x())
    qkv_c.total(r.acc_q)
    r.qkv_f[...] = r.acc_q[...].astype(BF)
    hand_out(4, r.qkv_f, r.qkv_o)
    early_x.wait_recv()
    early = r.vg_2[...] + r.vg_x[...]
    late = r.late_1[...]
    for d in range(nz - 1):
        late_z[d].wait_recv()
        late = late + r.late_z[d]
    heads = jnp.sum(jnp.where(row_l == 2 + z, late, 0.0), 0, keepdims=True)
    hidden = jnp.sum(jnp.where(row == 10 + u, early, 0.0), 0, keepdims=True)
    total = early[0:8] + jnp.where(row_l == 0, late, 0.0) + jnp.where(row_l == 2, late[1:2], 0.0)
    bias[0:1, 0:128] = heads[:, 0:128]
    bias[0:1, 128:192] = heads[:, 512:576]
    bias[1:2, 0:128] = heads[:, 256:384]
    bias[1:2, 128:192] = heads[:, 448:512]
    mine8 = pltpu.roll(total, 768 - 48 * (4 * z + u), 1)
    vp[0:8, :] = mine8
    both = pltpu.roll(bias[...], 256 - 48 * u, 1)
    vp[6:8, 0:256] = both[0:2]
    vp[8:16, :] = pltpu.roll(jnp.broadcast_to(hidden, (8, 768)), 768 - 192 * z, 1)
    r.vec_o[...] = vp[...]
    proj_last.wait_recv()
    og_last.wait_recv()
    await_native(0, r.fc_f, r.fc_o)
    await_native(4, r.qkv_f, r.qkv_o)

    for here, copy in finals:
        @pl.when(jnp.logical_not(here))
        def _():
            copy.wait_send()
    for step in range(nz - 1):
        for way in range(2):
            @pl.when(kv_sends(way, step))
            def _():
                for ch in range(3):
                    kv_copy(way, step, ch).wait_send()
    for step in range(1, nz):
        for way in range(2):
            @pl.when(z - step >= 0 if way == 0 else z + step < nz)
            def _():
                for ch in range(3):
                    chain_copy(way, step, ch).wait_send()
    for part in (qkv_s, fc_s, proj_s, out_s, proj_c, fc_c, qkv_c):
        part.finish()
    net.finish()


def block_call(nz, **operands):
    def vm(*shape, kind=BF):
        return pltpu.VMEM(shape, kind)

    outs = dict(
        output=((128, 768), BF), input_grad=((128, 768), BF), qkv_o=((4, 48, 576), BF),
        fc_o=((4, 48, 768), BF), proj_o=((192, 768), BF), out_o=((48, 768), BF), vec_o=((16, 768), F32),
    )
    f = lambda *shape: vm(*shape, kind=F32)
    keys = 512 * nz
    scratch = dict(
        qkv_raw=vm(48, 2304), fc_raw=vm(48, 3072), qkv_pre=vm(4, 48, 576), fc_pre=vm(4, 48, 768),
        vec_f32=f(16, 768), bias_f32=f(8, 256), vec_pre=vm(16, 768),
        pos_row=pltpu.VMEM((1, keys), jnp.int32), pos_col=pltpu.VMEM((keys, 1), jnp.int32),
        w_qkv=vm(768, 576), w_fc=vm(768, 768), w_proj=vm(768, 768), w_out=vm(768, 768), w_outp=vm(1024, 768),
        vec_land_z=vm(nz - 1, 16, 768), vec_u=vm(16, 768), vec_land_p=vm(3, 16, 768), vec=f(16, 768),
        x_all=vm(512, 768), cot_all=vm(512, 768), ln_all=vm(512, 768), lm_all=vm(512, 768),
        qm=vm(3, 512, 128), kv_all=vm(nz, 512, 384), s_buf=f(512, 512), pt=vm(nz * 3, 512, 512),
        m_run=f(3, 1, 512), l_run=f(3, 1, 512), l_inv=f(3, 1, 512), m_at=f(nz * 3, 1, 512), o_t=f(3, 128, 512),
        att_t=f(2, 128, 512), att=vm(512, 256), merged=vm(4, 128, 256),
        resid=f(128, 768), normed_mid=f(128, 768), inverse_mid=f(128, 1), slope=f(512, 768),
        act=vm(512, 768), grad_pre=vm(512, 768), fcb=f(1, 768), vec_g=f(16, 768),
        gm_part=vm(4, 128, 768), gm_c=vm(2, 128, 768), gm_mid=vm(128, 768), gm_y=vm(128, 768),
        br_part=vm(4, 128, 768), br_c=vm(2, 128, 768), br_mid=vm(128, 768), br_y=vm(128, 768),
        gi_part=vm(4, 128, 768), gi_c=vm(2, 128, 768), gi_mid=vm(128, 768), gi_y=vm(128, 768),
        grad_resid=f(128, 768), gb=vm(128, 768), gmer=vm(4, 128, 256), ga=vm(512, 256), gam=vm(3, 512, 128),
        delta=f(3, 1, 512), ds=vm(3, 512, 512), dq_t=f(3, 128, 512), dkv=f(512, 384),
        chain=vm(2 * (nz - 1), 512, 384), chain_land=vm(2 * (nz - 1), 512, 384), gqkv=vm(512, 576),
        qkv_g=vm(768, 576), fc_g=vm(768, 768), proj_g=vm(768, 768), out_g=vm(2, 2, 192, 768),
        qkv_x=vm(nz, 96, 576), fc_x=vm(nz, 96, 768), proj_x=vm(nz, 96, 768),
        qkv_m=vm(nz, 96, 576), fc_m=vm(nz, 96, 768), proj_m=vm(nz, 96, 768),
        qkv_z=vm(nz - 1, 96, 576), fc_z=vm(nz - 1, 96, 768), proj_z=vm(nz - 1, 96, 768),
        qkv_r=vm(96, 576), fc_r=vm(96, 768), proj_r=vm(96, 768), acc=f(96, 768), acc_q=f(96, 576),
        qkv_f=vm(96, 576), fc_f=vm(96, 768), proj_f=vm(96, 768),
        og_c=vm(2, 192, 768), og_1=vm(2, 192, 768), og_y=vm(192, 768), og_2=vm(192, 768),
        og_x=vm(192, 384), og_3=vm(192, 384), og_z=vm(nz - 1, 48, 384),
        late=f(8, 768), late_p=f(7, 8, 768), late_1=f(8, 768), late_z=f(nz - 1, 8, 768),
        vg_p=f(3, 16, 768), vg_1=f(16, 768), vg_z=f(nz - 1, 16, 768), vg_2=f(16, 768), vg_x=f(16, 768),
        send_sem=pltpu.SemaphoreType.DMA((112,)), recv_sem=pltpu.SemaphoreType.DMA((112,)),
        sp_send=pltpu.SemaphoreType.DMA((32,)), sp_recv=pltpu.SemaphoreType.DMA((32,)),
        co_send=pltpu.SemaphoreType.DMA((27,)), co_recv=pltpu.SemaphoreType.DMA((27,)),
        local_sem=pltpu.SemaphoreType.DMA((6,)),
        kv_send=pltpu.SemaphoreType.DMA((6 * nz,)), kv_recv=pltpu.SemaphoreType.DMA((6 * nz,)),
        ch_send=pltpu.SemaphoreType.DMA((6 * nz,)), ch_recv=pltpu.SemaphoreType.DMA((6 * nz,)),
        f_send=pltpu.SemaphoreType.DMA((8,)), f_recv=pltpu.SemaphoreType.DMA((8,)),
    )
    names = [*operands, *outs, *scratch]
    places = {name: pl.BlockSpec(memory_space=pl.ANY) for name in ("x_in", "cot_in", "qkv_in", "fc_in", "out_in", "proj_in")}
    places["order_in"] = pl.BlockSpec(memory_space=pltpu.SMEM)

    def kernel(*refs):
        block_kernel(nz, types.SimpleNamespace(**dict(zip(names, refs, strict=True))))

    got = pl.pallas_call(
        kernel,
        out_shape=tuple(jax.ShapeDtypeStruct(*s) for s in outs.values()),
        in_specs=[places.get(name, VSPEC) for name in operands],
        out_specs=(VSPEC,) * len(outs),
        scratch_shapes=list(scratch.values()),
        compiler_params=pltpu.CompilerParams(
            collective_id=0, has_side_effects=True, vmem_limit_bytes=60 * 2**20
        ),
        name="transformer_block",
    )(*operands.values())
    return dict(zip(outs, got, strict=True))


def hand_over_kernel(nz, output, input_grad, qkv_o, fc_o, proj_o, out_o, vec_o,
                     output_f, input_grad_f, gains_f, biases_f, mid_f, vb_f, qkv_f, out_f, fc_f, fcb_f, proj_f):
    output_f[...] = output[...]
    input_grad_f[...] = input_grad[...]
    gains_f[...] = vec_o[0:2, 0:48]
    biases_f[0:1, :] = vec_o[2:3, 0:48]
    biases_f[1:2, :] = vec_o[6:7, 0:48]
    biases_f[2:4, :] = vec_o[3:5, 0:48]
    mid_f[...] = vec_o[5:6, 0:48]
    vb_f[...] = vec_o[7:8, 0:48]
    fcb_f[...] = vec_o[8:9, 0:192]
    out_f[...] = out_o[...].astype(F32)
    proj_f[...] = proj_o[...].astype(F32)
    for g in range(4):
        for t in range(3):
            qkv_f[:, 768 * t + 192 * g:768 * t + 192 * g + 128] = qkv_o[g, :, 128 * t:128 * t + 128].astype(F32)
        for at, t in ((384, 1), (448, 2), (512, 0)):
            qkv_f[:, 768 * t + 192 * g + 128:768 * t + 192 * g + 192] = qkv_o[g, :, at:at + 64].astype(F32)
        for zz in range(nz):
            fc_f[:, 768 * zz + 192 * g:768 * zz + 192 * g + 192] = fc_o[g, :, 192 * zz:192 * zz + 192].astype(F32)


def hand_over(nz, got):
    shapes = [((128, 768), BF), ((128, 768), BF), ((2, 48), F32), ((4, 48), F32), ((1, 48), F32), ((1, 48), F32),
              ((48, 2304), F32), ((48, 768), F32), ((48, 3072), F32), ((1, 192), F32), ((192, 768), F32)]
    return pl.pallas_call(
        functools.partial(hand_over_kernel, nz),
        out_shape=tuple(jax.ShapeDtypeStruct(*s) for s in shapes),
        in_specs=[VSPEC] * len(got),
        out_specs=(VSPEC,) * len(shapes),
        compiler_params=pltpu.CompilerParams(vmem_limit_bytes=60 * 2**20),
        name="hand_over",
    )(*got.values())


def device_fast(nz, inputs, stretch_order, norm_gains, biases, mid_shift, value_bias, qkv_weight, out_weight, fc_weight, fc_bias, proj_weight, cotangent):
    got = block_call(
        nz,
        x_in=inputs[0],
        cot_in=cotangent[0],
        qkv_in=qkv_weight,
        fc_in=fc_weight,
        out_in=out_weight,
        proj_in=proj_weight,
        gains_in=norm_gains,
        biases_in=biases,
        mid_in=mid_shift[None],
        vb_in=value_bias[None],
        fcb_in=fc_bias[None],
        order_in=stretch_order,
    )
    output, input_grad, gains, rows, mid, vb, qkv, out, fc, fcb, proj = hand_over(nz, got)
    return output[None], input_grad[None], gains, rows, mid[0], vb[0], qkv, out, fc, fcb[0], proj


def solution(mesh):
    placed = (
        P("dp", ("blk", "uly"), None),
        P("dp", None),
        P(None, ("blk", "uly")),
        P(None, ("blk", "uly")),
        P(("blk", "uly")),
        P(("blk", "uly")),
        P(("blk", "uly"), None),
        P(("blk", "uly"), None),
        P(("blk", "uly"), None),
        P(("blk", "uly")),
        P(("blk", "uly"), None),
        P("dp", ("blk", "uly"), None),
    )
    sizes = dict(mesh.shape)
    nz = sizes["blk"]
    fast = sizes["uly"] == 4 and sizes["dp"] == 2 and nz == 4
    chosen = functools.partial(device_fast, nz) if fast else per_device
    return jax.shard_map(
        chosen,
        mesh=mesh,
        in_specs=placed,
        out_specs=(
            P("dp", ("blk", "uly"), None),
            P("dp", ("blk", "uly"), None),
            P(None, ("blk", "uly")),
            P(None, ("blk", "uly")),
            P(("blk", "uly")),
            P(("blk", "uly")),
            P(("blk", "uly"), None),
            P(("blk", "uly"), None),
            P(("blk", "uly"), None),
            P(("blk", "uly")),
            P(("blk", "uly"), None),
        ),
        check_vma=False,
    )
```
